32 devices in a mesh: seq: 2 (over x), fsdp: 16 (over z, y, core).
Axes of the slice: x: 2, y: 2, z: 4, core: 2. Of those that a mesh axis runs over, the one named last changes fastest.
Arguments:
- incoming_state: bfloat16 [16, 512, 768], P('fsdp', 'seq'), may hold values from -6 to 6
- projection_matrix_triple: bfloat16 [768, 2304], P(('seq', 'fsdp')), may hold values from -0.3125 to 0.3125
- merge_matrix: bfloat16 [768, 768], P(('seq', 'fsdp')), may hold values from -1.75 to 1.75
- widen_matrix: bfloat16 [768, 3072], P(('seq', 'fsdp')), may hold values from -0.21875 to 0.21875
- shrink_matrix: bfloat16 [3072, 768], P(('seq', 'fsdp')), may hold values from -0.109375 to 0.109375
- offset_table: bfloat16 [6, 768], P(None, ('seq', 'fsdp')), may hold values from -1.5 to 1.5
- norm_scales: bfloat16 [2, 768], P(None, ('seq', 'fsdp')), may hold values from 0.25 to 1.75
- widen_offset: bfloat16 [3072], P(('seq', 'fsdp')), may hold values from -1.5 to 1.5
- trainable_gate_scores: float32 [12, 512, 512], P('seq', 'fsdp'), may hold values from -8 to 8
- gate_perturbation: float32 [12, 512, 512], P('seq', 'fsdp'), may hold values from -6 to 6
- softening_scale: float32 [12], P('seq'), may hold values from 0.5 to 2
- passage_extents: int32 [32], replicated, may hold values from 1 to 512, 8192 in all
- result_cotangent: bfloat16 [16, 512, 768], P('fsdp', 'seq'), may hold values from -6 to 6
Outputs:
- layer_out: bfloat16 [16, 512, 768], P('fsdp', 'seq')
- input_grad: float32 [16, 512, 768], P('fsdp', 'seq')
- grad_w_qkv: float32 [768, 2304], P(('seq', 'fsdp'))
- grad_w_out: float32 [768, 768], P(('seq', 'fsdp'))
- grad_w_up: float32 [768, 3072], P(('seq', 'fsdp'))
- grad_w_down: float32 [3072, 768], P(('seq', 'fsdp'))
- grad_biases: float32 [6, 768], P(None, ('seq', 'fsdp'))
- grad_gains: float32 [2, 768], P(None, ('seq', 'fsdp'))
- grad_bias_up: float32 [3072], P(('seq', 'fsdp'))
- mask_logit_gradient: float32 [12, 512, 512], P('seq', 'fsdp')
The draws below stay inside these ranges and needn't reach their ends.
Inputs may be any that keep to these rules, and one draw needn't show every extreme that they name: `passage_extents`: they sum to 8192, and the longest is exactly 512.
All inputs are finite; a program needn't handle non-finite values.
Results may differ from the reference program's by a relative error of at most 0.013.
Values may be sent and summed in bfloat16 or wider, within the bound.
No kernel may reach another device: no remote copies, remote signals or barrier semaphores. Data moves between devices by JAX's collectives and lax.ppermute only.
A program may use at most 192 MiB of HBM per device.

```python
import math
import jax
import jax.numpy as jnp
import numpy as np
from jax import lax

D = 768
FF = 3072
FOCUS_COUNT = 12
HDIM = 64
MPOS = 512
GROUP_TOK = 512
GROUPS = 16
TOKENS = 8192
DOC_MAX = 512
NDOCS = 32


def levels(stream_key, dims, shards, low, high):
    def one(dim, blocks):
        heights = jax.random.uniform(jax.random.fold_in(jax.random.fold_in(stream_key, 6), dim), (blocks,), jnp.float32, low / len(shards), high / len(shards))
        return jnp.repeat(jnp.exp(heights), dims[dim] // blocks).reshape((-1,) + (1,) * (len(dims) - dim - 1))

    level = one(*shards[0])
    for cut in shards[1:]:
        level = level * one(*cut)
    return level


def profile(count, total, reach, skew):
    loads = [(1 << 20) // math.isqrt(standing ** skew) + 1 for standing in range(2, count + 1)]
    spare, holding = total - reach - (count - 1), [1] * (count - 1)
    while spare > 0:
        candidates = [i for i in range(count - 1) if holding[i] < reach]
        pool, remaining = sum([loads[i] for i in candidates]), spare
        for i in candidates:
            extra = min(reach - holding[i], max(1, remaining * loads[i] // pool), spare)
            holding[i] = holding[i] + extra
            spare = spare - extra
    return np.array([reach] + holding)


def uneven(rng, number_of, total, limit, slope):
    if number_of == 2:
        one = jax.random.randint(rng, (), max(1, total - limit), min(limit, total - 1) + 1)
        return jnp.stack([one, total - one])
    tallies = jnp.asarray(profile(number_of, total, limit, slope), jnp.int32)
    couples = (number_of - 1) // 2
    source_of, sink = tallies[1:1 + 2 * couples:2], tallies[2:2 + 2 * couples:2]
    margin = jnp.minimum(source_of - 1, limit - sink)
    moved = jax.random.randint(jax.random.fold_in(rng, 1), (couples,), 0, 1 << 20) % (margin + 1)
    tallies = tallies.at[1:1 + 2 * couples:2].set(source_of - moved).at[2:2 + 2 * couples:2].set(sink + moved)
    return tallies[jax.random.permutation(jax.random.fold_in(rng, 2), number_of)]


def noise(own_key, extent, deviation, limit, split=(), kind=jnp.bfloat16):
    array = jax.random.normal(own_key, extent, jnp.float32) * deviation
    if len(split) > 0:
        array = levels(own_key, extent, split, -0.22, 0.18) * array
    return jnp.clip(array, min=-limit, max=limit).astype(kind)


def setup_inputs(seed: int = 0) -> dict:
    splits = jax.random.split(jax.random.key(seed), 14)
    return {
        "incoming_state": noise(splits[0], (GROUPS, GROUP_TOK, D), 1.0, 6.0, ((0, 16), (1, 2))),
        "projection_matrix_triple": noise(splits[1], (D, 3 * D), (D // 2) ** -0.5, 0.3125, ((0, 32),)),
        "merge_matrix": noise(splits[2], (D, D), (D // 64) ** -0.5, 1.75, ((0, 32),)),
        "widen_matrix": noise(splits[3], (D, FF), D ** -0.5, 0.21875, ((0, 32),)),
        "shrink_matrix": noise(splits[4], (FF, D), FF ** -0.5, 0.109375, ((0, 32),)),
        "offset_table": noise(splits[5], (6, D), 0.3, 1.5, ((1, 32),)),
        "norm_scales": jnp.clip(1.0 + 0.15 * jax.random.normal(splits[6], (2, D), jnp.float32), 0.25, 1.75).astype(jnp.bfloat16),
        "widen_offset": noise(splits[7], (FF,), 0.3, 1.5, ((0, 32),)),
        "trainable_gate_scores": noise(splits[8], (FOCUS_COUNT, MPOS, MPOS), 1.5, 8.0, ((0, 2), (1, 16)), jnp.float32),
        "gate_perturbation": noise(splits[9], (FOCUS_COUNT, MPOS, MPOS), 1.0, 6.0, ((0, 2), (1, 16)), jnp.float32),
        "softening_scale": jnp.clip(jnp.exp(math.log(2.0) - 1.3862944 * jax.random.uniform(splits[10], (FOCUS_COUNT,), jnp.float32) ** levels(splits[10], (FOCUS_COUNT,), ((0, 2),), -0.2, 0.2)), 0.5, 2.0),
        "passage_extents": uneven(splits[11], NDOCS, TOKENS, DOC_MAX, 2).astype(jnp.int32),
        "result_cotangent": noise(splits[12], (GROUPS, GROUP_TOK, D), 1.0, 6.0, ((0, 16), (1, 2))),
    }


EPS = 1e-05
HIGH = lax.Precision.HIGHEST

@jax.custom_vjp
def low(v):
    return lax.optimization_barrier(v.astype(jnp.bfloat16)).astype(jnp.float32)

@jax.custom_vjp
def low_back(v):
    return v

def low_keep(v):
    return (low(v), None)

def low_pass(kept, grad):
    return (grad,)

def back_keep(v):
    return (v, None)

def back_low(kept, grad):
    return (low(grad),)
low.defvjp(low_keep, low_pass)
low_back.defvjp(back_keep, back_low)

def matmul_high(left, right):
    return jnp.dot(left, right, precision=HIGH, preferred_element_type=jnp.float32)

def layer_norm(values, gain, shift):
    center = values - lax.optimization_barrier(jnp.mean(values, axis=-1, keepdims=True))
    spread = lax.optimization_barrier(jnp.mean(center * center, axis=-1, keepdims=True))
    return center * lax.rsqrt(spread + EPS) * gain + shift

def locate(index, passage_opening, passage_finish, stream_rows):
    document = lax.optimization_barrier(jnp.sum((passage_finish[None, :] <= index[:, None]).astype(jnp.int32), axis=1)).astype(jnp.int32)
    begin = lax.optimization_barrier(jnp.max(jnp.where(passage_opening[None, :] <= index[:, None], passage_opening[None, :], 0), axis=1)).astype(jnp.int32)
    inside = (index >= 0) & (index < stream_rows)
    document = jnp.where(inside, document, -1).astype(jnp.int32)
    position = ((index - begin) % MPOS).astype(jnp.int32)
    return (document, position)

def block_evaluate(block_arguments, projection_matrix_triple, merge_matrix, widen_matrix, shrink_matrix, offset_table, norm_scales, widen_offset, trainable_gate_scores, gate_perturbation, softening_scale, passage_opening, passage_finish):
    stream_rows = block_arguments.shape[0]
    group_rows = GROUP_TOK
    smooth_gate = low(jax.nn.sigmoid((trainable_gate_scores + gate_perturbation) / softening_scale[:, None, None]))
    qkv_bias = jnp.concatenate([offset_table[0], jnp.zeros_like(offset_table[0]), offset_table[1]])
    qkv = low_back(low(matmul_high(block_arguments, projection_matrix_triple) + qkv_bias))
    query = qkv[:, :D].reshape(stream_rows, FOCUS_COUNT, HDIM)
    key = qkv[:, D:2 * D].reshape(stream_rows, FOCUS_COUNT, HDIM)
    value = qkv[:, 2 * D:].reshape(stream_rows, FOCUS_COUNT, HDIM)
    padding = jnp.zeros((group_rows, FOCUS_COUNT, HDIM), qkv.dtype)
    key_pad = jnp.concatenate([padding, key, padding], axis=0)
    value_pad = jnp.concatenate([padding, value, padding], axis=0)

    def attend(block):
        first = block * group_rows
        query_block = lax.dynamic_slice_in_dim(query, first, group_rows, 0)
        key_block = lax.dynamic_slice_in_dim(key_pad, first, 3 * group_rows, 0)
        value_block = lax.dynamic_slice_in_dim(value_pad, first, 3 * group_rows, 0)
        query_doc, query_pos = locate(first + jnp.arange(group_rows, dtype=jnp.int32), passage_opening, passage_finish, stream_rows)
        key_doc, key_pos = locate(first - group_rows + jnp.arange(3 * group_rows, dtype=jnp.int32), passage_opening, passage_finish, stream_rows)
        scores = low_back(jnp.einsum('qhd,khd->hqk', query_block, key_block, precision=HIGH) * 0.125)
        scores = jnp.where((query_doc[:, None] == key_doc[None, :])[None], scores, -1e+30)
        row_top = lax.optimization_barrier(jnp.max(scores, axis=-1, keepdims=True))
        weights = jnp.exp(scores - row_top)
        probs = weights / lax.optimization_barrier(jnp.sum(weights, axis=-1, keepdims=True))
        lookup = jnp.take(jnp.take(smooth_gate, query_pos, axis=1), key_pos, axis=2)
        mixed = low(probs * lookup)
        return jnp.einsum('hqk,khd->qhd', mixed, value_block, precision=HIGH)
    blocks = stream_rows // group_rows
    context = lax.map(jax.checkpoint(attend), jnp.arange(blocks, dtype=jnp.int32))
    context = low_back(low(context.reshape(stream_rows, D)))
    attn = low_back(matmul_high(context, merge_matrix) + offset_table[2])
    normed = layer_norm(block_arguments + attn, norm_scales[0], offset_table[4])
    up = low_back(matmul_high(low(normed), widen_matrix) + widen_offset)
    act = low(jax.nn.gelu(up, approximate=False))
    down = low_back(matmul_high(act, shrink_matrix) + offset_table[3])
    return layer_norm(normed + down, norm_scales[1], offset_table[5])

def reference(incoming_state, projection_matrix_triple, merge_matrix, widen_matrix, shrink_matrix, offset_table, norm_scales, widen_offset, trainable_gate_scores, gate_perturbation, softening_scale, passage_extents, result_cotangent):
    passage_finish = jnp.cumsum(passage_extents).astype(jnp.int32)
    passage_opening = (passage_finish - passage_extents).astype(jnp.int32)
    block_arguments = incoming_state.reshape(-1, D).astype(jnp.float32)

    def layer(block_arguments, projection_matrix_triple, merge_matrix, widen_matrix, shrink_matrix, offset_table, norm_scales, widen_offset, trainable_gate_scores):
        return block_evaluate(block_arguments, projection_matrix_triple, merge_matrix, widen_matrix, shrink_matrix, offset_table, norm_scales, widen_offset, trainable_gate_scores, gate_perturbation, softening_scale, passage_opening, passage_finish)
    output, pullback = jax.vjp(layer, block_arguments, projection_matrix_triple.astype(jnp.float32), merge_matrix.astype(jnp.float32), widen_matrix.astype(jnp.float32), shrink_matrix.astype(jnp.float32), offset_table.astype(jnp.float32), norm_scales.astype(jnp.float32), widen_offset.astype(jnp.float32), trainable_gate_scores)
    grads = pullback(result_cotangent.reshape(-1, D).astype(jnp.float32))
    return (output.astype(jnp.bfloat16).reshape(incoming_state.shape), grads[0].reshape(incoming_state.shape), grads[1], grads[2], grads[3], grads[4], grads[5], grads[6], grads[7], grads[8])
```

```python
from functools import partial

import jax
import jax.numpy as jnp
from jax import lax
from jax.experimental import pallas as pl
from jax.experimental.pallas import tpu as pltpu
from jax.sharding import PartitionSpec as P

D = 768
FF = 3072
HEADS = 12
HDIM = 64
MPOS = 512
EPS = 1e-05
GROUP = 512
HALF = 256
WINDOW = 3 * GROUP
OWN = 384
CHUNK = 256
NEG = -1e30
BF = jnp.bfloat16
F32 = jnp.float32
HIGH = lax.Precision.HIGHEST


def nn(left, right):
    return jnp.dot(left, right, preferred_element_type=F32)


def nt(left, right, precision=None):
    return lax.dot_general(
        left, right, (((1,), (1,)), ((), ())), precision=precision, preferred_element_type=F32
    )


def tn(left, right):
    return lax.dot_general(left, right, (((0,), (0,)), ((), ())), preferred_element_type=F32)


def load_projection(scal, parts, w, sem):
    copies = []
    for cr in range(2):
        for ur in range(8):
            row = (scal[1] ^ cr) * OWN + (ur ^ scal[0]) * 48
            copies.append(
                pltpu.make_async_copy(
                    parts[cr].at[ur],
                    w.at[pl.ds(pl.multiple_of(row, 16), 48), :],
                    sem.at[cr * 8 + ur],
                )
            )
    for copy in copies:
        copy.start()
    return copies


def load_table(scal, parts, table, sem):
    copies = []
    for cr in range(2):
        for ur in range(8):
            row = (2 * (ur ^ scal[0]) + (scal[1] ^ cr)) * 32
            copies.append(
                pltpu.make_async_copy(
                    parts[cr].at[ur],
                    table.at[:, pl.ds(pl.multiple_of(row, 32), 32), :],
                    sem.at[cr * 8 + ur],
                )
            )
    for copy in copies:
        copy.start()
    return copies


def project_kernel(
    scal, x1, x0, x2, y1, y0, y2, wa, wb, bias, q_ref, k_ref, v_ref, xg_ref, xw, w, sem
):
    copies = load_projection(scal, (wa, wb), w, sem)
    side = scal[2]
    for g, (mine, other) in enumerate(((x0, y0), (x1, y1), (x2, y2))):
        xw[pl.ds(pl.multiple_of(g * GROUP + side * HALF, HALF), HALF), :] = mine[...]
        xw[pl.ds(pl.multiple_of(g * GROUP + (1 - side) * HALF, HALF), HALF), :] = other[...]
    for copy in copies:
        copy.wait()
    for blk in range(6):
        rows = slice(blk * HALF, (blk + 1) * HALF)
        here = xw[rows, :]
        k_ref[rows, :] = nn(here, w[:, OWN : 2 * OWN]).astype(BF)
        v_ref[rows, :] = (nn(here, w[:, 2 * OWN :]) + bias[0:1, 2 * OWN :]).astype(BF)
        if blk in (2, 3):
            local = slice((blk - 2) * HALF, (blk - 1) * HALF)
            query = (nn(here, w[:, :OWN]) + bias[0:1, :OWN]).astype(BF)
            q_ref[local, :] = query * jnp.asarray(0.125, BF)
            xg_ref[local, :] = here


def head_lanes():
    return lax.broadcasted_iota(jnp.int32, (1, 128), 1) < HDIM


def fill_hot(pos_col, hot):
    for blk in range(6):
        rows = slice(blk * 256, (blk + 1) * 256)
        column = lax.broadcasted_iota(jnp.int32, (256, MPOS), 1)
        hot[rows, :] = jnp.where(pos_col[rows, :] == column, 1.0, 0.0).astype(BF)


def fill_hot_turned(pos_row, hot):
    for blk in range(6):
        rows = lax.broadcasted_iota(jnp.int32, (MPOS, 256), 0)
        hot[blk] = jnp.where(pos_row[blk] == rows, 1.0, 0.0).astype(BF)


def attend_kernel(
    scal, pos_col, doc_col, doc_row, q, k, v, ma, mb, ctx, lse, table, hot, sbuf, rbuf, acc, sem
):
    first = pl.program_id(0) == 0

    @pl.when(first)
    def _():
        copies = load_table(scal, (ma, mb), table, sem)
        fill_hot(pos_col, hot)
        for copy in copies:
            copy.wait()

    low = head_lanes()
    pair = pl.program_id(0)
    for qb in range(2):
        lo, hi = scal[3 + 2 * qb], scal[4 + 2 * qb]
        q_pair = q[qb * HALF : (qb + 1) * HALF, :]
        q_doc = doc_col[GROUP + qb * HALF : GROUP + (qb + 1) * HALF, :]
        q_hot = hot[GROUP + qb * HALF : GROUP + (qb + 1) * HALF, :]
        outs, tops = [], []
        for h in range(2):
            keep = low if h == 0 else jnp.logical_not(low)
            q_one = jnp.where(keep, q_pair, jnp.zeros_like(q_pair))
            rbuf[...] = nn(q_hot, table[2 * pair + h]).astype(BF)

            def score_step(c, top, q_one=q_one, q_doc=q_doc):
                rows = pl.ds(pl.multiple_of(c * CHUNK, CHUNK), CHUNK)
                s = jnp.where(q_doc == doc_row[c], nt(q_one, k[rows, :]), NEG)
                sbuf[c] = s
                return jnp.maximum(top, jnp.max(s, axis=1, keepdims=True))

            top = lax.fori_loop(lo, hi, score_step, jnp.full((HALF, 1), NEG, F32))
            acc[...] = jnp.zeros_like(acc)

            def mix_step(c, total, top=top):
                rows = pl.ds(pl.multiple_of(c * CHUNK, CHUNK), CHUNK)
                e = jnp.exp(sbuf[c] - top)
                lookup = nt(rbuf[...], hot[rows, :])
                acc[...] += nn((e * lookup).astype(BF), v[rows, :])
                return total + jnp.sum(e, axis=1, keepdims=True)

            total = lax.fori_loop(lo, hi, mix_step, jnp.zeros((HALF, 1), F32))
            outs.append(acc[...] / total)
            tops.append(top + jnp.log(total))
        ctx[scal[2] ^ qb] = jnp.where(low, outs[0], outs[1]).astype(BF)
        lane = lax.broadcasted_iota(jnp.int32, (1, 128), 1)
        both = jnp.where(lane == 0, tops[0], jnp.where(lane == 1, tops[1], 0.0))
        lse[0, :, qb * HALF : (qb + 1) * HALF] = both.T[0:8, :]


def attend_back_kernel(
    scal,
    pos_col,
    pos_row,
    doc_col,
    doc_row,
    q,
    k,
    v,
    ma,
    mb,
    ctx,
    dctx_mine,
    dctx_other,
    lse,
    dq,
    own,
    halo,
    grad_table,
    table,
    hot,
    hot_turned,
    rbuf,
    dk,
    dv,
    dq_acc,
    tt,
    tg,
    sem,
):
    pair = pl.program_id(0)

    @pl.when(pair == 0)
    def _():
        copies = load_table(scal, (ma, mb), table, sem)
        fill_hot(pos_col, hot)
        fill_hot_turned(pos_row, hot_turned)
        for copy in copies:
            copy.wait()

    low = head_lanes()
    side = scal[2]
    dk[...] = jnp.zeros_like(dk)
    dv[...] = jnp.zeros_like(dv)
    lane = lax.broadcasted_iota(jnp.int32, (8, 128), 1)
    row8 = lax.broadcasted_iota(jnp.int32, (8, 128), 0)
    pick = jnp.where((lane < HDIM) == (row8 == 0), 1.0, 0.0)
    for qb in range(2):
        lo, hi = scal[3 + 2 * qb], scal[4 + 2 * qb]
        q_pair = q[qb * HALF : (qb + 1) * HALF, :]
        d_pair = jnp.where(side == qb, dctx_mine[...], dctx_other[...])
        c_pair = ctx[side ^ qb]
        deltas = nt(pick, d_pair.astype(F32) * c_pair.astype(F32), HIGH)
        q_doc = doc_row[2 + qb]
        q_hot = hot[GROUP + qb * HALF : GROUP + (qb + 1) * HALF, :]
        for h in range(2):
            keep = low if h == 0 else jnp.logical_not(low)
            q_one = jnp.where(keep, q_pair, jnp.zeros_like(q_pair))
            d_one = jnp.where(keep, d_pair, jnp.zeros_like(d_pair))
            delta = deltas[h : h + 1, :]
            top = lse[0, h : h + 1, qb * HALF : (qb + 1) * HALF]
            rbuf[...] = nn(q_hot, table[2 * pair + h]).astype(BF)
            dq_acc[h] = jnp.zeros((HALF, 128), F32)
            tt[...] = jnp.zeros_like(tt)

            def step(c, carry, q_one=q_one, d_one=d_one, delta=delta, top=top, q_doc=q_doc, h=h):
                rows = pl.ds(pl.multiple_of(c * CHUNK, CHUNK), CHUNK)
                k_c = k[rows, :]
                s = nt(k_c, q_one)
                p = jnp.exp(jnp.where(doc_col[rows, :] == q_doc, s - top, NEG))
                lookup = nt(hot[rows, :], rbuf[...])
                dm = nt(v[rows, :], d_one)
                mixed = p * lookup
                dlook = p * dm
                ds = (mixed * dm - p * delta).astype(BF)
                dv[rows, :] += nn(mixed.astype(BF), d_one)
                dk[rows, :] += nn(ds, q_one)
                dq_acc[h] += tn(ds, k_c)
                tt[...] += nn(hot_turned[c], dlook.astype(BF))
                return carry

            lax.fori_loop(lo, hi, step, 0)
            piece = nt(hot_turned[2 + qb], tt[...].astype(BF))
            if qb == 0:
                tg[h] = piece
            else:
                tg[h] += piece
        dq[qb * HALF : (qb + 1) * HALF, :] = (
            jnp.where(low, dq_acc[0], dq_acc[1]) * 0.125
        ).astype(BF)
    own[0] = dk[GROUP : 2 * GROUP, :]
    own[1] = dv[GROUP : 2 * GROUP, :]
    halo[0, 0] = dk[:GROUP, :].astype(BF)
    halo[0, 1] = dv[:GROUP, :].astype(BF)
    halo[1, 0] = dk[2 * GROUP :, :].astype(BF)
    halo[1, 1] = dv[2 * GROUP :, :].astype(BF)
    for h in range(2):
        for cr in range(2):
            for t in range(8):
                ur = (t >> 2) | (t & 2) | ((t & 1) << 2)
                row = (2 * (ur ^ scal[0]) + (scal[1] ^ cr)) * 32
                grad_table[cr, t, h] = tg[h, pl.ds(pl.multiple_of(row, 32), 32), :].astype(BF)


def norm_stats(values):
    center = values - jnp.mean(values, axis=-1, keepdims=True)
    rstd = lax.rsqrt(jnp.mean(center * center, axis=-1, keepdims=True) + EPS)
    return center * rstd, rstd


def norm_back(grad, unit, rstd, gain):
    scaled = grad * gain
    return rstd * (
        scaled
        - jnp.mean(scaled, axis=-1, keepdims=True)
        - unit * jnp.mean(scaled * unit, axis=-1, keepdims=True)
    )


def column_sum(values):
    return jnp.sum(values, axis=0, keepdims=True)


def ffn_kernel(
    scal,
    x,
    ctx_mine,
    ctx_other,
    cot,
    small,
    bup,
    wg,
    lay,
    dh1,
    dctx,
    act,
    ddown,
    nlow,
    dup,
    ctxt,
    dattn,
    sums,
    wm,
    wu,
    wd,
    slope,
    hidden,
    sem,
):
    copies = []
    n = 0
    for c in range(2):
        for piece, (r, l) in enumerate(((192, 0), (192, OWN), (208, 0))):
            copies.append(
                pltpu.make_async_copy(
                    wg.at[:, c, r : r + 16, l : l + OWN],
                    wm.at[:, piece * 16 : piece * 16 + 16, c * OWN : (c + 1) * OWN],
                    sem.at[n],
                )
            )
            n += 1
    for c in range(2):
        for j in range(2):
            copies.append(
                pltpu.make_async_copy(
                    wg.at[:, c, 96 + 48 * j : 144 + 48 * j, :], wu.at[2 * c + j], sem.at[n]
                )
            )
            n += 1
    for c in range(2):
        copies.append(pltpu.make_async_copy(wg.at[:, c, 0:96, :], wd.at[:, c], sem.at[n]))
        n += 1
    for copy in copies:
        copy.start()
    even = scal[2] == 0
    mine, other = ctx_mine[...], ctx_other[...]
    ctxt[:, :OWN] = jnp.where(even, mine, other)
    ctxt[:, OWN:] = jnp.where(even, other, mine)
    for copy in copies[:6]:
        copy.wait()
    merge = wm[...].reshape(D, D)
    h1 = x[...].astype(F32) + (nn(ctxt[...], merge) + small[0:1, :])
    unit1, rstd1 = norm_stats(h1)
    normed = unit1 * small[4:5, :] + small[2:3, :]
    nlow[...] = normed.astype(BF)
    hidden[...] = normed + small[1:2, :]
    for copy in copies[6:]:
        copy.wait()

    def widen(i, carry):
        up = nn(nlow[...], wu[i].reshape(D, D)) + bup[i]
        half_cdf = 0.5 * (1.0 + lax.erf(up * 0.7071067811865476))
        act[i] = (up * half_cdf).astype(BF)
        slope[i] = half_cdf + up * (0.3989422804014327 * jnp.exp(-0.5 * up * up))
        return carry

    lax.fori_loop(0, 4, widen, 0)

    def shrink(i, carry):
        rows = wd[pl.ds(4 * i, 4)].reshape(D, D)
        hidden[...] += nn(act[i], rows)
        return carry

    lax.fori_loop(0, 4, shrink, 0)
    unit2, rstd2 = norm_stats(hidden[...])
    gain2 = small[5:6, :]
    lay[...] = (unit2 * gain2 + small[3:4, :]).astype(BF)
    dy = cot[...].astype(F32)
    sums[3:4, :] = column_sum(dy)
    sums[5:6, :] = column_sum(dy * unit2)
    dh2 = norm_back(dy, unit2, rstd2, gain2)
    ddown[...] = dh2.astype(BF)
    sums[1:2, :] = column_sum(ddown[...].astype(F32))
    hidden[...] = dh2

    def back(i, carry):
        rows = wd[pl.ds(4 * i, 4)].reshape(D, D)
        grad = (nt(ddown[...], rows) * slope[i]).astype(BF)
        dup[i] = grad
        sums[pl.ds(8 + i, 1), :] = column_sum(grad.astype(F32))
        hidden[...] += nt(grad, wu[i].reshape(D, D))
        return carry

    lax.fori_loop(0, 4, back, 0)
    dnormed = hidden[...]
    sums[2:3, :] = column_sum(dnormed)
    sums[4:5, :] = column_sum(dnormed * unit1)
    grad1 = norm_back(dnormed, unit1, rstd1, small[4:5, :])
    dh1[...] = grad1
    low = grad1.astype(BF)
    dattn[...] = low
    sums[0:1, :] = column_sum(low.astype(F32))
    sums[6:8, :] = jnp.zeros((2, D), F32)
    sums[12:16, :] = jnp.zeros((4, D), F32)
    grad_ctx = nt(low, merge).astype(BF)
    left, right = grad_ctx[:, :OWN], grad_ctx[:, OWN:]
    dctx[0] = jnp.where(even, left, right)
    dctx[1] = jnp.where(even, right, left)


def weight_grad_kernel(act, ddown, nlow, dup, ctxt, dattn, out):
    for i in range(4):
        g = tn(act[i], ddown[...]).astype(BF)
        out[4 * i : 4 * i + 4, :, 0:96, :] = g.reshape(4, 2, 96, D)
    for i in range(4):
        g = tn(nlow[...], dup[i]).astype(BF).reshape(16, 48, D)
        out[:, i // 2, 96 + 48 * (i % 2) : 144 + 48 * (i % 2), :] = g
    g = tn(ctxt[...], dattn[...]).astype(BF).reshape(16, 48, D)
    for c in range(2):
        half = g[:, :, c * OWN : (c + 1) * OWN]
        out[:, c, 192:208, 0:OWN] = half[:, 0:16]
        out[:, c, 192:208, OWN:] = half[:, 16:32]
        out[:, c, 208:224, 0:OWN] = half[:, 32:48]
        out[:, c, 208:224, OWN:] = jnp.zeros((16, 16, OWN), BF)


def project_back_kernel(
    scal, xg, dq, own, left, right, dh1, wa, wb, gw, dx, dx_send, sums, w, dqkv, gbuf, sem
):
    copies = load_projection(scal, (wa, wb), w, sem)
    dqkv[:, :OWN] = dq[...]
    for i in range(2):
        total = own[i] + left[i].astype(F32) + right[i].astype(F32)
        dqkv[:, (1 + i) * OWN : (2 + i) * OWN] = total.astype(BF)
    grad = dqkv[...]
    sums[...] = jnp.broadcast_to(column_sum(grad.astype(F32)), sums.shape)
    gbuf[...] = tn(xg[...], grad)
    for cr in range(2):
        for t in range(8):
            ur = (t >> 2) | (t & 2) | ((t & 1) << 2)
            row = (scal[1] ^ cr) * OWN + (ur ^ scal[0]) * 48
            gw[cr, t] = gbuf[pl.ds(pl.multiple_of(row, 16), 48), :].astype(BF)
    for copy in copies:
        copy.wait()
    side = scal[2]
    mine = dqkv[pl.ds(pl.multiple_of(side * HALF, HALF), HALF), :]
    other = dqkv[pl.ds(pl.multiple_of((1 - side) * HALF, HALF), HALF), :]
    dx[...] = dh1[...] + nt(mine, w[...])
    dx_send[...] = nt(other, w[...]).astype(BF)


SMEM = pl.BlockSpec(memory_space=pltpu.SMEM)
VM = pl.BlockSpec(memory_space=pltpu.VMEM)
HBM = pl.BlockSpec(memory_space=pl.ANY)


def params(mib, **more):
    return pltpu.CompilerParams(vmem_limit_bytes=mib * 1024 * 1024, **more)


def cost(flops, moved, transcendentals=0):
    return pl.CostEstimate(
        flops=int(flops), bytes_accessed=int(moved), transcendentals=int(transcendentals)
    )


def shape(dims, kind):
    return jax.ShapeDtypeStruct(dims, kind)


def project(scal, pieces, wa, wb, bias):
    return pl.pallas_call(
        project_kernel,
        name="project",
        out_shape=(
            shape((GROUP, OWN), BF),
            shape((WINDOW, OWN), BF),
            shape((WINDOW, OWN), BF),
            shape((GROUP, D), BF),
        ),
        in_specs=[SMEM] + [VM] * 6 + [HBM] * 2 + [VM],
        out_specs=[VM] * 4,
        scratch_shapes=[
            pltpu.VMEM((WINDOW, D), BF),
            pltpu.VMEM((D, 3 * OWN), BF),
            pltpu.SemaphoreType.DMA((16,)),
        ],
        compiler_params=params(32),
        cost_estimate=cost(2 * WINDOW * D * 1000, 8e6),
    )(scal, *pieces, wa, wb, bias)


def attend(scal, pos_col, doc_col, doc_row, q, k, v, ma, mb):
    whole = lambda *dims: pl.BlockSpec(dims, lambda p: (0,) * len(dims))
    return pl.pallas_call(
        attend_kernel,
        name="attend",
        grid=(3,),
        out_shape=(shape((2, HALF, OWN), BF), shape((3, 8, GROUP), F32)),
        in_specs=[
            SMEM,
            whole(WINDOW, 1),
            whole(WINDOW, 1),
            whole(6, 1, CHUNK),
            pl.BlockSpec((GROUP, 128), lambda p: (0, p)),
            pl.BlockSpec((WINDOW, 128), lambda p: (0, p)),
            pl.BlockSpec((WINDOW, 128), lambda p: (0, p)),
            HBM,
            HBM,
        ],
        out_specs=[
            pl.BlockSpec((2, HALF, 128), lambda p: (0, 0, p)),
            pl.BlockSpec((1, 8, GROUP), lambda p: (p, 0, 0)),
        ],
        scratch_shapes=[
            pltpu.VMEM((6, MPOS, MPOS), BF),
            pltpu.VMEM((WINDOW, MPOS), BF),
            pltpu.VMEM((6, HALF, CHUNK), F32),
            pltpu.VMEM((HALF, MPOS), BF),
            pltpu.VMEM((HALF, 128), F32),
            pltpu.SemaphoreType.DMA((16,)),
        ],
        compiler_params=params(32),
        cost_estimate=cost(20e9, 10e6, 5e6),
    )(scal, pos_col, doc_col, doc_row, q, k, v, ma, mb)


def attend_back(scal, pos_col, pos_row, doc_col, doc_row, q, k, v, ma, mb, ctx, mine, other, lse):
    whole = lambda *dims: pl.BlockSpec(dims, lambda p: (0,) * len(dims))
    return pl.pallas_call(
        attend_back_kernel,
        name="attend_back",
        grid=(3,),
        out_shape=(
            shape((GROUP, OWN), BF),
            shape((2, GROUP, OWN), F32),
            shape((2, 2, GROUP, OWN), BF),
            shape((2, 8, 6, 32, MPOS), BF),
        ),
        in_specs=[
            SMEM,
            whole(WINDOW, 1),
            whole(6, 1, CHUNK),
            whole(WINDOW, 1),
            whole(6, 1, CHUNK),
            pl.BlockSpec((GROUP, 128), lambda p: (0, p)),
            pl.BlockSpec((WINDOW, 128), lambda p: (0, p)),
            pl.BlockSpec((WINDOW, 128), lambda p: (0, p)),
            HBM,
            HBM,
            pl.BlockSpec((2, HALF, 128), lambda p: (0, 0, p)),
            pl.BlockSpec((HALF, 128), lambda p: (0, p)),
            pl.BlockSpec((HALF, 128), lambda p: (0, p)),
            pl.BlockSpec((1, 8, GROUP), lambda p: (p, 0, 0)),
        ],
        out_specs=[
            pl.BlockSpec((GROUP, 128), lambda p: (0, p)),
            pl.BlockSpec((2, GROUP, 128), lambda p: (0, 0, p)),
            pl.BlockSpec((2, 2, GROUP, 128), lambda p: (0, 0, 0, p)),
            pl.BlockSpec((2, 8, 2, 32, MPOS), lambda p: (0, 0, p, 0, 0)),
        ],
        scratch_shapes=[
            pltpu.VMEM((6, MPOS, MPOS), BF),
            pltpu.VMEM((WINDOW, MPOS), BF),
            pltpu.VMEM((6, MPOS, CHUNK), BF),
            pltpu.VMEM((HALF, MPOS), BF),
            pltpu.VMEM((WINDOW, 128), F32),
            pltpu.VMEM((WINDOW, 128), F32),
            pltpu.VMEM((2, HALF, 128), F32),
            pltpu.VMEM((MPOS, HALF), F32),
            pltpu.VMEM((2, MPOS, MPOS), F32),
            pltpu.SemaphoreType.DMA((16,)),
        ],
        compiler_params=params(40),
        cost_estimate=cost(50e9, 20e6, 5e6),
    )(scal, pos_col, pos_row, doc_col, doc_row, q, k, v, ma, mb, ctx, mine, other, lse)


def feed_forward(scal, x, mine, other, cot, small, bup, wg):
    return pl.pallas_call(
        ffn_kernel,
        name="feed_forward",
        out_shape=(
            shape((HALF, D), BF),
            shape((HALF, D), F32),
            shape((2, HALF, OWN), BF),
            shape((4, HALF, D), BF),
            shape((HALF, D), BF),
            shape((HALF, D), BF),
            shape((4, HALF, D), BF),
            shape((HALF, D), BF),
            shape((HALF, D), BF),
            shape((16, D), F32),
        ),
        in_specs=[SMEM] + [VM] * 6 + [HBM],
        out_specs=[VM] * 10,
        scratch_shapes=[
            pltpu.VMEM((16, 48, D), BF),
            pltpu.VMEM((4, 16, 48, D), BF),
            pltpu.VMEM((16, 2, 96, D), BF),
            pltpu.VMEM((4, HALF, D), F32),
            pltpu.VMEM((HALF, D), F32),
            pltpu.SemaphoreType.DMA((12,)),
        ],
        compiler_params=params(50),
        cost_estimate=cost(6e9, 20e6, 2e6),
    )(scal, x, mine, other, cot, small, bup, wg)


def weight_grads(act, ddown, nlow, dup, ctxt, dattn):
    return pl.pallas_call(
        weight_grad_kernel,
        name="weight_grads",
        out_shape=shape((16, 2, 224, D), BF),
        in_specs=[VM] * 6,
        out_specs=VM,
        compiler_params=params(50),
        cost_estimate=cost(3e9, 15e6),
    )(act, ddown, nlow, dup, ctxt, dattn)


def project_back(scal, xg, dq, own, left, right, dh1, wa, wb):
    return pl.pallas_call(
        project_back_kernel,
        name="project_back",
        out_shape=(
            shape((2, 8, 48, 3 * OWN), BF),
            shape((HALF, D), F32),
            shape((HALF, D), BF),
            shape((8, 3 * OWN), F32),
        ),
        in_specs=[SMEM] + [VM] * 6 + [HBM] * 2,
        out_specs=[VM] * 4,
        scratch_shapes=[
            pltpu.VMEM((D, 3 * OWN), BF),
            pltpu.VMEM((GROUP, 3 * OWN), BF),
            pltpu.VMEM((D, 3 * OWN), F32),
            pltpu.SemaphoreType.DMA((16,)),
        ],
        compiler_params=params(40),
        cost_estimate=cost(2e9, 12e6),
    )(scal, xg, dq, own, left, right, dh1, wa, wb)


def swap(value, axis, bit):
    count = lax.axis_size(axis)
    return lax.ppermute(value, axis, [(i, i ^ bit) for i in range(count)])


def shifted(value, axis, steps):
    count = lax.axis_size(axis)
    leading, last = (max(0, -steps), min(count, count - steps))
    return lax.ppermute(value, axis, [(source, source + steps) for source in range(leading, last)])


def gather_steps(value, steps):
    for axis, bit in steps:
        value = jnp.stack([value, swap(value, axis, bit)], axis=0)
    return value


def reduce_steps(value, steps):
    for axis, bit in steps:
        got = swap(value[1], axis, bit)
        value = (value[0].astype(F32) + got.astype(F32)).astype(value.dtype)
    return value


def by_core(core, mine, other, axis):
    first = jnp.where(core == 0, mine, other)
    second = jnp.where(core == 0, other, mine)
    return jnp.concatenate([first, second], axis=axis)


def locate(index, opening, finish, stream_rows):
    document = jnp.sum((finish[None, :] <= index[:, None]).astype(jnp.int32), axis=1)
    begin = jnp.max(jnp.where(opening[None, :] <= index[:, None], opening[None, :], 0), axis=1)
    inside = (index >= 0) & (index < stream_rows)
    document = jnp.where(inside, document, -1)
    position = (index - begin) % MPOS
    return document, position


def per_device(
    incoming_state,
    projection_matrix_triple,
    merge_matrix,
    widen_matrix,
    shrink_matrix,
    offset_table,
    norm_scales,
    widen_offset,
    trainable_gate_scores,
    gate_perturbation,
    softening_scale,
    passage_extents,
    result_cotangent,
):
    BOTH = ("seq", "fsdp")
    ns, nf = lax.axis_size("seq"), lax.axis_size("fsdp")
    count = ns * nf
    fast = nf == 16
    side, place = lax.axis_index("seq"), lax.axis_index("fsdp")
    tokens = incoming_state.reshape(HALF, D)
    cot = result_cotangent.reshape(HALF, D)
    stream_rows = GROUP * nf
    rows = projection_matrix_triple.shape[0]

    before = shifted(tokens, "fsdp", 1)
    after = shifted(tokens, "fsdp", -1)
    other_tokens = swap(tokens, "seq", 1)
    other_before = swap(before, "seq", 1)
    other_after = swap(after, "seq", 1)

    relaxed = jax.nn.sigmoid(
        (trainable_gate_scores + gate_perturbation) / softening_scale[:, None, None]
    )
    relaxed_low = relaxed.astype(BF)

    packed = jnp.concatenate(
        [offset_table.T.reshape(-1), norm_scales.T.reshape(-1), widen_offset]
    )
    heads_weight = projection_matrix_triple.reshape(rows, 3, 2, OWN)
    if fast:
        core = place % 2
        unit = place // 2
        own_cols = lax.dynamic_index_in_dim(heads_weight, side, 2, False).reshape(rows, 3 * OWN)
        sent_cols = lax.dynamic_index_in_dim(heads_weight, 1 - side, 2, False).reshape(
            rows, 3 * OWN
        )
        got_cols = swap(sent_cols, "seq", 1)
        for_me = jnp.where(core == side, own_cols, got_cols)
        for_core = jnp.where(core == side, got_cols, own_cols)
        wq = by_core(core, for_me, swap(for_core, "fsdp", 1), 0)
        wq = gather_steps(wq, (("fsdp", 8), ("fsdp", 4), ("fsdp", 2)))
        wa = wq.transpose(2, 1, 0, 3, 4).reshape(8, 48, 3 * OWN)
        wb = swap(wa, "fsdp", 1)
        ma = gather_steps(relaxed_low, (("fsdp", 8), ("fsdp", 4), ("fsdp", 2)))
        ma = ma.transpose(2, 1, 0, 3, 4, 5).reshape(8, 6, 32, MPOS)
        mb = swap(ma, "fsdp", 1)
        me = side * 16 + place
        small_rel = gather_steps(
            packed[None, :],
            (("fsdp", 1), ("fsdp", 2), ("fsdp", 4), ("fsdp", 8), ("seq", 1)),
        ).reshape(count, -1)
        index = jnp.arange(count, dtype=jnp.int32)
        turn = ((index[:, None] ^ me) == index[None, :]).astype(BF)
        small_all = jnp.dot(turn, small_rel, preferred_element_type=F32)
        wide = jnp.concatenate([widen_matrix.reshape(rows, 2, FF // 2), merge_matrix.reshape(rows, 2, OWN)], axis=2)
        mine = lax.dynamic_index_in_dim(wide, core, 1, False)
        sent = lax.dynamic_index_in_dim(wide, 1 - core, 1, False)
        wide = by_core(core, mine, swap(sent, "fsdp", 1), 0)
        merged = wide[:, FF // 2 :]
        shard = jnp.concatenate(
            [
                shrink_matrix,
                wide[:, :D],
                wide[:, D : 2 * D],
                jnp.concatenate([merged[0:16], merged[16:32]], axis=1),
                jnp.concatenate([merged[32:48], jnp.zeros((16, OWN), BF)], axis=1),
            ],
            axis=0,
        )
        wg = lax.all_gather(shard, BOTH, axis=0, tiled=True).reshape(16, 2, 224, D)
    else:
        core = jnp.zeros((), jnp.int32)
        unit = jnp.zeros((), jnp.int32)
        full = lax.all_gather(projection_matrix_triple, BOTH, axis=0, tiled=True)
        full = lax.dynamic_index_in_dim(full.reshape(D, 3, 2, OWN), side, 2, False)
        full = full.reshape(2, 8, 48, 3 * OWN)
        wa, wb = full[0], full[1]
        table = lax.all_gather(relaxed_low, "fsdp", axis=1, tiled=True)
        table = table.reshape(6, 8, 2, 32, MPOS).transpose(2, 1, 0, 3, 4)
        ma, mb = table[0], table[1]
        small_all = lax.all_gather(packed, BOTH, axis=0, tiled=True).reshape(count, -1).astype(F32)
        up = lax.all_gather(widen_matrix, BOTH, axis=0, tiled=True)
        up = up.reshape(16, 48, 2, 2, D).transpose(0, 2, 3, 1, 4).reshape(16, 2, 96, D)
        down = lax.all_gather(shrink_matrix, BOTH, axis=0, tiled=True).reshape(16, 2, 96, D)
        out = lax.all_gather(merge_matrix, BOTH, axis=0, tiled=True)
        out = out.reshape(16, 3, 16, 2, OWN).transpose(0, 3, 1, 2, 4)
        out = jnp.concatenate([out, jnp.zeros((16, 2, 1, 16, OWN), BF)], axis=2)
        out = out.reshape(16, 2, 2, 2, 16, OWN).transpose(0, 1, 2, 4, 3, 5).reshape(16, 2, 32, D)
        wg = jnp.concatenate([down, up, out], axis=2)
    wide_cols = D // count
    biases = small_all[:, : 6 * wide_cols].reshape(D, 6)
    gains = small_all[:, 6 * wide_cols : 8 * wide_cols].reshape(D, 2)
    bup = small_all[:, 8 * wide_cols :].reshape(4, 1, D)
    small = jnp.concatenate([biases[:, 2:].T, gains.T, jnp.zeros((2, D), F32)], axis=0)
    head_bias = lax.dynamic_slice_in_dim(biases[:, :2], side * OWN, OWN, 0)
    qkv_bias = jnp.concatenate(
        [head_bias[:, 0], jnp.zeros((OWN,), F32), head_bias[:, 1]]
    ).reshape(1, 3 * OWN)

    finish = jnp.cumsum(passage_extents)
    opening = finish - passage_extents
    base = place * GROUP - GROUP
    doc, pos = locate(
        base + jnp.arange(WINDOW, dtype=jnp.int32), opening, finish, stream_rows
    )
    edges = base + GROUP + jnp.asarray([0, HALF - 1, HALF, GROUP - 1], jnp.int32)
    edge_begin = jnp.max(jnp.where(opening[None, :] <= edges[:, None], opening[None, :], 0), axis=1)
    edge_end = jnp.min(
        jnp.where(finish[None, :] > edges[:, None], finish[None, :], stream_rows), axis=1
    )
    lows = jnp.clip((edge_begin - base) // CHUNK, 0, 6)
    highs = jnp.clip((edge_end - base + CHUNK - 1) // CHUNK, 0, 6)
    scal = jnp.stack([unit, core, side, lows[0], highs[1], lows[2], highs[3], core]).astype(
        jnp.int32
    )
    pos_col, doc_col = pos.reshape(WINDOW, 1), doc.reshape(WINDOW, 1)
    pos_row, doc_row = pos.reshape(6, 1, CHUNK), doc.reshape(6, 1, CHUNK)

    pieces = (tokens, before, after, other_tokens, other_before, other_after)
    q, k, v, group_tokens = project(scal, pieces, wa, wb, qkv_bias)
    ctx, lse = attend(scal, pos_col, doc_col, doc_row, q, k, v, ma, mb)
    ctx_other = swap(ctx[1], "seq", 1)
    (lay, dh1, dctx, act, ddown, nlow, dup, ctxt, dattn, sums) = feed_forward(
        scal, tokens, ctx[0], ctx_other, cot, small, bup, wg
    )
    dctx_other = swap(dctx[1], "seq", 1)
    gg = weight_grads(act, ddown, nlow, dup, ctxt, dattn)
    dq, own, halo, grad_table = attend_back(
        scal, pos_col, pos_row, doc_col, doc_row, q, k, v, ma, mb, ctx, dctx[0], dctx_other, lse
    )
    from_right = shifted(halo[0], "fsdp", -1)
    from_left = shifted(halo[1], "fsdp", 1)
    gw, dx, dx_send, qkv_sums = project_back(
        scal, group_tokens, dq, own, from_left, from_right, dh1, wa, wb
    )
    input_grad = dx + swap(dx_send, "seq", 1).astype(F32)

    own_sums = jnp.stack([qkv_sums[0, :OWN], qkv_sums[0, 2 * OWN :]], axis=0)
    blank = jnp.zeros_like(own_sums)
    head_sums = jnp.concatenate(
        [jnp.where(side == 0, own_sums, blank), jnp.where(side == 0, blank, own_sums)], axis=1
    )
    bias_sums = jnp.concatenate([head_sums, sums[0:4]], axis=0)
    small_grads = jnp.concatenate(
        [
            bias_sums.reshape(6, count, wide_cols).transpose(1, 0, 2).reshape(count, -1),
            sums[4:6].reshape(2, count, wide_cols).transpose(1, 0, 2).reshape(count, -1),
            sums[8:12].reshape(count, FF // count),
        ],
        axis=1,
    )
    if fast:
        order = turn.astype(F32)
        small_grads = jnp.dot(order, small_grads, precision=HIGH, preferred_element_type=F32)
        small_mine = reduce_steps(
            small_grads.reshape(2, 2, 2, 2, 2, -1),
            (("seq", 1), ("fsdp", 8), ("fsdp", 4), ("fsdp", 2), ("fsdp", 1)),
        )
        shard = lax.psum_scatter(
            gg.reshape(32 * 224, D), BOTH, scatter_dimension=0, tiled=True
        )
        table_total = reduce_steps(
            grad_table.reshape(2, 2, 2, 2, 6, 32, MPOS),
            (("fsdp", 1), ("fsdp", 2), ("fsdp", 4), ("fsdp", 8)),
        ).astype(F32)
        own_rows = reduce_steps(
            gw.reshape(2, 2, 2, 2, 48, 3 * OWN),
            (("fsdp", 1), ("fsdp", 2), ("fsdp", 4), ("fsdp", 8)),
        ).reshape(2, rows, 3 * OWN)
        mine = lax.dynamic_index_in_dim(own_rows, core, 0, False)
        got = swap(lax.dynamic_index_in_dim(own_rows, 1 - core, 0, False), "fsdp", 1)
        to_keep = jnp.where(core == side, mine, got)
        to_send = jnp.where(core == side, got, mine)
        both = by_core(
            side,
            to_keep.reshape(rows, 3, 1, OWN),
            swap(to_send, "seq", 1).reshape(rows, 3, 1, OWN),
            2,
        )
        grad_w_qkv = both.reshape(rows, 3 * D).astype(F32)
        grad_w_down = shard[0:96].astype(F32)
        merged = jnp.concatenate(
            [shard[192:208, :OWN], shard[192:208, OWN:], shard[208:224, :OWN]], axis=0
        )
        wide = jnp.concatenate([shard[96:144], shard[144:192], merged], axis=1)
        wide = wide.reshape(2, rows, 2 * D + OWN)
        mine = lax.dynamic_index_in_dim(wide, core, 0, False)
        got = swap(lax.dynamic_index_in_dim(wide, 1 - core, 0, False), "fsdp", 1)
        grad_w_up = by_core(core, mine[:, : 2 * D], got[:, : 2 * D], 1).astype(F32)
        grad_w_out = by_core(core, mine[:, 2 * D :], got[:, 2 * D :], 1).astype(F32)
    else:
        scatter = partial(lax.psum_scatter, axis_name=BOTH, scatter_dimension=0, tiled=True)
        small_mine = scatter(small_grads.reshape(-1))
        table = grad_table.reshape(2, 2, 2, 2, 6, 32, MPOS).transpose(4, 3, 2, 1, 0, 5, 6)
        table_total = lax.psum_scatter(
            table.reshape(6, MPOS, MPOS), "fsdp", scatter_dimension=1, tiled=True
        ).astype(F32)
        head_rows = gw.reshape(2, 2, 2, 2, 48, 3, 1, OWN).transpose(0, 3, 2, 1, 4, 5, 6, 7)
        head_rows = head_rows.reshape(D, 3, 1, OWN)
        blank = jnp.zeros_like(head_rows)
        both = jnp.concatenate(
            [jnp.where(side == 0, head_rows, blank), jnp.where(side == 0, blank, head_rows)], axis=2
        )
        grad_w_qkv = scatter(both.reshape(D, 3 * D)).astype(F32)
        grad_w_down = scatter(gg[:, :, 0:96].reshape(FF, D)).astype(F32)
        wide = gg[:, :, 96:192].reshape(16, 2, 2, 48, D).transpose(0, 3, 1, 2, 4).reshape(D, FF)
        grad_w_up = scatter(wide).astype(F32)
        out = gg[:, :, 192:224].reshape(16, 2, 2, 16, 2, OWN).transpose(0, 1, 2, 4, 3, 5)
        out = out.reshape(16, 2, 4, 16, OWN)[:, :, :3].transpose(0, 2, 3, 1, 4).reshape(D, D)
        grad_w_out = scatter(out).astype(F32)
    grad_biases = small_mine[: 6 * wide_cols].reshape(6, wide_cols)
    grad_gains = small_mine[6 * wide_cols : 8 * wide_cols].reshape(2, wide_cols)
    grad_bias_up = small_mine[8 * wide_cols :]
    mask_logit_gradient = (
        table_total * relaxed * (1.0 - relaxed) / softening_scale[:, None, None]
    )
    return (
        lay.reshape(1, HALF, D),
        input_grad.reshape(1, HALF, D),
        grad_w_qkv,
        grad_w_out,
        grad_w_up,
        grad_w_down,
        grad_biases,
        grad_gains,
        grad_bias_up,
        mask_logit_gradient,
    )


def solution(mesh):
    rows = P(("seq", "fsdp"), None)
    columns = P(None, ("seq", "fsdp"))
    block = P("fsdp", "seq", None)
    table = P("seq", "fsdp", None)
    return jax.shard_map(
        per_device,
        mesh=mesh,
        in_specs=(
            block, rows, rows, rows, rows, columns, columns, P(("seq", "fsdp")),
            table, table, P("seq"), P(), block,
        ),
        out_specs=(
            block, block, rows, rows, rows, rows, columns, columns, P(("seq", "fsdp")), table,
        ),
        check_vma=False,
    )
```

```python
from functools import partial

import jax
import jax.numpy as jnp
from jax import lax
from jax.experimental import pallas as pl
from jax.experimental.pallas import tpu as pltpu
from jax.sharding import PartitionSpec as P

D = 768
FF = 3072
HEADS = 12
HDIM = 64
MPOS = 512
EPS = 1e-05
GROUP = 512
HALF = 256
WINDOW = 3 * GROUP
OWN = 384
CHUNK = 256
NEG = -1e30
BF = jnp.bfloat16
F32 = jnp.float32
HIGH = lax.Precision.HIGHEST
PART_TABLE = 144
PART_SUMS = 400
PART = 416
PART_OUT = 464
PART_MORE = 544


def nn(left, right):
    return jnp.dot(left, right, preferred_element_type=F32)


def nt(left, right, precision=None):
    return lax.dot_general(
        left, right, (((1,), (1,)), ((), ())), precision=precision, preferred_element_type=F32
    )


def tn(left, right):
    return lax.dot_general(left, right, (((0,), (0,)), ((), ())), preferred_element_type=F32)


def load_projection(gathered, w, sem):
    copies = []
    for f in range(16):
        row = (f % 2) * OWN + (f // 2) * 48
        copies.append(
            pltpu.make_async_copy(gathered.at[f, 16:25], w.at[:, row : row + 48, :], sem.at[f])
        )
    for copy in copies:
        copy.start()
    return copies


def table_of(table, head):
    return jnp.concatenate(
        [table[:, 4 * head + part].reshape(MPOS, 128) for part in range(4)], axis=1
    )


def spread_out(values, spread, owner, group):
    return jnp.sum(jnp.where(owner == group, nn(values, spread), 0.0), axis=0, keepdims=True)


def columns_of(w, first, count=3):
    return jnp.concatenate([w[first + part] for part in range(count)], axis=1)


def unit_of(t):
    return (t >> 2) | ((t & 3) << 1)


def project_kernel(
    scal,
    x1,
    x0,
    x2,
    y1,
    y0,
    y2,
    gathered,
    near,
    owner,
    spread,
    group,
    q_ref,
    k_ref,
    v_ref,
    xw,
    w,
    sem,
):
    copies = load_projection(gathered, w, sem)
    side = scal[2]
    for g, (mine, other) in enumerate(((x0, y0), (x1, y1), (x2, y2))):
        xw[pl.ds(pl.multiple_of(g * GROUP + side * HALF, HALF), HALF), :] = mine[...]
        xw[pl.ds(pl.multiple_of(g * GROUP + (1 - side) * HALF, HALF), HALF), :] = other[...]
    bias = [
        spread_out(near[i], spread[:, :OWN], owner[...], group[:, :OWN]) for i in range(2)
    ]
    for copy in copies:
        copy.wait()
    for blk in range(6):
        rows = slice(blk * HALF, (blk + 1) * HALF)
        here = xw[rows, :]
        k_ref[rows, :] = nn(here, columns_of(w, 3)).astype(BF)
        v_ref[rows, :] = (nn(here, columns_of(w, 6)) + bias[1]).astype(BF)
        if blk in (2, 3):
            local = slice((blk - 2) * HALF, (blk - 1) * HALF)
            query = (nn(here, columns_of(w, 0)) + bias[0]).astype(BF)
            q_ref[local, :] = query * jnp.asarray(0.125, BF)


def head_lanes():
    return lax.broadcasted_iota(jnp.int32, (1, 128), 1) < HDIM


def fill_hot(pos_col, hot):
    for blk in range(6):
        rows = slice(blk * 256, (blk + 1) * 256)
        column = lax.broadcasted_iota(jnp.int32, (256, MPOS), 1)
        hot[rows, :] = jnp.where(pos_col[rows, :] == column, 1.0, 0.0).astype(BF)


def fill_hot_turned(pos_row, hot):
    for blk in range(6):
        rows = lax.broadcasted_iota(jnp.int32, (MPOS, 256), 0)
        hot[blk] = jnp.where(pos_row[blk] == rows, 1.0, 0.0).astype(BF)


def set_pair(low, value, target):
    blank = jnp.zeros_like(value)
    target[:HALF, :] = jnp.where(low, value, blank)
    target[HALF:, :] = jnp.where(low, blank, value)


def fold(values, how):
    rows, columns = values.shape
    return how(values.reshape(rows // 8, 8, columns), axis=0)


def attend_kernel(
    scal,
    pos_col,
    pos_row,
    doc_col,
    doc_row,
    q,
    k,
    v,
    table,
    ctx,
    lse,
    hot,
    hot_turned,
    sbuf,
    looks,
    queries,
    acc,
):
    @pl.when(pl.program_id(0) == 0)
    def _():
        fill_hot(pos_col, hot)
        fill_hot_turned(pos_row, hot_turned)

    low = head_lanes()
    for qb in range(2):
        lo, hi = scal[3 + 2 * qb], scal[4 + 2 * qb]
        here = slice(qb * HALF, (qb + 1) * HALF)
        set_pair(low, q[here, :], queries)
        q_doc = jnp.concatenate([doc_row[2 + qb]] * 2, axis=1)
        q_hot = hot[GROUP + qb * HALF : GROUP + (qb + 1) * HALF, :]
        for h in range(2):
            looks[h * HALF : (h + 1) * HALF, :] = nn(q_hot, table_of(table, h)).astype(BF)

        def score_step(c, top, q_doc=q_doc):
            rows = pl.ds(pl.multiple_of(c * CHUNK, CHUNK), CHUNK)
            s = jnp.where(doc_col[rows, :] == q_doc, nt(k[rows, :], queries[...]), NEG)
            sbuf[c] = s
            return jnp.maximum(top, fold(s, jnp.max))

        top = lax.fori_loop(lo, hi, score_step, jnp.full((8, 2 * HALF), NEG, F32))
        top = jnp.max(top, axis=0, keepdims=True)
        acc[...] = jnp.zeros_like(acc)

        def mix_step(c, total, top=top):
            rows = pl.ds(pl.multiple_of(c * CHUNK, CHUNK), CHUNK)
            e = jnp.exp(sbuf[c] - top)
            mixed = (e * nt(hot[rows, :], looks[...])).astype(BF)
            acc[...] += tn(mixed, v[rows, :])
            return total + fold(e, jnp.sum)

        total = lax.fori_loop(lo, hi, mix_step, jnp.zeros((8, 2 * HALF), F32))
        total = jnp.sum(total, axis=0, keepdims=True)
        stat = top + jnp.log(total)
        lse[0, 0:1, here] = stat[:, :HALF]
        lse[0, 1:2, here] = stat[:, HALF:]
        lse[0, 2:8, here] = jnp.zeros((6, HALF), F32)
        inverse = 1.0 / total
        scale = jnp.concatenate(
            [
                jnp.broadcast_to(inverse[:, :HALF], (HDIM, HALF)),
                jnp.broadcast_to(inverse[:, HALF:], (HDIM, HALF)),
            ],
            axis=0,
        ).T
        ctx[qb] = (jnp.where(low, acc[:HALF, :], acc[HALF:, :]) * scale).astype(BF)


def attend_back_kernel(
    scal,
    doc_col,
    doc_row,
    q,
    k,
    v,
    table,
    hot,
    hot_turned,
    xw,
    sums,
    ctx,
    ctx_all,
    dctx,
    dattn,
    lse,
    dq,
    own,
    halo_low,
    halo_high,
    part_keep,
    part_send,
    looks,
    queries,
    grads,
    dk,
    dv,
    dq_acc,
    tt,
    tg,
    gw,
    gout,
):

    low = head_lanes()
    dk[...] = jnp.zeros_like(dk)
    dv[...] = jnp.zeros_like(dv)
    lane = lax.broadcasted_iota(jnp.int32, (8, 128), 1)
    row8 = lax.broadcasted_iota(jnp.int32, (8, 128), 0)
    pick = jnp.where((lane < HDIM) == (row8 == 0), 1.0, 0.0)
    for qb in range(2):
        lo, hi = scal[3 + 2 * qb], scal[4 + 2 * qb]
        here = slice(qb * HALF, (qb + 1) * HALF)
        d_pair = dctx[here, :]
        deltas = nt(pick, d_pair.astype(F32) * ctx[qb].astype(F32), HIGH)
        delta = jnp.concatenate([deltas[0:1, :], deltas[1:2, :]], axis=1)
        top = jnp.concatenate([lse[0, 0:1, here], lse[0, 1:2, here]], axis=1)
        set_pair(low, q[here, :], queries)
        set_pair(low, d_pair, grads)
        q_doc = jnp.concatenate([doc_row[2 + qb]] * 2, axis=1)
        q_hot = hot[GROUP + qb * HALF : GROUP + (qb + 1) * HALF, :]
        for h in range(2):
            looks[h * HALF : (h + 1) * HALF, :] = nn(q_hot, table_of(table, h)).astype(BF)
        dq_acc[...] = jnp.zeros_like(dq_acc)
        tt[...] = jnp.zeros_like(tt)

        def step(c, carry, delta=delta, top=top, q_doc=q_doc):
            rows = pl.ds(pl.multiple_of(c * CHUNK, CHUNK), CHUNK)
            k_c = k[rows, :]
            s = nt(k_c, queries[...])
            p = jnp.exp(jnp.where(doc_col[rows, :] == q_doc, s - top, NEG))
            mixed = p * nt(hot[rows, :], looks[...])
            dm = nt(v[rows, :], grads[...])
            ds = (mixed * dm - p * delta).astype(BF)
            dv[rows, :] += nn(mixed.astype(BF), grads[...])
            dk[rows, :] += nn(ds, queries[...])
            dq_acc[...] += tn(ds, k_c)
            tt[...] += nn(hot_turned[c], (p * dm).astype(BF))
            return carry

        lax.fori_loop(lo, hi, step, 0)
        for h in range(2):
            piece = nt(hot_turned[2 + qb], tt[:, h * HALF : (h + 1) * HALF].astype(BF))
            if qb == 0:
                tg[h] = piece
            else:
                tg[h] += piece
        dq[here, :] = (jnp.where(low, dq_acc[:HALF, :], dq_acc[HALF:, :]) * 0.125).astype(BF)
    own[0] = dk[GROUP : 2 * GROUP, :]
    own[1] = dv[GROUP : 2 * GROUP, :]
    halo_low[0] = dk[:GROUP, :].astype(BF)
    halo_low[1] = dv[:GROUP, :].astype(BF)
    halo_high[0] = dk[2 * GROUP :, :].astype(BF)
    halo_high[1] = dv[2 * GROUP :, :].astype(BF)
    query_grad = dq[...]
    pair_grad = jnp.concatenate([dk[...].astype(BF), dv[...].astype(BF)], axis=1)
    gw[:, 0:128] = tn(xw[GROUP : 2 * GROUP, :], query_grad)
    gw[:, 128:384] = tn(xw[...], pair_grad)
    totals = jnp.concatenate(
        [
            column_sum(query_grad.astype(F32)),
            column_sum(pair_grad[:, 128:].astype(F32)),
            jnp.zeros((14, 128), F32),
        ],
        axis=0,
    ).astype(BF)
    more = part_keep.shape[1] == PART_MORE
    if more:
        gout[...] = tn(ctx_all[...].reshape(GROUP, OWN), dattn[...])
    for cr, out in enumerate((part_keep, part_send)):
        for t in range(8):
            place = 2 * (unit_of(t) ^ scal[0]) + (scal[1] ^ cr)
            rows = [
                gw[pl.ds(pl.multiple_of(part * OWN + place * 24, 8), 24), :] for part in range(2)
            ]
            both = jnp.concatenate(rows, axis=0).astype(BF)
            for i in range(3):
                out[t, i * 48 : i * 48 + 48, :] = both[:, i * 128 : (i + 1) * 128]
            for h in range(2):
                mask = tg[h, pl.ds(pl.multiple_of(place * 32, 32), 32), :].astype(BF)
                for i in range(4):
                    at = PART_TABLE + (4 * h + i) * 32
                    out[t, at : at + 32, :] = mask[:, i * 128 : (i + 1) * 128]
            out[t, PART_SUMS:PART, :] = totals
            if more:
                rows = gout[pl.ds(pl.multiple_of(place * 24, 8), 24), :]
                slices = [rows[:, i * 128 : (i + 1) * 128] for i in range(3)]
                slices.append(jnp.zeros((8, 128), F32))
                out[t, PART_OUT:PART_MORE, :] = jnp.concatenate(slices, axis=0).astype(BF)
                for i in range(3):
                    at = PART + 16 * i
                    out[t, at : at + 16, :] = sums[:, i * 128 : (i + 1) * 128].astype(BF)


def norm_stats(values):
    center = values - jnp.mean(values, axis=-1, keepdims=True)
    rstd = lax.rsqrt(jnp.mean(center * center, axis=-1, keepdims=True) + EPS)
    return center * rstd, rstd


def norm_back(grad, unit, rstd, gain):
    scaled = grad * gain
    return rstd * (
        scaled
        - jnp.mean(scaled, axis=-1, keepdims=True)
        - unit * jnp.mean(scaled * unit, axis=-1, keepdims=True)
    )


def column_sum(values):
    return jnp.sum(values, axis=0, keepdims=True)


def load_feed(wg, sem, wm=None, wu=None, wd=None):
    copies = []

    def bring(source, target):
        copies.append(pltpu.make_async_copy(source, target, sem.at[len(copies)]))
        copies[-1].start()

    for c in range(2):
        for s in range(2):
            if wm is not None:
                bring(
                    wg.at[:, c, 192:240, s * OWN : (s + 1) * OWN],
                    wm.at[s, :, :, c * OWN : (c + 1) * OWN],
                )
            if wu is not None:
                bring(wg.at[:, c, 96 + 48 * s : 144 + 48 * s, :], wu.at[c, s])
        if wd is not None:
            bring(wg.at[:, c, 0:96, :], wd.at[:, c])
    return copies


def shrink_rows(wd, i):
    return wd[pl.ds(4 * i, 4)].reshape(D, D)


def rows_of(i):
    return pl.ds(pl.multiple_of(i * HALF, HALF), HALF)


def both_sides(side, mine, other, target):
    target[rows_of(side), :] = mine[...]
    target[rows_of(1 - side), :] = other[...]


def feed_up_kernel(
    scal,
    x,
    ctx_mine,
    ctx_other,
    smalls,
    owner,
    near,
    near_owner,
    spread,
    group,
    spread_up,
    group_up,
    wg,
    unit1,
    rstd1,
    nlow,
    base,
    send,
    act,
    slope,
    wm,
    wu,
    wd,
    ctxt,
    bup,
    sem,
):
    copies = load_feed(wg, sem, wm, wu, wd)
    vector = lambda i: spread_out(smalls[i], spread[...], owner[...], group[...])
    bias_out, bias_down, shift1, gain1 = [vector(i) for i in (2, 3, 4, 6)]
    for n in range(2):
        bup[n] = spread_out(
            near[8], spread_up[...], near_owner[...], group_up[...] + n * (near.shape[1] // 2)
        )
    even = scal[2] == 0
    mine, other = ctx_mine[...].reshape(GROUP, OWN), ctx_other[...].reshape(GROUP, OWN)
    ctxt[:, :OWN] = jnp.where(even, mine, other)
    ctxt[:, OWN:] = jnp.where(even, other, mine)
    for copy in copies:
        copy.wait()

    def enter(i, carry):
        rows = rows_of(i)
        attn = nn(ctxt[rows, :], wm[...].reshape(D, D)) + bias_out
        unit, rstd = norm_stats(x[rows, :].astype(F32) + attn)
        unit1[rows, :] = unit
        rstd1[rows, :] = jnp.broadcast_to(rstd, (HALF, 128))
        normed = unit * gain1 + shift1
        nlow[rows, :] = normed.astype(BF)
        base[rows, :] = normed + bias_down
        return carry

    lax.fori_loop(0, 2, enter, 0)

    def widen(i, carry):
        n, rows = i >> 1, rows_of(i & 1)
        up = nn(nlow[rows, :], wu[n].reshape(D, D)) + bup[n]
        half_cdf = 0.5 * (1.0 + lax.erf(up * 0.7071067811865476))
        act[n, rows, :] = (up * half_cdf).astype(BF)
        slope[n, rows, :] = half_cdf + up * (0.3989422804014327 * jnp.exp(-0.5 * up * up))
        return carry

    lax.fori_loop(0, 4, widen, 0)

    def shrink(i, carry):
        rows = rows_of(i)
        part = nn(act[0, rows, :], shrink_rows(wd, 0)) + nn(act[1, rows, :], shrink_rows(wd, 1))
        base[rows, :] += part
        send[rows, :] = part.astype(BF)
        return carry

    lax.fori_loop(0, 2, shrink, 0)


def feed_back_kernel(
    scal,
    base,
    got,
    cot_mine,
    cot_other,
    slope,
    smalls,
    owner,
    spread,
    group,
    wg,
    lay,
    ddown,
    dup,
    base2,
    send,
    sums,
    wu,
    wd,
    cot,
    out,
    sem,
):
    copies = load_feed(wg, sem, None, wu, wd)
    vector = lambda i: spread_out(smalls[i], spread[...], owner[...], group[...])
    shift2, gain2 = vector(5), vector(7)
    side = scal[2]
    both_sides(side, cot_mine, cot_other, cot)
    sums[...] = jnp.zeros_like(sums)

    def norm(i, carry):
        rows = rows_of(i)
        unit, rstd = norm_stats(base[rows, :] + got[rows, :].astype(F32))
        out[rows, :] = (unit * gain2 + shift2).astype(BF)
        dy = cot[rows, :].astype(F32)
        sums[3:4, :] += column_sum(dy)
        sums[5:6, :] += column_sum(dy * unit)
        grad = norm_back(dy, unit, rstd, gain2)
        low = grad.astype(BF)
        ddown[rows, :] = low
        sums[1:2, :] += column_sum(low.astype(F32))
        base2[rows, :] = grad
        return carry

    lax.fori_loop(0, 2, norm, 0)
    lay[...] = out[rows_of(side), :]
    for copy in copies:
        copy.wait()

    def back(i, carry):
        n, rows = i >> 1, rows_of(i & 1)
        grad = (nt(ddown[rows, :], shrink_rows(wd, n)) * slope[n, rows, :]).astype(BF)
        dup[n, rows, :] = grad
        sums[pl.ds(8 + n, 1), :] += column_sum(grad.astype(F32))
        return carry

    lax.fori_loop(0, 4, back, 0)

    def leave(i, carry):
        rows = rows_of(i)
        part = nt(dup[0, rows, :], wu[0].reshape(D, D)) + nt(dup[1, rows, :], wu[1].reshape(D, D))
        base2[rows, :] += part
        send[rows, :] = part.astype(BF)
        return carry

    lax.fori_loop(0, 2, leave, 0)


def feed_close_kernel(
    scal,
    base,
    got,
    unit1,
    rstd1,
    sums_in,
    smalls,
    owner,
    spread,
    group,
    wg,
    dh1,
    dattn,
    dctx,
    sums,
    wm,
    grads,
    sem,
):
    copies = load_feed(wg, sem, wm)
    gain1 = spread_out(smalls[6], spread[...], owner[...], group[...])
    side = scal[2]
    sums[...] = sums_in[...]
    for copy in copies:
        copy.wait()

    def close(i, carry):
        rows = rows_of(i)
        grad = base[rows, :] + got[rows, :].astype(F32)
        unit = unit1[rows, :]
        sums[2:3, :] += column_sum(grad)
        sums[4:5, :] += column_sum(grad * unit)
        grad = norm_back(grad, unit, rstd1[rows, 0:1], gain1)
        grads[rows, :] = grad
        low = grad.astype(BF)
        dattn[rows, :] = low
        sums[0:1, :] += column_sum(low.astype(F32))
        dctx[rows, :] = nt(low, wm[side].reshape(OWN, D)).astype(BF)
        return carry

    lax.fori_loop(0, 2, close, 0)
    dh1[...] = grads[rows_of(side), :]


def weight_grad_kernel(scal, act, ddown, nlow, dup, keep, send, down, up):
    for n in range(2):
        up[n] = tn(nlow[...], dup[n])
        down[n * D : (n + 1) * D, :] = tn(act[n], ddown[...])
    for cr, out in enumerate((keep, send)):
        for t in range(8):
            place = 2 * (unit_of(t) ^ scal[0]) + (scal[1] ^ cr)
            out[t, 0:96, :] = down[pl.ds(pl.multiple_of(place * 96, 8), 96), :].astype(BF)
            parts = [
                up[n, pl.ds(pl.multiple_of(s * OWN + place * 24, 8), 24), :]
                for s in range(2)
                for n in range(2)
            ]
            out[t, 96:192, :] = jnp.concatenate(parts, axis=0).astype(BF)


def project_back_kernel(scal, parts, dh1, gathered, dx, dx_send, w, dqkv, sem):
    copies = load_projection(gathered, w, sem)
    at = 0
    for dq, own, left, right in parts:
        width = dq.shape[1]
        dqkv[:, at : at + width] = dq[...]
        for i in range(2):
            start = (1 + i) * OWN + at
            total = own[i] + left[i].astype(F32) + right[i].astype(F32)
            dqkv[:, start : start + width] = total.astype(BF)
        at += width
    for copy in copies:
        copy.wait()
    side = scal[2]
    mine = dqkv[pl.ds(pl.multiple_of(side * HALF, HALF), HALF), :]
    other = dqkv[pl.ds(pl.multiple_of((1 - side) * HALF, HALF), HALF), :]
    for part in range(3):
        cols = slice(part * 256, (part + 1) * 256)
        rows = jnp.concatenate([w[j, cols, :] for j in range(9)], axis=1)
        dx[:, cols] = dh1[:, cols] + nt(mine, rows)
        dx_send[:, cols] = nt(other, rows).astype(BF)


SMEM = pl.BlockSpec(memory_space=pltpu.SMEM)
VM = pl.BlockSpec()
HBM = pl.BlockSpec(memory_space=pl.ANY)


def params():
    return pltpu.CompilerParams(vmem_limit_bytes=60 * 1024 * 1024)


def cost(microseconds):
    return pl.CostEstimate(
        flops=int(microseconds * 1.15e9), bytes_accessed=1000, transcendentals=0
    )


def shape(dims, kind):
    return jax.ShapeDtypeStruct(dims, kind)


def project(scal, pieces, gathered, near, owner, spread, group):
    return pl.pallas_call(
        project_kernel,
        name="project",
        out_shape=(
            shape((GROUP, OWN), BF),
            shape((WINDOW, OWN), BF),
            shape((WINDOW, OWN), BF),
            shape((WINDOW, D), BF),
        ),
        in_specs=[SMEM] + [VM] * 6 + [HBM] + [VM] * 4,
        out_specs=[VM] * 4,
        scratch_shapes=[
            pltpu.VMEM((9, D, 128), BF),
            pltpu.SemaphoreType.DMA((16,)),
        ],
        compiler_params=params(),
        cost_estimate=cost(9),
    )(scal, *pieces, gathered, near, owner, spread, group)


def whole(*dims):
    return pl.BlockSpec(dims, lambda p: (0,) * len(dims))


def attend(scal, pos_col, pos_row, doc_col, doc_row, q, k, v, table):
    return pl.pallas_call(
        attend_kernel,
        name="attend",
        grid=(3,),
        out_shape=(
            shape((2, HALF, OWN), BF),
            shape((3, 8, GROUP), F32),
            shape((WINDOW, MPOS), BF),
            shape((6, MPOS, CHUNK), BF),
        ),
        in_specs=[
            SMEM,
            whole(WINDOW, 1),
            whole(6, 1, CHUNK),
            whole(WINDOW, 1),
            whole(6, 1, CHUNK),
            pl.BlockSpec((GROUP, 128), lambda p: (0, p)),
            pl.BlockSpec((WINDOW, 128), lambda p: (0, p)),
            pl.BlockSpec((WINDOW, 128), lambda p: (0, p)),
            pl.BlockSpec((16, 8, 32, 128), lambda p: (0, p, 0, 0)),
        ],
        out_specs=[
            pl.BlockSpec((2, HALF, 128), lambda p: (0, 0, p)),
            pl.BlockSpec((1, 8, GROUP), lambda p: (p, 0, 0)),
            whole(WINDOW, MPOS),
            whole(6, MPOS, CHUNK),
        ],
        scratch_shapes=[
            pltpu.VMEM((6, CHUNK, 2 * HALF), F32),
            pltpu.VMEM((2 * HALF, MPOS), BF),
            pltpu.VMEM((2 * HALF, 128), BF),
            pltpu.VMEM((2 * HALF, 128), F32),
        ],
        compiler_params=params(),
        cost_estimate=cost(26),
    )(scal, pos_col, pos_row, doc_col, doc_row, q, k, v, table)


def attend_back(
    first, pairs, scal, doc_col, doc_row, q, k, v, table, hots, xw, sums, ctx, dctx, dattn, lse
):
    columns = lambda rows: pl.BlockSpec((rows, 128), lambda p: (0, first + p))
    size = PART_MORE if pairs == 2 else PART
    return pl.pallas_call(
        attend_back_kernel,
        name=f"attend_back_{first}",
        grid=(pairs,),
        out_shape=(
            shape((GROUP, 128 * pairs), BF),
            shape((2, GROUP, 128 * pairs), F32),
            shape((2, GROUP, 128 * pairs), BF),
            shape((2, GROUP, 128 * pairs), BF),
            shape((8, size * pairs, 128), BF),
            shape((8, size * pairs, 128), BF),
        ),
        in_specs=[
            SMEM,
            whole(WINDOW, 1),
            whole(6, 1, CHUNK),
            columns(GROUP),
            columns(WINDOW),
            columns(WINDOW),
            pl.BlockSpec((16, 8, 32, 128), lambda p: (0, first + p, 0, 0)),
            whole(WINDOW, MPOS),
            whole(6, MPOS, CHUNK),
            whole(WINDOW, D),
            pl.BlockSpec((16, OWN), lambda p: (0, p)),
            pl.BlockSpec((2, HALF, 128), lambda p: (0, 0, first + p)),
            whole(2, HALF, OWN),
            columns(GROUP),
            pl.BlockSpec((GROUP, OWN), lambda p: (0, p)),
            pl.BlockSpec((1, 8, GROUP), lambda p: (first + p, 0, 0)),
        ],
        out_specs=[
            pl.BlockSpec((GROUP, 128), lambda p: (0, p)),
            pl.BlockSpec((2, GROUP, 128), lambda p: (0, 0, p)),
            pl.BlockSpec((2, GROUP, 128), lambda p: (0, 0, p)),
            pl.BlockSpec((2, GROUP, 128), lambda p: (0, 0, p)),
            pl.BlockSpec((8, size, 128), lambda p: (0, p, 0)),
            pl.BlockSpec((8, size, 128), lambda p: (0, p, 0)),
        ],
        scratch_shapes=[
            pltpu.VMEM((2 * HALF, MPOS), BF),
            pltpu.VMEM((2 * HALF, 128), BF),
            pltpu.VMEM((2 * HALF, 128), BF),
            pltpu.VMEM((WINDOW, 128), F32),
            pltpu.VMEM((WINDOW, 128), F32),
            pltpu.VMEM((2 * HALF, 128), F32),
            pltpu.VMEM((MPOS, 2 * HALF), F32),
            pltpu.VMEM((2, MPOS, MPOS), F32),
            pltpu.VMEM((D, OWN), F32),
            pltpu.VMEM((OWN, OWN), F32),
        ],
        compiler_params=params(),
        cost_estimate=cost(14 * pairs),
    )(scal, doc_col, doc_row, q, k, v, table, *hots, xw, sums, ctx, ctx, dctx, dattn, lse)


WIDEN = pltpu.VMEM((2, 2, 8, 48, D), BF)
SHRINK = pltpu.VMEM((8, 2, 96, D), BF)
MERGE = pltpu.VMEM((2, 8, 48, D), BF)


def feed_up(scal, xw, mine, other, smalls, owner, near, near_owner, spreads, wg):
    arrays = (mine, other, smalls, owner, near, near_owner, *spreads)
    return pl.pallas_call(
        feed_up_kernel,
        name="feed_up",
        grid=(1,),
        out_shape=(
            shape((GROUP, D), F32),
            shape((GROUP, 128), F32),
            shape((GROUP, D), BF),
            shape((GROUP, D), F32),
            shape((GROUP, D), BF),
            shape((2, GROUP, D), BF),
            shape((2, GROUP, D), F32),
        ),
        in_specs=[SMEM, pl.BlockSpec((GROUP, D), lambda p: (1, 0))]
        + [whole(*a.shape) for a in arrays]
        + [HBM],
        out_specs=[
            whole(GROUP, D),
            whole(GROUP, 128),
            whole(GROUP, D),
            whole(GROUP, D),
            whole(GROUP, D),
            whole(2, GROUP, D),
            whole(2, GROUP, D),
        ],
        scratch_shapes=[
            MERGE,
            WIDEN,
            SHRINK,
            pltpu.VMEM((GROUP, D), BF),
            pltpu.VMEM((2, 1, D), F32),
            pltpu.SemaphoreType.DMA((10,)),
        ],
        compiler_params=params(),
        cost_estimate=cost(10),
    )(scal, xw, *arrays, wg)


def feed_back(scal, base, got, cot, cot_other, slope, smalls, owner, spread, group, wg):
    return pl.pallas_call(
        feed_back_kernel,
        name="feed_back",
        out_shape=(
            shape((HALF, D), BF),
            shape((GROUP, D), BF),
            shape((2, GROUP, D), BF),
            shape((GROUP, D), F32),
            shape((GROUP, D), BF),
            shape((16, D), F32),
        ),
        in_specs=[SMEM] + [VM] * 9 + [HBM],
        out_specs=[VM] * 6,
        scratch_shapes=[
            WIDEN,
            SHRINK,
            pltpu.VMEM((GROUP, D), BF),
            pltpu.VMEM((GROUP, D), BF),
            pltpu.SemaphoreType.DMA((6,)),
        ],
        compiler_params=params(),
        cost_estimate=cost(9),
    )(scal, base, got, cot, cot_other, slope, smalls, owner, spread, group, wg)


def feed_close(scal, base, got, unit1, rstd1, sums, smalls, owner, spread, group, wg):
    return pl.pallas_call(
        feed_close_kernel,
        name="feed_close",
        out_shape=(
            shape((HALF, D), F32),
            shape((GROUP, D), BF),
            shape((GROUP, OWN), BF),
            shape((16, D), F32),
        ),
        in_specs=[SMEM] + [VM] * 9 + [HBM],
        out_specs=[VM] * 4,
        scratch_shapes=[
            MERGE,
            pltpu.VMEM((GROUP, D), F32),
            pltpu.SemaphoreType.DMA((4,)),
        ],
        compiler_params=params(),
        cost_estimate=cost(5),
    )(scal, base, got, unit1, rstd1, sums, smalls, owner, spread, group, wg)


def weight_grads(scal, act, ddown, nlow, dup):
    return pl.pallas_call(
        weight_grad_kernel,
        name="weight_grads",
        out_shape=(shape((8, 192, D), BF), shape((8, 192, D), BF)),
        in_specs=[SMEM] + [VM] * 4,
        out_specs=[VM] * 2,
        scratch_shapes=[pltpu.VMEM((2 * D, D), F32), pltpu.VMEM((2, D, D), F32)],
        compiler_params=params(),
        cost_estimate=cost(7),
    )(scal, act, ddown, nlow, dup)


def project_back(scal, parts, dh1, gathered):
    def kernel(scal, *refs):
        project_back_kernel(scal, [refs[:4], refs[4:8]], *refs[8:])

    return pl.pallas_call(
        kernel,
        name="project_back",
        out_shape=(shape((HALF, D), F32), shape((HALF, D), BF)),
        in_specs=[SMEM] + [VM] * 9 + [HBM],
        out_specs=[VM] * 2,
        scratch_shapes=[
            pltpu.VMEM((9, D, 128), BF),
            pltpu.VMEM((GROUP, 3 * OWN), BF),
            pltpu.SemaphoreType.DMA((16,)),
        ],
        compiler_params=params(),
        cost_estimate=cost(6),
    )(scal, *[x for part in parts for x in part], dh1, gathered)


def swap(value, axis, bit):
    count = lax.axis_size(axis)
    return lax.ppermute(value, axis, [(i, i ^ bit) for i in range(count)])


def shifted(value, axis, steps):
    count = lax.axis_size(axis)
    leading, last = (max(0, -steps), min(count, count - steps))
    return lax.ppermute(value, axis, [(source, source + steps) for source in range(leading, last)])


def tie(*values):
    return lax.optimization_barrier(values)


CORE, ALONG_Y, SIDE = ("fsdp", 1), ("fsdp", 2), ("seq", 1)


def along_z(values):
    return [swap(values[z], "fsdp", 4 * z) for z in range(1, 4)]


def add(mine, got):
    return (mine.astype(F32) + got.astype(F32)).astype(mine.dtype)


def by_core(value):
    return value.reshape(2, 4, *value.shape[1:])


def sum_core(keep, got):
    keep = by_core(keep)
    return add(keep[0], got[0]), add(keep[1], got[1])


def sum_y(keep, got):
    return tuple(add(keep[z], got[z]) for z in range(4))


def sum_z(mine, got):
    total = mine.astype(F32)
    for value in got:
        total = total + value.astype(F32)
    return total.astype(mine.dtype)


def in_order(flag, mine, other, axis):
    first = jnp.where(flag == 0, mine, other)
    second = jnp.where(flag == 0, other, mine)
    return jnp.concatenate([first, second], axis=axis)


def locate(index, opening, finish, stream_rows):
    document = jnp.sum((finish[None, :] <= index[:, None]).astype(jnp.int32), axis=1)
    begin = jnp.max(jnp.where(opening[None, :] <= index[:, None], opening[None, :], 0), axis=1)
    inside = (index >= 0) & (index < stream_rows)
    document = jnp.where(inside, document, -1)
    position = (index - begin) % MPOS
    return document, position


def own_columns(weight, nf, side, place):
    rows = weight.shape[0]
    weight = weight.reshape(rows, 3, 2, OWN)
    core = place % 2
    keep = lax.dynamic_index_in_dim(weight, side, 2, False).reshape(rows, 3 * OWN)
    give = lax.dynamic_index_in_dim(weight, 1 - side, 2, False).reshape(rows, 3 * OWN)
    straight, crossed, near = [], [], []
    for s in range(2):
        for f in range(nf):
            here = s * nf + f
            if f % 2 == s:
                straight.append((here, (1 - s) * nf + f))
            else:
                crossed.append((here, (1 - s) * nf + (f ^ 1)))
                near.append((here, s * nf + (f ^ 1)))
    axes = ("seq", "fsdp")
    same = core == side
    mine = jnp.where(same, keep, lax.ppermute(give, axes, straight))
    other = jnp.where(same, lax.ppermute(keep, axes, near), lax.ppermute(give, axes, crossed))
    return in_order(core, mine, other, 0)


def per_device(
    incoming_state,
    projection_matrix_triple,
    merge_matrix,
    widen_matrix,
    shrink_matrix,
    offset_table,
    norm_scales,
    widen_offset,
    trainable_gate_scores,
    gate_perturbation,
    softening_scale,
    passage_extents,
    result_cotangent,
):
    BOTH = ("seq", "fsdp")
    ns, nf = lax.axis_size("seq"), lax.axis_size("fsdp")
    count = ns * nf
    fast = nf == 16
    side, place = lax.axis_index("seq"), lax.axis_index("fsdp")
    tokens = incoming_state.reshape(HALF, D)
    cot = result_cotangent.reshape(HALF, D)
    stream_rows = GROUP * nf
    rows = projection_matrix_triple.shape[0]
    zero = jnp.zeros((), jnp.int32)
    core, unit = (place % 2, place // 2) if fast else (zero, zero)

    relaxed = jax.nn.sigmoid(
        (trainable_gate_scores + gate_perturbation) / softening_scale[:, None, None]
    )
    relaxed_low = relaxed.astype(BF)
    wide_cols, up_cols = D // count, FF // count
    pad_to = lambda value: jnp.pad(value, ((0, 0), (0, 128 - value.shape[1])))
    packed = jnp.concatenate(
        [
            pad_to(offset_table),
            pad_to(norm_scales),
            pad_to(widen_offset.reshape(1, up_cols)),
            jnp.zeros((7, 128), BF),
        ],
        axis=0,
    )
    lane, row = jnp.arange(D, dtype=jnp.int32)[None, :], jnp.arange(128, dtype=jnp.int32)[:, None]
    spread, group = (lane % wide_cols == row).astype(BF), lane // wide_cols
    spread_up, group_up = (lane % up_cols == row).astype(BF), lane // up_cols

    finish = jnp.cumsum(passage_extents)
    opening = finish - passage_extents
    base = place * GROUP - GROUP
    doc, pos = locate(base + jnp.arange(WINDOW, dtype=jnp.int32), opening, finish, stream_rows)
    edges = base + GROUP + jnp.asarray([0, HALF - 1, HALF, GROUP - 1], jnp.int32)
    edge_begin = jnp.max(jnp.where(opening[None, :] <= edges[:, None], opening[None, :], 0), axis=1)
    edge_end = jnp.min(
        jnp.where(finish[None, :] > edges[:, None], finish[None, :], stream_rows), axis=1
    )
    lows = jnp.clip((edge_begin - base) // CHUNK, 0, 6)
    highs = jnp.clip((edge_end - base + CHUNK - 1) // CHUNK, 0, 6)
    scal = jnp.stack(
        [unit, core, side, lows[0], highs[1], lows[2], highs[3], zero]
    ).astype(jnp.int32)
    before = shifted(tokens, "fsdp", 1)
    after = shifted(tokens, "fsdp", -1)
    other_tokens = swap(tokens, "seq", 1)
    if fast:
        halves = widen_matrix.reshape(rows, 2, FF // 2)
        keep = lax.dynamic_index_in_dim(halves, side, 1, False)
        give = lax.dynamic_index_in_dim(halves, 1 - side, 1, False)
        mine = jnp.concatenate([keep, merge_matrix], axis=1)[None]
        got = swap(jnp.concatenate([give, merge_matrix], axis=1)[None], *SIDE)
        wide = in_order(side, mine, got, 0)
        wide = jnp.concatenate(
            [wide[:, :, : FF // 2].reshape(2, rows, 2, D), wide[:, :, FF // 2 :].reshape(2, rows, 2, OWN)],
            axis=3,
        )
        mine = lax.dynamic_index_in_dim(wide, core, 2, False)
        sent = lax.dynamic_index_in_dim(wide, 1 - core, 2, False)
        wide = in_order(core, mine, swap(sent, *CORE), 1)
        shard = jnp.concatenate(
            [
                shrink_matrix,
                wide[:, :, :D].reshape(96, D),
                wide[:, :, D:].transpose(1, 0, 2).reshape(48, D),
            ],
            axis=0,
        )
        wq = own_columns(projection_matrix_triple, nf, side, place)
        pack = jnp.concatenate(
            [
                relaxed_low.reshape(6, 32, 4, 128).transpose(0, 2, 1, 3).reshape(768, 128),
                wq.reshape(48, 9, 128).transpose(1, 0, 2).reshape(432, 128),
                packed,
                jnp.zeros((32, 128), BF),
            ],
            axis=0,
        )
        gathered = lax.all_gather(pack, "fsdp", axis=0, tiled=True)
        other_tokens, before, after, scal, pos, doc = tie(
            other_tokens, before, after, scal, pos, doc
        )
        other_before = swap(before, *SIDE)
        other_after = swap(after, *SIDE)
        other_before, other_after, shard, cot = tie(other_before, other_after, shard, cot)
        wg = lax.all_gather(shard, "fsdp", axis=0, tiled=True).reshape(8, 2, 240, D)
        cot_other = swap(cot, *SIDE)
        cot_other, gathered = tie(cot_other, gathered)
        weights, table = gathered.reshape(16, 26, 48, 128), gathered.reshape(16, 39, 32, 128)
        near_owner = jnp.arange(nf, dtype=jnp.int32)[:, None]
        near = weights[:, 25, 0:16].transpose(1, 0, 2)
    else:
        other_before = swap(before, "seq", 1)
        other_after = swap(after, "seq", 1)
        full = lax.all_gather(projection_matrix_triple, BOTH, axis=0, tiled=True)
        full = lax.dynamic_index_in_dim(full.reshape(D, 3, 2, OWN), side, 2, False)
        full = full.reshape(2, 8, 48, 9, 128).transpose(1, 0, 3, 2, 4).reshape(16, 9, 48, 128)
        table = lax.all_gather(relaxed_low, "fsdp", axis=1, tiled=True)
        table = table.reshape(6, 16, 32, 4, 128).transpose(1, 0, 3, 2, 4).reshape(16, 24, 32, 128)
        weights = jnp.concatenate([table.reshape(16, 16, 48, 128), full], axis=1)
        smalls = lax.all_gather(packed[None], BOTH, axis=0, tiled=True).transpose(1, 0, 2)
        near = lax.dynamic_slice_in_dim(smalls, side * nf, nf, 1)
        near_owner = jnp.arange(nf, dtype=jnp.int32)[:, None]
        owner = jnp.arange(count, dtype=jnp.int32)[:, None]
        cot_other = swap(cot, *SIDE)
        up = lax.all_gather(widen_matrix, BOTH, axis=0, tiled=True)
        up = lax.dynamic_slice_in_dim(up, side * (FF // 2), FF // 2, 1)
        up = up.reshape(2, 8, 48, 2, D).transpose(1, 3, 0, 2, 4).reshape(8, 2, 96, D)
        down = lax.all_gather(shrink_matrix, "fsdp", axis=0, tiled=True).reshape(8, 2, 96, D)
        out = lax.all_gather(merge_matrix, BOTH, axis=0, tiled=True)
        out = out.reshape(2, 8, 48, 2, OWN).transpose(1, 3, 2, 0, 4).reshape(8, 2, 48, D)
        wg = jnp.concatenate([down, up, out], axis=2)

    pos_col, doc_col = pos.reshape(WINDOW, 1), doc.reshape(WINDOW, 1)
    pos_row, doc_row = pos.reshape(6, 1, CHUNK), doc.reshape(6, 1, CHUNK)
    pieces = (tokens, before, after, other_tokens, other_before, other_after)
    q, k, v, xw = project(scal, pieces, weights, near, near_owner, spread, group)
    if fast:
        far = swap(near, "seq", 1)
        smalls = jnp.concatenate([near, far], axis=1)
        owner = jnp.concatenate([side * nf + near_owner, (1 - side) * nf + near_owner], axis=0)
        q, smalls = tie(q, smalls)
    ctx, lse, *hots = attend(scal, pos_col, pos_row, doc_col, doc_row, q, k, v, table)
    ctx_other = swap(ctx, *SIDE)
    unit1, rstd1, nlow, base_up, send_up, act, slope = feed_up(
        scal, xw, ctx, ctx_other, smalls, owner, near, near_owner,
        (spread, group, spread_up, group_up), wg,
    )
    lay, ddown, dup, base_down, send_down, sums = feed_back(
        scal, base_up, swap(send_up, *SIDE), cot, cot_other, slope, smalls, owner, spread, group, wg
    )
    got_down = swap(send_down, *SIDE)
    feed = weight_grads(scal, act, ddown, nlow, dup)
    got_down, feed = tie(got_down, feed)
    if fast:
        feed_got = swap(by_core(feed[1]), *CORE)
    closed = feed_close(
        scal, base_down, got_down, unit1, rstd1, sums, smalls, owner, spread, group, wg
    )
    if fast:
        closed, feed_got = tie(closed, feed_got)
        feed = sum_core(feed[0], feed_got)
    dh1, dattn, dctx, sums = closed

    def back(first, pairs, dctx):
        dq, own, low, high, keep, send = attend_back(
            first, pairs, scal, doc_col, doc_row, q, k, v, table, hots, xw, sums, ctx, dctx,
            dattn, lse,
        )
        return dq, own, low, high, (keep, send)

    own_cols = lambda values, at, size: lax.dynamic_slice_in_dim(values, at * size, size, 1)
    if fast:
        both_ways = lambda high, low: (shifted(high, "fsdp", 1), shifted(low, "fsdp", -1))
        feed_got = swap(feed[1], *ALONG_Y)
        outs0, feed_got = tie(back(0, 2, dctx), feed_got)
        dq0, own0, low0, high0, part0 = outs0
        feed = sum_y(feed[0], feed_got)
        part0_got = swap(by_core(part0[1]), *CORE)
        part0_got, feed = tie(part0_got, feed)
        part0 = sum_core(part0[0], part0_got)
        part0, dctx = tie(part0, dctx)
        part0_got = swap(part0[1], *ALONG_Y)
        feed_got = along_z(feed)
        ways0 = both_ways(high0, low0)
        outs1, part0_got, feed_got, ways0 = tie(back(2, 1, dctx), part0_got, feed_got, ways0)
        dq1, own1, low1, high1, part1 = outs1
        part0, shard = sum_y(part0[0], part0_got), sum_z(feed[0], feed_got)
        part1_got = swap(by_core(part1[1]), *CORE)
        ways1 = both_ways(high1, low1)
        part0_got = along_z(part0)
        part1_got, ways1 = tie(part1_got, ways1)
        part1 = sum_core(part1[0], part1_got)
        part1_got = swap(part1[1], *ALONG_Y)
        backed = project_back(scal, ((dq0, own0, *ways0), (dq1, own1, *ways1)), dh1, weights)
        (dx, dx_send), part1_got, part0_got = tie(backed, part1_got, part0_got)
        part1, part0 = sum_y(part1[0], part1_got), sum_z(part0[0], part0_got)
        part1 = sum_z(part1[0], along_z(part1))
        dx_got = swap(dx_send, *SIDE)
        blocks = [part0[:PART_MORE], part0[PART_MORE:], part1]
        masks = [
            block[PART_TABLE:PART_SUMS].reshape(2, 4, 32, 128).transpose(0, 2, 1, 3)
            for block in blocks
        ]
        masks = [mask.reshape(2, 32, MPOS) for mask in masks]
        pair_sums = [block[PART_SUMS : PART_SUMS + 2] for block in blocks]
        weight = jnp.stack([block[:PART_TABLE].reshape(3, 2, rows, 128) for block in blocks], axis=1)
        mine = lax.dynamic_index_in_dim(weight, side, 2, False)
        sent = lax.dynamic_index_in_dim(weight, 1 - side, 2, False)
        token_sums = jnp.stack([block[PART:PART_OUT] for block in blocks[:2]]).reshape(6, 16, 128)
        sums = token_sums.transpose(1, 0, 2).reshape(16, D).astype(F32)
        outs = jnp.stack([block[PART_OUT : PART_OUT + 3 * rows] for block in blocks[:2]])
        grad_w_out = outs.reshape(6, rows, 128).transpose(1, 0, 2).reshape(rows, D).astype(F32)
        got = swap(sent.reshape(-1, 128), *SIDE)
        got = got.reshape(3, 3, rows, 128)
        table_total = jnp.concatenate(masks, axis=0).astype(F32)
        mine = mine.transpose(2, 0, 1, 3).reshape(rows, 3, 1, OWN)
        got = got.transpose(2, 0, 1, 3).reshape(rows, 3, 1, OWN)
        grad_w_qkv = in_order(side, mine, got, 2).reshape(rows, 3 * D).astype(F32)
        head_sums = jnp.concatenate(pair_sums, axis=1).astype(F32)
        head_grads = own_cols(head_sums, place, wide_cols)
        grad_w_down = shard[:96].astype(F32)
        wide = shard[96:192].reshape(2, 2, rows, D).transpose(0, 2, 1, 3).reshape(2, rows, FF // 2)
        mine = lax.dynamic_index_in_dim(wide, side, 0, False)
        got = swap(lax.dynamic_index_in_dim(wide, 1 - side, 0, False), *SIDE)
        grad_w_up = in_order(side, mine, got, 1).astype(F32)
    else:
        scatter = partial(lax.psum_scatter, axis_name=BOTH, scatter_dimension=0, tiled=True)
        outs = [back(0, 2, dctx), back(2, 1, dctx)]
        dx, dx_send = project_back(
            scal,
            [
                (dq, own, shifted(high, "fsdp", 1), shifted(low, "fsdp", -1))
                for dq, own, low, high, _ in outs
            ],
            dh1,
            weights,
        )
        dx_got = swap(dx_send, "seq", 1)

        def plain(pair):
            both = jnp.stack(pair, axis=1)
            return jnp.stack([both[4 * (u & 1) + (u >> 1)] for u in range(8)], axis=0)

        first, second = plain(outs[0][4]), plain(outs[1][4])
        parts = [first[:, :, :PART_MORE], first[:, :, PART_MORE:], second]
        table_grad = jnp.stack([p[:, :, PART_TABLE:PART_SUMS] for p in parts])
        table_grad = table_grad.reshape(3, 8, 2, 2, 4, 32, 128).transpose(0, 3, 1, 2, 5, 4, 6)
        table_total = lax.psum_scatter(
            table_grad.reshape(6, MPOS, MPOS), "fsdp", scatter_dimension=1, tiled=True
        ).astype(F32)
        head_rows = jnp.stack([p[:, :, :PART_TABLE] for p in parts])
        head_rows = head_rows.reshape(3, 8, 2, 3, 2, 24, 128).transpose(4, 1, 2, 5, 3, 0, 6)
        head_rows = head_rows.reshape(D, 3, 1, OWN)
        blank = jnp.zeros_like(head_rows)
        both = jnp.concatenate(
            [jnp.where(side == 0, head_rows, blank), jnp.where(side == 0, blank, head_rows)], axis=2
        )
        grad_w_qkv = scatter(both.reshape(D, 3 * D)).astype(F32)
        pair_sums = [p[0, 0, PART_SUMS : PART_SUMS + 2].astype(F32) for p in parts]
        head_sums = lax.psum(jnp.concatenate(pair_sums, axis=1), "fsdp")
        head_grads = own_cols(head_sums, place, wide_cols)
        def placed(value, axis):
            blank = jnp.zeros_like(value)
            sides = [jnp.where(side == 0, value, blank), jnp.where(side == 0, blank, value)]
            return jnp.concatenate(sides, axis=axis)

        gg = plain(feed).reshape(16, 192, D)
        grad_w_down = scatter(placed(gg[:, :96].reshape(FF // 2, D), 0)).astype(F32)
        up = gg[:, 96:192].reshape(16, 2, 2, 24, D).transpose(1, 0, 3, 2, 4).reshape(D, FF // 2)
        grad_w_up = scatter(placed(up, 1)).astype(F32)
        out = jnp.stack([p[:, :, PART_OUT : PART_OUT + 72] for p in parts[:2]])
        out = out.reshape(2, 8, 2, 3, 24, 128).transpose(1, 2, 4, 0, 3, 5).reshape(OWN, D)
        grad_w_out = scatter(placed(out, 0)).astype(F32)
        sums = lax.psum(sums, "fsdp")
    ours = own_cols(sums[:6], side * nf + place, wide_cols)
    grad_biases = jnp.concatenate([head_grads, ours[:4]], axis=0)
    grad_gains = ours[4:]
    grad_bias_up = lax.dynamic_slice_in_dim(
        sums[8:10].reshape(-1), place * up_cols, up_cols, 0
    )
    input_grad = dx + dx_got.astype(F32)
    mask_logit_gradient = (
        table_total * relaxed * (1.0 - relaxed) / softening_scale[:, None, None]
    )
    return (
        lay.reshape(1, HALF, D),
        input_grad.reshape(1, HALF, D),
        grad_w_qkv,
        grad_w_out,
        grad_w_up,
        grad_w_down,
        grad_biases,
        grad_gains,
        grad_bias_up,
        mask_logit_gradient,
    )


def solution(mesh):
    rows = P(("seq", "fsdp"), None)
    columns = P(None, ("seq", "fsdp"))
    block = P("fsdp", "seq", None)
    table = P("seq", "fsdp", None)
    return jax.shard_map(
        per_device,
        mesh=mesh,
        in_specs=(
            block, rows, rows, rows, rows, columns, columns, P(("seq", "fsdp")),
            table, table, P("seq"), P(), block,
        ),
        out_specs=(
            block, block, rows, rows, rows, rows, columns, columns, P(("seq", "fsdp")), table,
        ),
        check_vma=False,
    )
```

```python
from functools import partial

import jax
import jax.numpy as jnp
from jax import lax
from jax.experimental import pallas as pl
from jax.experimental.pallas import tpu as pltpu
from jax.sharding import PartitionSpec as P

D = 768
FF = 3072
HEADS = 12
HDIM = 64
MPOS = 512
EPS = 1e-05
GROUP = 512
HALF = 256
WINDOW = 3 * GROUP
OWN = 384
CHUNK = 256
NEG = -1e30
BF = jnp.bfloat16
F32 = jnp.float32
HIGH = lax.Precision.HIGHEST
PART_TOTALS = 144
PART_SUMS = 160
PART_OUT = 192
PART = 240
PART_TABLE = 256


def nn(left, right):
    return jnp.dot(left, right, preferred_element_type=F32)


def nt(left, right, precision=None):
    return lax.dot_general(
        left, right, (((1,), (1,)), ((), ())), precision=precision, preferred_element_type=F32
    )


def tn(left, right):
    return lax.dot_general(left, right, (((0,), (0,)), ((), ())), preferred_element_type=F32)


def load_projection(gathered, w, sem):
    copies = []
    for f in range(16):
        row = (f % 2) * OWN + (f // 2) * 48
        copies.append(
            pltpu.make_async_copy(gathered.at[f, 16:25], w.at[:, row : row + 48, :], sem.at[f])
        )
    for copy in copies:
        copy.start()
    return copies


def table_of(table, head):
    return jnp.concatenate(
        [table[:, 4 * head + part].reshape(MPOS, 128) for part in range(4)], axis=1
    )


def spread_out(values, spread, owner, group):
    return jnp.sum(jnp.where(owner == group, nn(values, spread), 0.0), axis=0, keepdims=True)


def columns_of(w, first, count=3):
    return jnp.concatenate([w[first + part] for part in range(count)], axis=1)


def place_of(t, cr, scal):
    unit = ((t >> 2) ^ (scal[0] & 1)) | ((t & 3) << 1)
    return 2 * unit + (scal[1] ^ cr)


def near_place_of(t, cr, scal):
    unit = ((t >> 2) | (t & 2) | ((t & 1) << 2)) ^ scal[0]
    return 2 * unit + (scal[1] ^ cr)


def project_kernel(
    scal,
    x1,
    x0,
    x2,
    y1,
    y0,
    y2,
    gathered,
    near,
    owner,
    spread,
    group,
    q_ref,
    k_ref,
    v_ref,
    xw,
    w,
    sem,
):
    copies = load_projection(gathered, w, sem)
    side = scal[2]
    for g, (mine, other) in enumerate(((x0, y0), (x1, y1), (x2, y2))):
        xw[pl.ds(pl.multiple_of(g * GROUP + side * HALF, HALF), HALF), :] = mine[...]
        xw[pl.ds(pl.multiple_of(g * GROUP + (1 - side) * HALF, HALF), HALF), :] = other[...]
    bias = [
        spread_out(near[i], spread[:, :OWN], owner[...], group[:, :OWN]) for i in range(2)
    ]
    for copy in copies:
        copy.wait()
    for blk in range(6):
        rows = slice(blk * HALF, (blk + 1) * HALF)
        here = xw[rows, :]
        k_ref[rows, :] = nn(here, columns_of(w, 3)).astype(BF)
        v_ref[rows, :] = (nn(here, columns_of(w, 6)) + bias[1]).astype(BF)
        if blk in (2, 3):
            local = slice((blk - 2) * HALF, (blk - 1) * HALF)
            query = (nn(here, columns_of(w, 0)) + bias[0]).astype(BF)
            q_ref[local, :] = query * jnp.asarray(0.125, BF)


def head_lanes():
    return lax.broadcasted_iota(jnp.int32, (1, 128), 1) < HDIM


def fill_hot(pos_col, hot):
    for blk in range(6):
        rows = slice(blk * 256, (blk + 1) * 256)
        column = lax.broadcasted_iota(jnp.int32, (256, MPOS), 1)
        hot[rows, :] = jnp.where(pos_col[rows, :] == column, 1.0, 0.0).astype(BF)


def fill_hot_turned(pos_row, hot):
    for blk in range(6):
        rows = lax.broadcasted_iota(jnp.int32, (MPOS, 256), 0)
        hot[blk] = jnp.where(pos_row[blk] == rows, 1.0, 0.0).astype(BF)


def set_pair(low, value, target):
    blank = jnp.zeros_like(value)
    target[:HALF, :] = jnp.where(low, value, blank)
    target[HALF:, :] = jnp.where(low, blank, value)


def fold(values, how):
    rows, columns = values.shape
    return how(values.reshape(rows // 8, 8, columns), axis=0)


def attend_kernel(
    scal,
    pos_col,
    pos_row,
    doc_col,
    doc_row,
    q,
    k,
    v,
    table,
    ctx,
    inverses,
    weights,
    mixes,
    hot_turned,
    hot,
    sbuf,
    looks,
    queries,
    acc,
):
    @pl.when(pl.program_id(0) == 0)
    def _():
        fill_hot(pos_col, hot)
        fill_hot_turned(pos_row, hot_turned)

    low = head_lanes()
    for qb in range(2):
        lo, hi = scal[3 + 2 * qb], scal[4 + 2 * qb]
        here = slice(qb * HALF, (qb + 1) * HALF)
        set_pair(low, q[here, :], queries)
        q_doc = jnp.concatenate([doc_row[2 + qb]] * 2, axis=1)
        q_hot = hot[GROUP + qb * HALF : GROUP + (qb + 1) * HALF, :]
        for h in range(2):
            looks[h * HALF : (h + 1) * HALF, :] = nn(q_hot, table_of(table, h)).astype(BF)

        def score_step(c, top, q_doc=q_doc):
            rows = pl.ds(pl.multiple_of(c * CHUNK, CHUNK), CHUNK)
            s = jnp.where(doc_col[rows, :] == q_doc, nt(k[rows, :], queries[...]), NEG)
            sbuf[c] = s
            return jnp.maximum(top, fold(s, jnp.max))

        top = lax.fori_loop(lo, hi, score_step, jnp.full((8, 2 * HALF), NEG, F32))
        top = jnp.max(top, axis=0, keepdims=True)
        acc[...] = jnp.zeros_like(acc)

        def mix_step(c, total, top=top, qb=qb):
            rows = pl.ds(pl.multiple_of(c * CHUNK, CHUNK), CHUNK)
            e = jnp.exp(sbuf[c] - top)
            mixed = (e * nt(hot[rows, :], looks[...])).astype(BF)
            weights[0, qb, c] = e.astype(BF)
            mixes[0, qb, c] = mixed
            acc[...] += tn(mixed, v[rows, :])
            return total + fold(e, jnp.sum)

        total = lax.fori_loop(lo, hi, mix_step, jnp.zeros((8, 2 * HALF), F32))
        total = jnp.sum(total, axis=0, keepdims=True)
        inverse = 1.0 / total
        inverses[0, 0:1, here] = inverse[:, :HALF]
        inverses[0, 1:2, here] = inverse[:, HALF:]
        inverses[0, 2:8, here] = jnp.zeros((6, HALF), F32)
        scale = jnp.concatenate(
            [
                jnp.broadcast_to(inverse[:, :HALF], (HDIM, HALF)),
                jnp.broadcast_to(inverse[:, HALF:], (HDIM, HALF)),
            ],
            axis=0,
        ).T
        ctx[qb] = (jnp.where(low, acc[:HALF, :], acc[HALF:, :]) * scale).astype(BF)


def attend_back_kernel(
    carried,
    scal,
    q,
    k,
    v,
    weights,
    mixes,
    hot_turned,
    xw,
    sums,
    ctx,
    ctx_all,
    dctx0,
    dctx1,
    dattn0,
    dattn1,
    inverses,
    *refs,
):
    outs = refs[carried : carried + 8]
    dq, own, halo_low, halo_high, part_keep, part_send, table_keep, table_send = outs
    queries, grads, dk, dv, dq_acc, tt, tg, gw, gout = refs[carried + 8 :]
    low = head_lanes()
    dk[...] = jnp.zeros_like(dk)
    dv[...] = jnp.zeros_like(dv)
    lane = lax.broadcasted_iota(jnp.int32, (8, 128), 1)
    row8 = lax.broadcasted_iota(jnp.int32, (8, 128), 0)
    pick = jnp.where((lane < HDIM) == (row8 == 0), 1.0, 0.0)
    for qb in range(2):
        lo, hi = scal[3 + 2 * qb], scal[4 + 2 * qb]
        here = slice(qb * HALF, (qb + 1) * HALF)
        inverse = inverses[0, 0:2, here]
        d_pair = (dctx0, dctx1)[qb][...].astype(F32)
        deltas = nt(pick, d_pair * ctx[qb].astype(F32), HIGH)[0:2, :] * inverse
        delta = jnp.concatenate([deltas[0:1, :], deltas[1:2, :]], axis=1)
        scale = jnp.concatenate(
            [
                jnp.broadcast_to(inverse[0:1, :], (HDIM, HALF)),
                jnp.broadcast_to(inverse[1:2, :], (HDIM, HALF)),
            ],
            axis=0,
        ).T
        set_pair(low, q[here, :], queries)
        set_pair(low, (d_pair * scale).astype(BF), grads)
        dq_acc[...] = jnp.zeros_like(dq_acc)
        tt[...] = jnp.zeros_like(tt)

        def step(c, carry, delta=delta, qb=qb):
            rows = pl.ds(pl.multiple_of(c * CHUNK, CHUNK), CHUNK)
            mixed = mixes[0, qb, c]
            e = weights[0, qb, c].astype(F32)
            dm = nt(v[rows, :], grads[...])
            ds = (mixed.astype(F32) * dm - e * delta).astype(BF)
            dv[rows, :] += nn(mixed, grads[...])
            dk[rows, :] += nn(ds, queries[...])
            dq_acc[...] += tn(ds, k[rows, :])
            tt[...] += nn(hot_turned[c], (e * dm).astype(BF))
            return carry

        lax.fori_loop(lo, hi, step, 0)
        for h in range(2):
            piece = nt(hot_turned[2 + qb], tt[:, h * HALF : (h + 1) * HALF].astype(BF))
            if qb == 0:
                tg[h] = piece
            else:
                tg[h] += piece
        dq[here, :] = (jnp.where(low, dq_acc[:HALF, :], dq_acc[HALF:, :]) * 0.125).astype(BF)
    own[0] = dk[GROUP : 2 * GROUP, :]
    own[1] = dv[GROUP : 2 * GROUP, :]
    halo_low[0] = dk[:GROUP, :].astype(BF)
    halo_low[1] = dv[:GROUP, :].astype(BF)
    halo_high[0] = dk[2 * GROUP :, :].astype(BF)
    halo_high[1] = dv[2 * GROUP :, :].astype(BF)
    query_grad = dq[...]
    pair_grad = jnp.concatenate([dk[...].astype(BF), dv[...].astype(BF)], axis=1)
    gw[:, 0:128] = tn(xw[GROUP : 2 * GROUP, :], query_grad)
    gw[:, 128:384] = tn(xw[...], pair_grad)
    gout[...] = tn(ctx_all[0], dattn0[...]) + tn(ctx_all[1], dattn1[...])
    totals = jnp.concatenate(
        [
            column_sum(query_grad.astype(F32)),
            column_sum(pair_grad[:, 128:].astype(F32)),
            jnp.zeros((14, 128), F32),
            sums[:, 0:128],
            sums[:, 128:256],
        ],
        axis=0,
    ).astype(BF)
    for cr in range(2):
        out, table = (part_keep, table_keep) if cr == 0 else (part_send, table_send)
        for t in range(8):
            place = place_of(t, cr, scal)
            rows = [
                gw[pl.ds(pl.multiple_of(part * OWN + place * 24, 8), 24), :] for part in range(2)
            ]
            both = jnp.concatenate(rows, axis=0).astype(BF)
            for i in range(3):
                out[t, i * 48 : i * 48 + 48, :] = both[:, i * 128 : (i + 1) * 128]
            out[t, PART_TOTALS:PART_OUT, :] = totals
            rows = gout[pl.ds(pl.multiple_of(place * 24, 8), 24), :]
            out[t, PART_OUT:PART, :] = jnp.concatenate(
                [rows[:, 0:128], rows[:, 128:256]], axis=0
            ).astype(BF)
            for h in range(2):
                mask = tg[h, pl.ds(pl.multiple_of(place * 32, 32), 32), :].astype(BF)
                for i in range(4):
                    at = (4 * h + i) * 32
                    table[t, at : at + 32, :] = mask[:, i * 128 : (i + 1) * 128]


def norm_stats(values):
    center = values - jnp.mean(values, axis=-1, keepdims=True)
    rstd = lax.rsqrt(jnp.mean(center * center, axis=-1, keepdims=True) + EPS)
    return center * rstd, rstd


def norm_back(grad, unit, rstd, gain):
    scaled = grad * gain
    return rstd * (
        scaled
        - jnp.mean(scaled, axis=-1, keepdims=True)
        - unit * jnp.mean(scaled * unit, axis=-1, keepdims=True)
    )


def column_sum(values):
    return jnp.sum(values, axis=0, keepdims=True)


def load_feed(wg, sem, wm=None, wu=None, wd=None):
    copies = []

    def bring(source, target):
        copies.append(pltpu.make_async_copy(source, target, sem.at[len(copies)]))
        copies[-1].start()

    for c in range(2):
        for s in range(2):
            if wm is not None:
                bring(
                    wg.at[:, c, 192:240, s * OWN : (s + 1) * OWN],
                    wm.at[s, :, :, c * OWN : (c + 1) * OWN],
                )
    for c in range(2):
        for s in range(2):
            if wu is not None:
                bring(wg.at[:, c, 96 + 48 * s : 144 + 48 * s, :], wu.at[c, s])
    for c in range(2):
        if wd is not None:
            bring(wg.at[:, c, 0:96, :], wd.at[:, c])
    return copies


def shrink_rows(wd, i):
    return wd[pl.ds(4 * i, 4)].reshape(D, D)


def wait_for(copies):
    for copy in copies:
        copy.wait()


def feed_up_kernel(
    scal,
    x,
    ctx_mine,
    ctx_other,
    smalls,
    owner,
    near,
    near_owner,
    spread,
    group,
    spread_up,
    group_up,
    wg,
    unit1,
    rstd1,
    nlow,
    base,
    send,
    act,
    slope,
    wm,
    wu,
    wd,
    ctxt,
    bup,
    sem,
):
    copies = load_feed(wg, sem, wm, wu, wd)
    vector = lambda i: spread_out(smalls[i], spread[...], owner[...], group[...])
    bias_out, bias_down, shift1, gain1 = [vector(i) for i in (2, 3, 4, 6)]
    for n in range(2):
        bup[n] = spread_out(
            near[8], spread_up[...], near_owner[...], group_up[...] + n * (near.shape[1] // 2)
        )
    even = scal[2] == 0
    mine, other = ctx_mine[0], ctx_other[0]
    ctxt[:, :OWN] = jnp.where(even, mine, other)
    ctxt[:, OWN:] = jnp.where(even, other, mine)
    wait_for(copies[:4])
    attn = nn(ctxt[...], wm[...].reshape(D, D)) + bias_out
    unit, rstd = norm_stats(x[...].astype(F32) + attn)
    unit1[...] = unit
    rstd1[...] = jnp.broadcast_to(rstd, (HALF, 128))
    normed = unit * gain1 + shift1
    nlow[...] = normed.astype(BF)
    base[...] = normed + bias_down
    wait_for(copies[4:8])

    def widen(n, carry):
        up = nn(nlow[...], wu[n].reshape(D, D)) + bup[n]
        half_cdf = 0.5 * (1.0 + lax.erf(up * 0.7071067811865476))
        act[n] = (up * half_cdf).astype(BF)
        slope[n] = half_cdf + up * (0.3989422804014327 * jnp.exp(-0.5 * up * up))
        return carry

    lax.fori_loop(0, 2, widen, 0)
    wait_for(copies[8:])
    part = nn(act[0], shrink_rows(wd, 0)) + nn(act[1], shrink_rows(wd, 1))
    base[...] += part
    send[...] = part.astype(BF)


def feed_back_kernel(
    index,
    scal,
    base,
    got,
    cot_mine,
    cot_other,
    slope,
    smalls,
    owner,
    spread,
    group,
    wg,
    lay,
    ddown,
    dup,
    base2,
    send,
    sums,
    wu,
    wd,
    sem,
):
    copies = load_feed(wg, sem, None, wu, wd)
    vector = lambda i: spread_out(smalls[i], spread[...], owner[...], group[...])
    shift2, gain2 = vector(5), vector(7)
    sums[...] = jnp.zeros_like(sums)
    unit, rstd = norm_stats(base[...] + got[...].astype(F32))
    lay[...] = (unit * gain2 + shift2).astype(BF)
    dy = jnp.where(scal[2] == index, cot_mine[...], cot_other[...]).astype(F32)
    sums[3:4, :] = column_sum(dy)
    sums[5:6, :] = column_sum(dy * unit)
    grad = norm_back(dy, unit, rstd, gain2)
    ddown[...] = grad.astype(BF)
    sums[1:2, :] = column_sum(ddown[...].astype(F32))
    base2[...] = grad
    wait_for(copies)

    def back(n, carry):
        low = (nt(ddown[...], shrink_rows(wd, n)) * slope[n]).astype(BF)
        dup[n] = low
        sums[pl.ds(8 + n, 1), :] = column_sum(low.astype(F32))
        return carry

    lax.fori_loop(0, 2, back, 0)
    part = nt(dup[0], wu[0].reshape(D, D)) + nt(dup[1], wu[1].reshape(D, D))
    base2[...] += part
    send[...] = part.astype(BF)


def feed_close_kernel(
    scal,
    base,
    got,
    unit1,
    rstd1,
    sums_in,
    smalls,
    owner,
    spread,
    group,
    wg,
    dh1,
    dattn,
    dctx,
    sums,
    wm,
    sem,
):
    copies = load_feed(wg, sem, wm)
    gain1 = spread_out(smalls[6], spread[...], owner[...], group[...])
    sums[...] = sums_in[...]
    grad = base[...] + got[...].astype(F32)
    unit = unit1[...]
    sums[2:3, :] += column_sum(grad)
    sums[4:5, :] += column_sum(grad * unit)
    grad = norm_back(grad, unit, rstd1[:, 0:1], gain1)
    dh1[...] = grad
    dattn[...] = grad.astype(BF)
    sums[0:1, :] += column_sum(dattn[...].astype(F32))
    wait_for(copies)
    dctx[...] = nt(dattn[...], wm[scal[2]].reshape(OWN, D)).astype(BF)


def weight_grad_kernel(
    scal, act0, ddown0, nlow0, dup0, act1, ddown1, nlow1, dup1, keep, send, down, up
):
    for n in range(2):
        up[n] = tn(nlow0[...], dup0[n]) + tn(nlow1[...], dup1[n])
        down[n * D : (n + 1) * D, :] = tn(act0[n], ddown0[...]) + tn(act1[n], ddown1[...])
    for cr, out in enumerate((keep, send)):
        for t in range(8):
            place = near_place_of(t, cr, scal)
            out[t, 0:96, :] = down[pl.ds(pl.multiple_of(place * 96, 8), 96), :].astype(BF)
            parts = [
                up[n, pl.ds(pl.multiple_of(s * OWN + place * 24, 8), 24), :]
                for s in range(2)
                for n in range(2)
            ]
            out[t, 96:192, :] = jnp.concatenate(parts, axis=0).astype(BF)


def project_back_kernel(scal, parts, dh1s, gathered, dx, dx_send, w, dqkv, sem):
    copies = load_projection(gathered, w, sem)
    dq, own, left, right = parts
    dqkv[:, :OWN] = dq[...]
    for i in range(2):
        total = own[i] + left[i].astype(F32) + right[i].astype(F32)
        dqkv[:, (1 + i) * OWN : (2 + i) * OWN] = total.astype(BF)
    for copy in copies:
        copy.wait()
    side = scal[2]
    mine = dqkv[pl.ds(pl.multiple_of(side * HALF, HALF), HALF), :]
    other = dqkv[pl.ds(pl.multiple_of((1 - side) * HALF, HALF), HALF), :]
    for part in range(3):
        cols = slice(part * 256, (part + 1) * 256)
        rows = jnp.concatenate([w[j, cols, :] for j in range(9)], axis=1)
        dh1 = jnp.where(side == 0, dh1s[0][:, cols], dh1s[1][:, cols])
        dx[:, cols] = dh1 + nt(mine, rows)
        dx_send[:, cols] = nt(other, rows).astype(BF)


SMEM = pl.BlockSpec(memory_space=pltpu.SMEM)
VM = pl.BlockSpec()
HBM = pl.BlockSpec(memory_space=pl.ANY)


def params():
    return pltpu.CompilerParams(vmem_limit_bytes=60 * 1024 * 1024)


def cost(microseconds):
    return pl.CostEstimate(
        flops=int(microseconds * 1.15e9), bytes_accessed=1000, transcendentals=0
    )


def shape(dims, kind):
    return jax.ShapeDtypeStruct(dims, kind)


def project(scal, pieces, gathered, near, owner, spread, group):
    return pl.pallas_call(
        project_kernel,
        name="project",
        out_shape=(
            shape((GROUP, OWN), BF),
            shape((WINDOW, OWN), BF),
            shape((WINDOW, OWN), BF),
            shape((WINDOW, D), BF),
        ),
        in_specs=[SMEM] + [VM] * 6 + [HBM] + [VM] * 4,
        out_specs=[VM] * 4,
        scratch_shapes=[
            pltpu.VMEM((9, D, 128), BF),
            pltpu.SemaphoreType.DMA((16,)),
        ],
        compiler_params=params(),
        cost_estimate=cost(9),
    )(scal, *pieces, gathered, near, owner, spread, group)


def whole(*dims):
    return pl.BlockSpec(dims, lambda p: (0,) * len(dims))


def attend(scal, pos_col, pos_row, doc_col, doc_row, q, k, v, table):
    return pl.pallas_call(
        attend_kernel,
        name="attend",
        grid=(3,),
        out_shape=(
            shape((2, HALF, OWN), BF),
            shape((3, 8, GROUP), F32),
            shape((3, 2, 6, CHUNK, 2 * HALF), BF),
            shape((3, 2, 6, CHUNK, 2 * HALF), BF),
            shape((6, MPOS, CHUNK), BF),
        ),
        in_specs=[
            SMEM,
            whole(WINDOW, 1),
            whole(6, 1, CHUNK),
            whole(WINDOW, 1),
            whole(6, 1, CHUNK),
            pl.BlockSpec((GROUP, 128), lambda p: (0, p)),
            pl.BlockSpec((WINDOW, 128), lambda p: (0, p)),
            pl.BlockSpec((WINDOW, 128), lambda p: (0, p)),
            pl.BlockSpec((16, 8, 32, 128), lambda p: (0, p, 0, 0)),
        ],
        out_specs=[
            pl.BlockSpec((2, HALF, 128), lambda p: (0, 0, p)),
            pl.BlockSpec((1, 8, GROUP), lambda p: (p, 0, 0)),
            pl.BlockSpec((1, 2, 6, CHUNK, 2 * HALF), lambda p: (p, 0, 0, 0, 0)),
            pl.BlockSpec((1, 2, 6, CHUNK, 2 * HALF), lambda p: (p, 0, 0, 0, 0)),
            whole(6, MPOS, CHUNK),
        ],
        scratch_shapes=[
            pltpu.VMEM((WINDOW, MPOS), BF),
            pltpu.VMEM((6, CHUNK, 2 * HALF), F32),
            pltpu.VMEM((2 * HALF, MPOS), BF),
            pltpu.VMEM((2 * HALF, 128), BF),
            pltpu.VMEM((2 * HALF, 128), F32),
        ],
        compiler_params=params(),
        cost_estimate=cost(26),
    )(scal, pos_col, pos_row, doc_col, doc_row, q, k, v, table)


def attend_back(
    first, pairs, before, scal, q, k, v, kept, xw, sums, ctx, dctx, dattn, inverses
):
    columns = lambda rows: pl.BlockSpec((rows, 128), lambda p: (0, first + p))
    tiles = pl.BlockSpec((1, 2, 6, CHUNK, 2 * HALF), lambda p: (first + p, 0, 0, 0, 0))
    blocks = lambda rows: pl.BlockSpec((8, rows, 128), lambda p: (0, first + p, 0))
    both = pl.BlockSpec((2, GROUP, 128), lambda p: (0, 0, first + p))
    return pl.pallas_call(
        partial(attend_back_kernel, len(before)),
        name=f"attend_back_{first}",
        grid=(pairs,),
        input_output_aliases={16 + i: i for i in range(len(before))},
        out_shape=(
            shape((GROUP, OWN), BF),
            shape((2, GROUP, OWN), F32),
            shape((2, GROUP, OWN), BF),
            shape((2, GROUP, OWN), BF),
            shape((8, 3 * PART, 128), BF),
            shape((8, 3 * PART, 128), BF),
            shape((8, 3 * PART_TABLE, 128), BF),
            shape((8, 3 * PART_TABLE, 128), BF),
        ),
        in_specs=[
            SMEM,
            columns(GROUP),
            columns(WINDOW),
            columns(WINDOW),
            tiles,
            tiles,
            whole(6, MPOS, CHUNK),
            whole(WINDOW, D),
            pl.BlockSpec((16, 256), lambda p: (0, first + p)),
            pl.BlockSpec((2, HALF, 128), lambda p: (0, 0, first + p)),
            whole(2, HALF, OWN),
            columns(HALF),
            columns(HALF),
            pl.BlockSpec((HALF, 256), lambda p: (0, first + p)),
            pl.BlockSpec((HALF, 256), lambda p: (0, first + p)),
            pl.BlockSpec((1, 8, GROUP), lambda p: (first + p, 0, 0)),
        ]
        + [HBM] * len(before),
        out_specs=[
            columns(GROUP),
            both,
            both,
            both,
            blocks(PART),
            blocks(PART),
            blocks(PART_TABLE),
            blocks(PART_TABLE),
        ],
        scratch_shapes=[
            pltpu.VMEM((2 * HALF, 128), BF),
            pltpu.VMEM((2 * HALF, 128), BF),
            pltpu.VMEM((WINDOW, 128), F32),
            pltpu.VMEM((WINDOW, 128), F32),
            pltpu.VMEM((2 * HALF, 128), F32),
            pltpu.VMEM((MPOS, 2 * HALF), F32),
            pltpu.VMEM((2, MPOS, MPOS), F32),
            pltpu.VMEM((D, OWN), F32),
            pltpu.VMEM((OWN, 256), F32),
        ],
        compiler_params=params(),
        cost_estimate=cost(10 * pairs),
    )(scal, q, k, v, *kept, xw, sums, ctx, ctx, *dctx, *dattn, inverses, *before)


WIDEN = pltpu.VMEM((2, 2, 8, 48, D), BF)
SHRINK = pltpu.VMEM((8, 2, 96, D), BF)
MERGE = pltpu.VMEM((2, 8, 48, D), BF)


def feed_up(index, scal, xw, mine, other, smalls, owner, near, near_owner, spreads, wg):
    arrays = (smalls, owner, near, near_owner, *spreads)
    ctx = pl.BlockSpec((1, HALF, OWN), lambda p: (index, 0, 0))
    outs = (
        shape((HALF, D), F32),
        shape((HALF, 128), F32),
        shape((HALF, D), BF),
        shape((HALF, D), F32),
        shape((HALF, D), BF),
        shape((2, HALF, D), BF),
        shape((2, HALF, D), F32),
    )
    return pl.pallas_call(
        feed_up_kernel,
        name=f"feed_up_{index}",
        grid=(1,),
        out_shape=outs,
        in_specs=[SMEM, pl.BlockSpec((HALF, D), lambda p: (2 + index, 0)), ctx, ctx]
        + [whole(*a.shape) for a in arrays]
        + [HBM],
        out_specs=[whole(*out.shape) for out in outs],
        scratch_shapes=[
            MERGE,
            WIDEN,
            SHRINK,
            pltpu.VMEM((HALF, D), BF),
            pltpu.VMEM((2, 1, D), F32),
            pltpu.SemaphoreType.DMA((10,)),
        ],
        compiler_params=params(),
        cost_estimate=cost(8),
    )(scal, xw, mine, other, *arrays, wg)


def feed_back(index, scal, base, got, cot, cot_other, slope, smalls, owner, spread, group, wg):
    return pl.pallas_call(
        partial(feed_back_kernel, index),
        name=f"feed_back_{index}",
        out_shape=(
            shape((HALF, D), BF),
            shape((HALF, D), BF),
            shape((2, HALF, D), BF),
            shape((HALF, D), F32),
            shape((HALF, D), BF),
            shape((16, D), F32),
        ),
        in_specs=[SMEM] + [VM] * 9 + [HBM],
        out_specs=[VM] * 6,
        scratch_shapes=[WIDEN, SHRINK, pltpu.SemaphoreType.DMA((6,))],
        compiler_params=params(),
        cost_estimate=cost(7),
    )(scal, base, got, cot, cot_other, slope, smalls, owner, spread, group, wg)


def feed_close(index, scal, base, got, unit1, rstd1, sums, smalls, owner, spread, group, wg):
    return pl.pallas_call(
        feed_close_kernel,
        name=f"feed_close_{index}",
        out_shape=(
            shape((HALF, D), F32),
            shape((HALF, D), BF),
            shape((HALF, OWN), BF),
            shape((16, D), F32),
        ),
        in_specs=[SMEM] + [VM] * 9 + [HBM],
        out_specs=[VM] * 4,
        scratch_shapes=[MERGE, pltpu.SemaphoreType.DMA((4,))],
        compiler_params=params(),
        cost_estimate=cost(4),
    )(scal, base, got, unit1, rstd1, sums, smalls, owner, spread, group, wg)


def weight_grads(scal, *halves):
    return pl.pallas_call(
        weight_grad_kernel,
        name="weight_grads",
        out_shape=(shape((8, 192, D), BF), shape((8, 192, D), BF)),
        in_specs=[SMEM] + [VM] * 8,
        out_specs=[VM] * 2,
        scratch_shapes=[pltpu.VMEM((2 * D, D), F32), pltpu.VMEM((2, D, D), F32)],
        compiler_params=params(),
        cost_estimate=cost(7),
    )(scal, *halves)


def project_back(scal, parts, dh1, gathered):
    def kernel(scal, *refs):
        project_back_kernel(scal, refs[:4], refs[4:6], *refs[6:])

    return pl.pallas_call(
        kernel,
        name="project_back",
        out_shape=(shape((HALF, D), F32), shape((HALF, D), BF)),
        in_specs=[SMEM] + [VM] * 6 + [HBM],
        out_specs=[VM] * 2,
        scratch_shapes=[
            pltpu.VMEM((9, D, 128), BF),
            pltpu.VMEM((GROUP, 3 * OWN), BF),
            pltpu.SemaphoreType.DMA((16,)),
        ],
        compiler_params=params(),
        cost_estimate=cost(6),
    )(scal, *parts, *dh1, gathered)


def swap(value, axis, bit):
    count = lax.axis_size(axis)
    return lax.ppermute(value, axis, [(i, i ^ bit) for i in range(count)])


def shifted(value, axis, steps):
    count = lax.axis_size(axis)
    leading, last = (max(0, -steps), min(count, count - steps))
    return lax.ppermute(value, axis, [(source, source + steps) for source in range(leading, last)])


def tie(*values):
    return lax.optimization_barrier(values)


CORE, ALONG_Y, SIDE = ("fsdp", 1), ("fsdp", 2), ("seq", 1)


def along_z(values):
    groups = [[4 * z + i for z in range(4)] for i in range(4)]
    return lax.all_to_all(values, "fsdp", 0, 0, axis_index_groups=groups, tiled=True)


def add(mine, got):
    return (mine.astype(F32) + got.astype(F32)).astype(mine.dtype)


def by_core(value):
    return value.reshape(2, 4, *value.shape[1:])


def sum_core(keep, got):
    keep = by_core(keep)
    return add(keep[0], got[0]), add(keep[1], got[1])


def sum_z(got):
    return jnp.sum(got.astype(F32), axis=0).astype(got.dtype)


def in_order(flag, mine, other, axis):
    first = jnp.where(flag == 0, mine, other)
    second = jnp.where(flag == 0, other, mine)
    return jnp.concatenate([first, second], axis=axis)


def locate(index, opening, finish, stream_rows):
    document = jnp.sum((finish[None, :] <= index[:, None]).astype(jnp.int32), axis=1)
    begin = jnp.max(jnp.where(opening[None, :] <= index[:, None], opening[None, :], 0), axis=1)
    inside = (index >= 0) & (index < stream_rows)
    document = jnp.where(inside, document, -1)
    position = (index - begin) % MPOS
    return document, position


def own_columns(weight, nf, side, place):
    rows = weight.shape[0]
    weight = weight.reshape(rows, 3, 2, OWN)
    core = place % 2
    keep = lax.dynamic_index_in_dim(weight, side, 2, False).reshape(rows, 3 * OWN)
    give = lax.dynamic_index_in_dim(weight, 1 - side, 2, False).reshape(rows, 3 * OWN)
    straight, crossed, near = [], [], []
    for s in range(2):
        for f in range(nf):
            here = s * nf + f
            if f % 2 == s:
                straight.append((here, (1 - s) * nf + f))
            else:
                crossed.append((here, (1 - s) * nf + (f ^ 1)))
                near.append((here, s * nf + (f ^ 1)))
    axes = ("seq", "fsdp")
    same = core == side
    mine = jnp.where(same, keep, lax.ppermute(give, axes, straight))
    other = jnp.where(same, lax.ppermute(keep, axes, near), lax.ppermute(give, axes, crossed))
    return in_order(core, mine, other, 0)


def per_device(
    incoming_state,
    projection_matrix_triple,
    merge_matrix,
    widen_matrix,
    shrink_matrix,
    offset_table,
    norm_scales,
    widen_offset,
    trainable_gate_scores,
    gate_perturbation,
    softening_scale,
    passage_extents,
    result_cotangent,
):
    BOTH = ("seq", "fsdp")
    ns, nf = lax.axis_size("seq"), lax.axis_size("fsdp")
    count = ns * nf
    fast = nf == 16
    side, place = lax.axis_index("seq"), lax.axis_index("fsdp")
    tokens = incoming_state.reshape(HALF, D)
    cot = result_cotangent.reshape(HALF, D)
    stream_rows = GROUP * nf
    rows = projection_matrix_triple.shape[0]
    zero = jnp.zeros((), jnp.int32)
    core, unit = (place % 2, place // 2) if fast else (zero, zero)

    relaxed = jax.nn.sigmoid(
        (trainable_gate_scores + gate_perturbation) / softening_scale[:, None, None]
    )
    relaxed_low = relaxed.astype(BF)
    wide_cols, up_cols = D // count, FF // count
    pad_to = lambda value: jnp.pad(value, ((0, 0), (0, 128 - value.shape[1])))
    packed = jnp.concatenate(
        [
            pad_to(offset_table),
            pad_to(norm_scales),
            pad_to(widen_offset.reshape(1, up_cols)),
            jnp.zeros((7, 128), BF),
        ],
        axis=0,
    )
    lane, row = jnp.arange(D, dtype=jnp.int32)[None, :], jnp.arange(128, dtype=jnp.int32)[:, None]
    spread, group = (lane % wide_cols == row).astype(BF), lane // wide_cols
    spread_up, group_up = (lane % up_cols == row).astype(BF), lane // up_cols

    finish = jnp.cumsum(passage_extents)
    opening = finish - passage_extents
    base = place * GROUP - GROUP
    doc, pos = locate(base + jnp.arange(WINDOW, dtype=jnp.int32), opening, finish, stream_rows)
    edges = base + GROUP + jnp.asarray([0, HALF - 1, HALF, GROUP - 1], jnp.int32)
    edge_begin = jnp.max(jnp.where(opening[None, :] <= edges[:, None], opening[None, :], 0), axis=1)
    edge_end = jnp.min(
        jnp.where(finish[None, :] > edges[:, None], finish[None, :], stream_rows), axis=1
    )
    lows = jnp.clip((edge_begin - base) // CHUNK, 0, 6)
    highs = jnp.clip((edge_end - base + CHUNK - 1) // CHUNK, 0, 6)
    scal = jnp.stack(
        [unit, core, side, lows[0], highs[1], lows[2], highs[3], zero]
    ).astype(jnp.int32)
    before = shifted(tokens, "fsdp", 1)
    after = shifted(tokens, "fsdp", -1)
    other_tokens = swap(tokens, "seq", 1)
    if fast:
        halves = widen_matrix.reshape(rows, 2, FF // 2)
        keep = lax.dynamic_index_in_dim(halves, side, 1, False)
        give = lax.dynamic_index_in_dim(halves, 1 - side, 1, False)
        mine = jnp.concatenate([keep, merge_matrix], axis=1)[None]
        got = swap(jnp.concatenate([give, merge_matrix], axis=1)[None], *SIDE)
        wide = in_order(side, mine, got, 0)
        wide = jnp.concatenate(
            [wide[:, :, : FF // 2].reshape(2, rows, 2, D), wide[:, :, FF // 2 :].reshape(2, rows, 2, OWN)],
            axis=3,
        )
        mine = lax.dynamic_index_in_dim(wide, core, 2, False)
        sent = lax.dynamic_index_in_dim(wide, 1 - core, 2, False)
        wide = in_order(core, mine, swap(sent, *CORE), 1)
        shard = jnp.concatenate(
            [
                shrink_matrix,
                wide[:, :, :D].reshape(96, D),
                wide[:, :, D:].transpose(1, 0, 2).reshape(48, D),
            ],
            axis=0,
        )
        wq = own_columns(projection_matrix_triple, nf, side, place)
        pack = jnp.concatenate(
            [
                relaxed_low.reshape(6, 32, 4, 128).transpose(0, 2, 1, 3).reshape(768, 128),
                wq.reshape(48, 9, 128).transpose(1, 0, 2).reshape(432, 128),
                packed,
                jnp.zeros((32, 128), BF),
            ],
            axis=0,
        )
        gathered = lax.all_gather(pack, "fsdp", axis=0, tiled=True)
        other_tokens, before, after, scal, pos, doc = tie(
            other_tokens, before, after, scal, pos, doc
        )
        other_before = swap(before, *SIDE)
        other_after = swap(after, *SIDE)
        other_before, other_after, shard, cot = tie(other_before, other_after, shard, cot)
        wg = lax.all_gather(shard, "fsdp", axis=0, tiled=True).reshape(8, 2, 240, D)
        cot_other = swap(cot, *SIDE)
        cot_other, gathered = tie(cot_other, gathered)
        weights, table = gathered.reshape(16, 26, 48, 128), gathered.reshape(16, 39, 32, 128)
        near_owner = jnp.arange(nf, dtype=jnp.int32)[:, None]
        near = weights[:, 25, 0:16].transpose(1, 0, 2)
    else:
        other_before = swap(before, "seq", 1)
        other_after = swap(after, "seq", 1)
        full = lax.all_gather(projection_matrix_triple, BOTH, axis=0, tiled=True)
        full = lax.dynamic_index_in_dim(full.reshape(D, 3, 2, OWN), side, 2, False)
        full = full.reshape(2, 8, 48, 9, 128).transpose(1, 0, 3, 2, 4).reshape(16, 9, 48, 128)
        table = lax.all_gather(relaxed_low, "fsdp", axis=1, tiled=True)
        table = table.reshape(6, 16, 32, 4, 128).transpose(1, 0, 3, 2, 4).reshape(16, 24, 32, 128)
        weights = jnp.concatenate([table.reshape(16, 16, 48, 128), full], axis=1)
        smalls = lax.all_gather(packed[None], BOTH, axis=0, tiled=True).transpose(1, 0, 2)
        near = lax.dynamic_slice_in_dim(smalls, side * nf, nf, 1)
        near_owner = jnp.arange(nf, dtype=jnp.int32)[:, None]
        owner = jnp.arange(count, dtype=jnp.int32)[:, None]
        cot_other = swap(cot, *SIDE)
        up = lax.all_gather(widen_matrix, BOTH, axis=0, tiled=True)
        up = lax.dynamic_slice_in_dim(up, side * (FF // 2), FF // 2, 1)
        up = up.reshape(2, 8, 48, 2, D).transpose(1, 3, 0, 2, 4).reshape(8, 2, 96, D)
        down = lax.all_gather(shrink_matrix, "fsdp", axis=0, tiled=True).reshape(8, 2, 96, D)
        out = lax.all_gather(merge_matrix, BOTH, axis=0, tiled=True)
        out = out.reshape(2, 8, 48, 2, OWN).transpose(1, 3, 2, 0, 4).reshape(8, 2, 48, D)
        wg = jnp.concatenate([down, up, out], axis=2)

    pos_col, doc_col = pos.reshape(WINDOW, 1), doc.reshape(WINDOW, 1)
    pos_row, doc_row = pos.reshape(6, 1, CHUNK), doc.reshape(6, 1, CHUNK)
    pieces = (tokens, before, after, other_tokens, other_before, other_after)
    q, k, v, xw = project(scal, pieces, weights, near, near_owner, spread, group)
    if fast:
        far = swap(near, "seq", 1)
        smalls = jnp.concatenate([near, far], axis=1)
        owner = jnp.concatenate([side * nf + near_owner, (1 - side) * nf + near_owner], axis=0)
        q, smalls = tie(q, smalls)
    ctx, inverses, *kept = attend(scal, pos_col, pos_row, doc_col, doc_row, q, k, v, table)
    ctx_other = swap(ctx, *SIDE)
    params_of = (smalls, owner, spread, group, wg)
    up = lambda i: feed_up(
        i, scal, xw, ctx, ctx_other, smalls, owner, near, near_owner,
        (spread, group, spread_up, group_up), wg,
    )
    down = lambda i, base, got, slope: feed_back(
        i, scal, base, got, cot, cot_other, slope, *params_of
    )
    close = lambda i, base, got, unit, rstd, sums: feed_close(
        i, scal, base, got, unit, rstd, sums, *params_of
    )
    up0 = up(0)
    got0 = swap(up0[4], *SIDE)
    up1, got0 = tie(up(1), got0)
    got1 = swap(up1[4], *SIDE)
    down0, got1 = tie(down(0, up0[3], got0, up0[6]), got1)
    got0 = swap(down0[4], *SIDE)
    down1, got0 = tie(down(1, up1[3], got1, up1[6]), got0)
    got1 = swap(down1[4], *SIDE)
    closed0 = close(0, down0[3], got0, up0[0], up0[1], down0[5] + down1[5])
    feed = weight_grads(
        scal, up0[5], down0[1], up0[2], down0[2], up1[5], down1[1], up1[2], down1[2]
    )
    closed0, feed, got1 = tie(closed0, feed, got1)
    if fast:
        feed_got = swap(by_core(feed[1]), *CORE)
    closed1 = close(1, down1[3], got1, up1[0], up1[1], closed0[3])
    if fast:
        closed1, feed_got = tie(closed1, feed_got)
        feed = sum_core(feed[0], feed_got)
        feed_got = swap(feed[1], *ALONG_Y)
    dh1, dattn, dctx = [[c[i] for c in (closed0, closed1)] for i in range(3)]
    sums = closed1[3]
    lay = jnp.where(side == 0, down0[0], down1[0])
    back = lambda first, pairs, before: attend_back(
        first, pairs, before, scal, q, k, v, kept, xw, sums, ctx, dctx, dattn, inverses
    )
    outs = back(0, 2, ())
    if fast:
        outs, feed_got = tie(outs, feed_got)
        feed = add(feed[0][:2], feed_got[:2]), add(feed[0][2:], feed_got[2:])
        outs, feed = tie(outs, feed)
        feed_got = swap(feed[1], "fsdp", 4)
    outs = back(2, 1, outs)
    if fast:
        outs, feed_got = tie(outs, feed_got)
        feed = add(feed[0][0], feed_got[0]), add(feed[0][1], feed_got[1])
        outs, feed = tie(outs, feed)
        feed_got = swap(feed[1], "fsdp", 8)
    dq, own, low, high, *parts = outs
    own_cols = lambda values, at, size: lax.dynamic_slice_in_dim(values, at * size, size, 1)
    if fast:
        part_got = swap(by_core(parts[1]), *CORE)
        table_got = swap(by_core(parts[3]), *CORE)
        part_got, table_got = tie(part_got, table_got)
        part, table_part = sum_core(parts[0], part_got), sum_core(parts[2], table_got)
        part_got = swap(part[1], *ALONG_Y)
        part_got, feed_got, table_part, low, high = tie(
            part_got, feed_got, table_part, low, high
        )
        part_got = along_z(add(part[0], part_got))
        table_got = swap(table_part[1], *ALONG_Y)
        left, right = shifted(high, "fsdp", 1), shifted(low, "fsdp", -1)
        table_got, left, right = tie(table_got, left, right)
        table_got = along_z(add(table_part[0], table_got))
        dx, dx_send = project_back(scal, (dq, own, left, right), dh1, weights)
        dx_got = swap(dx_send, *SIDE)
        shard = add(feed[0], feed_got)
        part = sum_z(part_got)
        table_total = sum_z(table_got)
        table_total = table_total.reshape(3, 2, 4, 32, 128).transpose(0, 1, 3, 2, 4)
        table_total = table_total.reshape(6, 32, MPOS).astype(F32)
        blocks = part.reshape(3, PART, 128)
        weight = blocks[:, :PART_TOTALS].reshape(3, 3, 2, rows, 128).transpose(1, 0, 2, 3, 4)
        mine = lax.dynamic_index_in_dim(weight, side, 2, False)
        sent = lax.dynamic_index_in_dim(weight, 1 - side, 2, False)
        sums = blocks[:, PART_SUMS:PART_OUT].reshape(6, 16, 128)
        sums = sums.transpose(1, 0, 2).reshape(16, D).astype(F32)
        outs = blocks[:, PART_OUT:].reshape(6, rows, 128)
        grad_w_out = outs.transpose(1, 0, 2).reshape(rows, D).astype(F32)
        got = swap(sent.reshape(-1, 128), *SIDE)
        got = got.reshape(3, 3, rows, 128)
        mine = mine.transpose(2, 0, 1, 3).reshape(rows, 3, 1, OWN)
        got = got.transpose(2, 0, 1, 3).reshape(rows, 3, 1, OWN)
        grad_w_qkv = in_order(side, mine, got, 2).reshape(rows, 3 * D).astype(F32)
        head_sums = blocks[:, PART_TOTALS : PART_TOTALS + 2].transpose(1, 0, 2).reshape(2, OWN)
        head_sums = head_sums.astype(F32)
        head_grads = own_cols(head_sums, place, wide_cols)
        grad_w_down = shard[:96].astype(F32)
        wide = shard[96:192].reshape(2, 2, rows, D).transpose(0, 2, 1, 3).reshape(2, rows, FF // 2)
        mine = lax.dynamic_index_in_dim(wide, side, 0, False)
        got = swap(lax.dynamic_index_in_dim(wide, 1 - side, 0, False), *SIDE)
        grad_w_up = in_order(side, mine, got, 1).astype(F32)
    else:
        scatter = partial(lax.psum_scatter, axis_name=BOTH, scatter_dimension=0, tiled=True)
        left, right = shifted(high, "fsdp", 1), shifted(low, "fsdp", -1)
        dx, dx_send = project_back(scal, (dq, own, left, right), dh1, weights)
        dx_got = swap(dx_send, "seq", 1)

        def plain(pair, at=lambda u: 4 * (u & 1) + (u >> 1)):
            both = jnp.stack(pair, axis=1)
            return jnp.stack([both[at(u)] for u in range(8)], axis=0)

        blocks = plain(parts[:2]).reshape(8, 2, 3, PART, 128)
        table_grad = plain(parts[2:]).reshape(8, 2, 3, 2, 4, 32, 128).transpose(2, 3, 0, 1, 5, 4, 6)
        table_total = lax.psum_scatter(
            table_grad.reshape(6, MPOS, MPOS), "fsdp", scatter_dimension=1, tiled=True
        ).astype(F32)
        head_rows = blocks[:, :, :, :PART_TOTALS].reshape(8, 2, 3, 3, 2, 24, 128)
        head_rows = head_rows.transpose(4, 0, 1, 5, 3, 2, 6).reshape(D, 3, 1, OWN)
        blank = jnp.zeros_like(head_rows)
        both = jnp.concatenate(
            [jnp.where(side == 0, head_rows, blank), jnp.where(side == 0, blank, head_rows)], axis=2
        )
        grad_w_qkv = scatter(both.reshape(D, 3 * D)).astype(F32)
        head_sums = blocks[0, 0, :, PART_TOTALS : PART_TOTALS + 2].transpose(1, 0, 2)
        head_sums = lax.psum(head_sums.reshape(2, OWN).astype(F32), "fsdp")
        head_grads = own_cols(head_sums, place, wide_cols)
        def placed(value, axis):
            blank = jnp.zeros_like(value)
            sides = [jnp.where(side == 0, value, blank), jnp.where(side == 0, blank, value)]
            return jnp.concatenate(sides, axis=axis)

        gg = plain(feed, lambda u: 4 * (u & 1) + (u & 2) + (u >> 2)).reshape(16, 192, D)
        grad_w_down = scatter(placed(gg[:, :96].reshape(FF // 2, D), 0)).astype(F32)
        up = gg[:, 96:192].reshape(16, 2, 2, 24, D).transpose(1, 0, 3, 2, 4).reshape(D, FF // 2)
        grad_w_up = scatter(placed(up, 1)).astype(F32)
        out = blocks[:, :, :, PART_OUT:].reshape(8, 2, 3, 2, 24, 128).transpose(0, 1, 4, 2, 3, 5)
        out = out.reshape(OWN, D)
        grad_w_out = scatter(placed(out, 0)).astype(F32)
        sums = lax.psum(sums, "fsdp")
    ours = own_cols(sums[:6], side * nf + place, wide_cols)
    grad_biases = jnp.concatenate([head_grads, ours[:4]], axis=0)
    grad_gains = ours[4:]
    grad_bias_up = lax.dynamic_slice_in_dim(
        sums[8:10].reshape(-1), place * up_cols, up_cols, 0
    )
    input_grad = dx + dx_got.astype(F32)
    mask_logit_gradient = (
        table_total * relaxed * (1.0 - relaxed) / softening_scale[:, None, None]
    )
    return (
        lay.reshape(1, HALF, D),
        input_grad.reshape(1, HALF, D),
        grad_w_qkv,
        grad_w_out,
        grad_w_up,
        grad_w_down,
        grad_biases,
        grad_gains,
        grad_bias_up,
        mask_logit_gradient,
    )


def solution(mesh):
    rows = P(("seq", "fsdp"), None)
    columns = P(None, ("seq", "fsdp"))
    block = P("fsdp", "seq", None)
    table = P("seq", "fsdp", None)
    return jax.shard_map(
        per_device,
        mesh=mesh,
        in_specs=(
            block, rows, rows, rows, rows, columns, columns, P(("seq", "fsdp")),
            table, table, P("seq"), P(), block,
        ),
        out_specs=(
            block, block, rows, rows, rows, rows, columns, columns, P(("seq", "fsdp")), table,
        ),
        check_vma=False,
    )
```

```python
from functools import partial

import jax
import jax.numpy as jnp
from jax import lax
from jax.experimental import pallas as pl
from jax.experimental.pallas import tpu as pltpu
from jax.sharding import PartitionSpec as P

D = 768
FF = 3072
HEADS = 12
HDIM = 64
MPOS = 512
EPS = 1e-05
GROUP = 512
HALF = 256
WINDOW = 3 * GROUP
OWN = 384
CHUNK = 256
NEG = -1e30
BF = jnp.bfloat16
F32 = jnp.float32
HIGH = lax.Precision.HIGHEST
PART_TOTALS = 144
PART_SUMS = 160
PART_OUT = 192
PART = 240
PART_TABLE = 256


def nn(left, right):
    return jnp.dot(left, right, preferred_element_type=F32)


def nt(left, right, precision=None):
    return lax.dot_general(
        left, right, (((1,), (1,)), ((), ())), precision=precision, preferred_element_type=F32
    )


def tn(left, right):
    return lax.dot_general(left, right, (((0,), (0,)), ((), ())), preferred_element_type=F32)


def load_projection(gathered, w, sem):
    copies = []
    for f in range(16):
        row = (f % 2) * OWN + (f // 2) * 48
        copies.append(
            pltpu.make_async_copy(gathered.at[f, 16:25], w.at[:, row : row + 48, :], sem.at[f])
        )
    for copy in copies:
        copy.start()
    return copies


def table_of(table, head):
    return jnp.concatenate(
        [table[:, 4 * head + part].reshape(MPOS, 128) for part in range(4)], axis=1
    )


def spread_out(values, spread, owner, group):
    return jnp.sum(jnp.where(owner == group, nn(values, spread), 0.0), axis=0, keepdims=True)


def columns_of(w, first, count=3):
    return jnp.concatenate([w[first + part] for part in range(count)], axis=1)


def place_of(t, cr, scal):
    unit = ((t >> 2) ^ (scal[0] & 1)) | ((t & 3) << 1)
    return 2 * unit + (scal[1] ^ cr)


def near_place_of(t, cr, scal):
    unit = ((t >> 2) | (t & 2) | ((t & 1) << 2)) ^ scal[0]
    return 2 * unit + (scal[1] ^ cr)


def project_kernel(
    scal,
    x1,
    x0,
    x2,
    y1,
    y0,
    y2,
    gathered,
    near,
    owner,
    spread,
    group,
    q_ref,
    k_ref,
    v_ref,
    xw,
    k_turned,
    x_turned,
    w,
    sem,
):
    copies = load_projection(gathered, w, sem)
    side = scal[2]
    for g, (mine, other) in enumerate(((x0, y0), (x1, y1), (x2, y2))):
        xw[pl.ds(pl.multiple_of(g * GROUP + side * HALF, HALF), HALF), :] = mine[...]
        xw[pl.ds(pl.multiple_of(g * GROUP + (1 - side) * HALF, HALF), HALF), :] = other[...]
    bias = [
        spread_out(near[i], spread[:, :OWN], owner[...], group[:, :OWN]) for i in range(2)
    ]
    for copy in copies:
        copy.wait()
    for blk in range(6):
        rows = slice(blk * HALF, (blk + 1) * HALF)
        here = xw[rows, :]
        key = nn(here, columns_of(w, 3))
        k_ref[rows, :] = key.astype(BF)
        k_turned[blk] = key.T.astype(BF)
        x_turned[:, rows] = here.astype(F32).T.astype(BF)
        v_ref[rows, :] = (nn(here, columns_of(w, 6)) + bias[1]).astype(BF)
        if blk in (2, 3):
            local = slice((blk - 2) * HALF, (blk - 1) * HALF)
            query = (nn(here, columns_of(w, 0)) + bias[0]).astype(BF)
            q_ref[local, :] = query * jnp.asarray(0.125, BF)


def head_lanes():
    return lax.broadcasted_iota(jnp.int32, (1, 128), 1) < HDIM


def fill_hot(pos_col, hot):
    for blk in range(6):
        rows = slice(blk * 256, (blk + 1) * 256)
        column = lax.broadcasted_iota(jnp.int32, (256, MPOS), 1)
        hot[rows, :] = jnp.where(pos_col[rows, :] == column, 1.0, 0.0).astype(BF)


def fill_hot_turned(pos_row, hot):
    for blk in range(6):
        rows = lax.broadcasted_iota(jnp.int32, (MPOS, 256), 0)
        hot[blk] = jnp.where(pos_row[blk] == rows, 1.0, 0.0).astype(BF)


def set_pair(low, value, target):
    blank = jnp.zeros_like(value)
    target[:HALF, :] = jnp.where(low, value, blank)
    target[HALF:, :] = jnp.where(low, blank, value)


def fold(values, how):
    rows, columns = values.shape
    return how(values.reshape(rows // 8, 8, columns), axis=0)


def attend_kernel(
    scal,
    pos_col,
    pos_row,
    doc_col,
    doc_row,
    q,
    k,
    v,
    table,
    ctx,
    inverses,
    weights,
    mixes,
    hot_turned,
    hot,
    sbuf,
    looks,
    queries,
    acc,
):
    @pl.when(pl.program_id(0) == 0)
    def _():
        fill_hot(pos_col, hot)
        fill_hot_turned(pos_row, hot_turned)

    low = head_lanes()
    for qb in range(2):
        lo, hi = scal[3 + 2 * qb], scal[4 + 2 * qb]
        here = slice(qb * HALF, (qb + 1) * HALF)
        set_pair(low, q[here, :], queries)
        q_doc = jnp.concatenate([doc_row[2 + qb]] * 2, axis=1)
        q_hot = hot[GROUP + qb * HALF : GROUP + (qb + 1) * HALF, :]
        for h in range(2):
            looks[h * HALF : (h + 1) * HALF, :] = nn(q_hot, table_of(table, h)).astype(BF)

        def score_step(c, top, q_doc=q_doc):
            rows = pl.ds(pl.multiple_of(c * CHUNK, CHUNK), CHUNK)
            s = jnp.where(doc_col[rows, :] == q_doc, nt(k[rows, :], queries[...]), NEG)
            sbuf[c] = s
            return jnp.maximum(top, fold(s, jnp.max))

        top = lax.fori_loop(lo, hi, score_step, jnp.full((8, 2 * HALF), NEG, F32))
        top = jnp.max(top, axis=0, keepdims=True)
        acc[...] = jnp.zeros_like(acc)

        def mix_step(c, total, top=top, qb=qb):
            rows = pl.ds(pl.multiple_of(c * CHUNK, CHUNK), CHUNK)
            e = jnp.exp(sbuf[c] - top)
            mixed = (e * nt(hot[rows, :], looks[...])).astype(BF)
            weights[0, qb, c] = e.astype(BF)
            mixes[0, qb, c] = mixed
            acc[...] += tn(mixed, v[rows, :])
            return total + fold(e, jnp.sum)

        total = lax.fori_loop(lo, hi, mix_step, jnp.zeros((8, 2 * HALF), F32))
        total = jnp.sum(total, axis=0, keepdims=True)
        inverse = 1.0 / total
        inverses[0, 0:1, here] = inverse[:, :HALF]
        inverses[0, 1:2, here] = inverse[:, HALF:]
        inverses[0, 2:8, here] = jnp.zeros((6, HALF), F32)
        scale = jnp.concatenate(
            [
                jnp.broadcast_to(inverse[:, :HALF], (HDIM, HALF)),
                jnp.broadcast_to(inverse[:, HALF:], (HDIM, HALF)),
            ],
            axis=0,
        ).T
        ctx[qb] = (jnp.where(low, acc[:HALF, :], acc[HALF:, :]) * scale).astype(BF)


def attend_back_kernel(
    carried,
    scal,
    q,
    k,
    v,
    weights,
    mixes,
    hot_turned,
    xw,
    sums,
    ctx,
    ctx_all,
    dctx0,
    dctx1,
    dattn0,
    dattn1,
    inverses,
    *refs,
):
    outs = refs[carried : carried + 8]
    dq, own, halo_low, halo_high, part_keep, part_send, table_keep, table_send = outs
    queries, grads, dk, dv, dq_acc, tt, tg, gw, gout = refs[carried + 8 :]
    low = head_lanes()
    dk[...] = jnp.zeros_like(dk)
    dv[...] = jnp.zeros_like(dv)
    lane = lax.broadcasted_iota(jnp.int32, (8, 128), 1)
    row8 = lax.broadcasted_iota(jnp.int32, (8, 128), 0)
    pick = jnp.where((lane < HDIM) == (row8 == 0), 1.0, 0.0)
    for qb in range(2):
        lo, hi = scal[3 + 2 * qb], scal[4 + 2 * qb]
        here = slice(qb * HALF, (qb + 1) * HALF)
        inverse = inverses[0, 0:2, here]
        d_pair = (dctx0, dctx1)[qb][...].astype(F32)
        deltas = nt(pick, d_pair * ctx[qb].astype(F32), HIGH)[0:2, :] * inverse
        delta = jnp.concatenate([deltas[0:1, :], deltas[1:2, :]], axis=1)
        scale = jnp.concatenate(
            [
                jnp.broadcast_to(inverse[0:1, :], (HDIM, HALF)),
                jnp.broadcast_to(inverse[1:2, :], (HDIM, HALF)),
            ],
            axis=0,
        ).T
        set_pair(low, q[here, :], queries)
        set_pair(low, (d_pair * scale).astype(BF), grads)
        dq_acc[...] = jnp.zeros_like(dq_acc)
        tt[...] = jnp.zeros_like(tt)

        def step(c, carry, delta=delta, qb=qb):
            rows = pl.ds(pl.multiple_of(c * CHUNK, CHUNK), CHUNK)
            mixed = mixes[0, qb, c]
            e = weights[0, qb, c].astype(F32)
            dm = nt(v[rows, :], grads[...])
            ds = (mixed.astype(F32) * dm - e * delta).astype(BF)
            dv[rows, :] += nn(mixed, grads[...])
            dk[rows, :] += nn(ds, queries[...])
            dq_acc[...] += nn(k[c], ds)
            tt[...] += nn(hot_turned[c], (e * dm).astype(BF))
            return carry

        lax.fori_loop(lo, hi, step, 0)
        for h in range(2):
            piece = nt(hot_turned[2 + qb], tt[:, h * HALF : (h + 1) * HALF].astype(BF))
            if qb == 0:
                tg[h] = piece
            else:
                tg[h] += piece
        both = jnp.concatenate([dq_acc[:HDIM, :HALF], dq_acc[HDIM:, HALF:]], axis=0)
        dq[here, :] = (both.T * 0.125).astype(BF)
    own[0] = dk[GROUP : 2 * GROUP, :]
    own[1] = dv[GROUP : 2 * GROUP, :]
    halo_low[0] = dk[:GROUP, :].astype(BF)
    halo_low[1] = dv[:GROUP, :].astype(BF)
    halo_high[0] = dk[2 * GROUP :, :].astype(BF)
    halo_high[1] = dv[2 * GROUP :, :].astype(BF)
    query_grad = dq[...]
    pair_grad = jnp.concatenate([dk[...].astype(BF), dv[...].astype(BF)], axis=1)
    gw[:, 0:128] = nn(xw[:, GROUP : 2 * GROUP], query_grad)
    gw[:, 128:384] = nn(xw[...], pair_grad)
    gout[...] = tn(ctx_all[0], dattn0[...]) + tn(ctx_all[1], dattn1[...])
    totals = jnp.concatenate(
        [
            column_sum(query_grad.astype(F32)),
            column_sum(pair_grad[:, 128:].astype(F32)),
            jnp.zeros((14, 128), F32),
            sums[:, 0:128],
            sums[:, 128:256],
        ],
        axis=0,
    ).astype(BF)
    for cr in range(2):
        out, table = (part_keep, table_keep) if cr == 0 else (part_send, table_send)
        for t in range(8):
            place = place_of(t, cr, scal)
            rows = [
                gw[pl.ds(pl.multiple_of(part * OWN + place * 24, 8), 24), :] for part in range(2)
            ]
            both = jnp.concatenate(rows, axis=0).astype(BF)
            for i in range(3):
                out[t, i * 48 : i * 48 + 48, :] = both[:, i * 128 : (i + 1) * 128]
            out[t, PART_TOTALS:PART_OUT, :] = totals
            rows = gout[pl.ds(pl.multiple_of(place * 24, 8), 24), :]
            out[t, PART_OUT:PART, :] = jnp.concatenate(
                [rows[:, 0:128], rows[:, 128:256]], axis=0
            ).astype(BF)
            for h in range(2):
                mask = tg[h, pl.ds(pl.multiple_of(place * 32, 32), 32), :].astype(BF)
                for i in range(4):
                    at = (4 * h + i) * 32
                    table[t, at : at + 32, :] = mask[:, i * 128 : (i + 1) * 128]


def norm_stats(values):
    center = values - jnp.mean(values, axis=-1, keepdims=True)
    rstd = lax.rsqrt(jnp.mean(center * center, axis=-1, keepdims=True) + EPS)
    return center * rstd, rstd


def norm_back(grad, unit, rstd, gain):
    scaled = grad * gain
    return rstd * (
        scaled
        - jnp.mean(scaled, axis=-1, keepdims=True)
        - unit * jnp.mean(scaled * unit, axis=-1, keepdims=True)
    )


def column_sum(values):
    return jnp.sum(values, axis=0, keepdims=True)


def load_feed(wg, sem, wm=None, wu=None, wd=None):
    copies = []

    def bring(source, target):
        copies.append(pltpu.make_async_copy(source, target, sem.at[len(copies)]))
        copies[-1].start()

    for c in range(2):
        for s in range(2):
            if wm is not None:
                bring(
                    wg.at[:, c, 192:240, s * OWN : (s + 1) * OWN],
                    wm.at[s, :, :, c * OWN : (c + 1) * OWN],
                )
    for c in range(2):
        for s in range(2):
            if wu is not None:
                bring(wg.at[:, c, 96 + 48 * s : 144 + 48 * s, :], wu.at[c, s])
    for c in range(2):
        if wd is not None:
            bring(wg.at[:, c, 0:96, :], wd.at[:, c])
    return copies


def shrink_rows(wd, i):
    return wd[pl.ds(4 * i, 4)].reshape(D, D)


def wait_for(copies):
    for copy in copies:
        copy.wait()


def feed_up_kernel(
    scal,
    x,
    ctx_mine,
    ctx_other,
    smalls,
    owner,
    near,
    near_owner,
    spread,
    group,
    spread_up,
    group_up,
    wg,
    unit1,
    rstd1,
    nlow,
    base,
    send,
    act,
    slope,
    wm,
    wu,
    wd,
    ctxt,
    bup,
    sem,
):
    copies = load_feed(wg, sem, wm, wu, wd)
    vector = lambda i: spread_out(smalls[i], spread[...], owner[...], group[...])
    bias_out, bias_down, shift1, gain1 = [vector(i) for i in (2, 3, 4, 6)]
    for n in range(2):
        bup[n] = spread_out(
            near[8], spread_up[...], near_owner[...], group_up[...] + n * (near.shape[1] // 2)
        )
    even = scal[2] == 0
    mine, other = ctx_mine[0], ctx_other[0]
    ctxt[:, :OWN] = jnp.where(even, mine, other)
    ctxt[:, OWN:] = jnp.where(even, other, mine)
    wait_for(copies[:4])
    attn = nn(ctxt[...], wm[...].reshape(D, D)) + bias_out
    unit, rstd = norm_stats(x[...].astype(F32) + attn)
    unit1[...] = unit
    rstd1[...] = jnp.broadcast_to(rstd, (HALF, 128))
    normed = unit * gain1 + shift1
    nlow[...] = normed.astype(BF)
    base[...] = normed + bias_down
    wait_for(copies[4:8])

    def widen(n, carry):
        up = nn(nlow[...], wu[n].reshape(D, D)) + bup[n]
        half_cdf = 0.5 * (1.0 + lax.erf(up * 0.7071067811865476))
        act[n] = (up * half_cdf).astype(BF)
        slope[n] = half_cdf + up * (0.3989422804014327 * jnp.exp(-0.5 * up * up))
        return carry

    lax.fori_loop(0, 2, widen, 0)
    wait_for(copies[8:])
    part = nn(act[0], shrink_rows(wd, 0)) + nn(act[1], shrink_rows(wd, 1))
    base[...] += part
    send[...] = part.astype(BF)


def feed_back_kernel(
    index,
    scal,
    base,
    got,
    cot_mine,
    cot_other,
    slope,
    smalls,
    owner,
    spread,
    group,
    wg,
    lay,
    ddown,
    dup,
    base2,
    send,
    sums,
    wu,
    wd,
    sem,
):
    copies = load_feed(wg, sem, None, wu, wd)
    vector = lambda i: spread_out(smalls[i], spread[...], owner[...], group[...])
    shift2, gain2 = vector(5), vector(7)
    sums[...] = jnp.zeros_like(sums)
    unit, rstd = norm_stats(base[...] + got[...].astype(F32))
    lay[...] = (unit * gain2 + shift2).astype(BF)
    dy = jnp.where(scal[2] == index, cot_mine[...], cot_other[...]).astype(F32)
    sums[3:4, :] = column_sum(dy)
    sums[5:6, :] = column_sum(dy * unit)
    grad = norm_back(dy, unit, rstd, gain2)
    ddown[...] = grad.astype(BF)
    sums[1:2, :] = column_sum(ddown[...].astype(F32))
    base2[...] = grad
    wait_for(copies)

    def back(n, carry):
        low = (nt(ddown[...], shrink_rows(wd, n)) * slope[n]).astype(BF)
        dup[n] = low
        sums[pl.ds(8 + n, 1), :] = column_sum(low.astype(F32))
        return carry

    lax.fori_loop(0, 2, back, 0)
    part = nt(dup[0], wu[0].reshape(D, D)) + nt(dup[1], wu[1].reshape(D, D))
    base2[...] += part
    send[...] = part.astype(BF)


def feed_close_kernel(
    scal,
    base,
    got,
    unit1,
    rstd1,
    sums_in,
    smalls,
    owner,
    spread,
    group,
    wg,
    dh1,
    dattn,
    dctx,
    sums,
    wm,
    sem,
):
    copies = load_feed(wg, sem, wm)
    gain1 = spread_out(smalls[6], spread[...], owner[...], group[...])
    sums[...] = sums_in[...]
    grad = base[...] + got[...].astype(F32)
    unit = unit1[...]
    sums[2:3, :] += column_sum(grad)
    sums[4:5, :] += column_sum(grad * unit)
    grad = norm_back(grad, unit, rstd1[:, 0:1], gain1)
    dh1[...] = grad
    dattn[...] = grad.astype(BF)
    sums[0:1, :] += column_sum(dattn[...].astype(F32))
    wait_for(copies)
    dctx[...] = nt(dattn[...], wm[scal[2]].reshape(OWN, D)).astype(BF)


def weight_grad_kernel(
    scal, act0, ddown0, nlow0, dup0, act1, ddown1, nlow1, dup1, keep, send, down, up
):
    for n in range(2):
        up[n] = tn(nlow0[...], dup0[n]) + tn(nlow1[...], dup1[n])
        down[n * D : (n + 1) * D, :] = tn(act0[n], ddown0[...]) + tn(act1[n], ddown1[...])
    for cr, out in enumerate((keep, send)):
        for t in range(8):
            place = near_place_of(t, cr, scal)
            out[t, 0:96, :] = down[pl.ds(pl.multiple_of(place * 96, 8), 96), :].astype(BF)
            parts = [
                up[n, pl.ds(pl.multiple_of(s * OWN + place * 24, 8), 24), :]
                for s in range(2)
                for n in range(2)
            ]
            out[t, 96:192, :] = jnp.concatenate(parts, axis=0).astype(BF)


def project_back_kernel(scal, parts, dh1s, gathered, dx, dx_send, w, dqkv, sem):
    copies = load_projection(gathered, w, sem)
    dq, own, left, right = parts
    dqkv[:, :OWN] = dq[...]
    for i in range(2):
        total = own[i] + left[i].astype(F32) + right[i].astype(F32)
        dqkv[:, (1 + i) * OWN : (2 + i) * OWN] = total.astype(BF)
    for copy in copies:
        copy.wait()
    side = scal[2]
    mine = dqkv[pl.ds(pl.multiple_of(side * HALF, HALF), HALF), :]
    other = dqkv[pl.ds(pl.multiple_of((1 - side) * HALF, HALF), HALF), :]
    for part in range(3):
        cols = slice(part * 256, (part + 1) * 256)
        rows = jnp.concatenate([w[j, cols, :] for j in range(9)], axis=1)
        dh1 = jnp.where(side == 0, dh1s[0][:, cols], dh1s[1][:, cols])
        dx[:, cols] = dh1 + nt(mine, rows)
        dx_send[:, cols] = nt(other, rows).astype(BF)


SMEM = pl.BlockSpec(memory_space=pltpu.SMEM)
VM = pl.BlockSpec()
HBM = pl.BlockSpec(memory_space=pl.ANY)


def params():
    return pltpu.CompilerParams(vmem_limit_bytes=60 * 1024 * 1024)


def cost(microseconds):
    return pl.CostEstimate(
        flops=int(microseconds * 1.15e9), bytes_accessed=1000, transcendentals=0
    )


def shape(dims, kind):
    return jax.ShapeDtypeStruct(dims, kind)


def project(scal, pieces, gathered, near, owner, spread, group):
    return pl.pallas_call(
        project_kernel,
        name="project",
        out_shape=(
            shape((GROUP, OWN), BF),
            shape((WINDOW, OWN), BF),
            shape((WINDOW, OWN), BF),
            shape((WINDOW, D), BF),
            shape((6, OWN, CHUNK), BF),
            shape((D, WINDOW), BF),
        ),
        in_specs=[SMEM] + [VM] * 6 + [HBM] + [VM] * 4,
        out_specs=[VM] * 6,
        scratch_shapes=[
            pltpu.VMEM((9, D, 128), BF),
            pltpu.SemaphoreType.DMA((16,)),
        ],
        compiler_params=params(),
        cost_estimate=cost(9),
    )(scal, *pieces, gathered, near, owner, spread, group)


def whole(*dims):
    return pl.BlockSpec(dims, lambda p: (0,) * len(dims))


def attend(scal, pos_col, pos_row, doc_col, doc_row, q, k, v, table):
    return pl.pallas_call(
        attend_kernel,
        name="attend",
        grid=(3,),
        out_shape=(
            shape((2, HALF, OWN), BF),
            shape((3, 8, GROUP), F32),
            shape((3, 2, 6, CHUNK, 2 * HALF), BF),
            shape((3, 2, 6, CHUNK, 2 * HALF), BF),
            shape((6, MPOS, CHUNK), BF),
        ),
        in_specs=[
            SMEM,
            whole(WINDOW, 1),
            whole(6, 1, CHUNK),
            whole(WINDOW, 1),
            whole(6, 1, CHUNK),
            pl.BlockSpec((GROUP, 128), lambda p: (0, p)),
            pl.BlockSpec((WINDOW, 128), lambda p: (0, p)),
            pl.BlockSpec((WINDOW, 128), lambda p: (0, p)),
            pl.BlockSpec((16, 8, 32, 128), lambda p: (0, p, 0, 0)),
        ],
        out_specs=[
            pl.BlockSpec((2, HALF, 128), lambda p: (0, 0, p)),
            pl.BlockSpec((1, 8, GROUP), lambda p: (p, 0, 0)),
            pl.BlockSpec((1, 2, 6, CHUNK, 2 * HALF), lambda p: (p, 0, 0, 0, 0)),
            pl.BlockSpec((1, 2, 6, CHUNK, 2 * HALF), lambda p: (p, 0, 0, 0, 0)),
            whole(6, MPOS, CHUNK),
        ],
        scratch_shapes=[
            pltpu.VMEM((WINDOW, MPOS), BF),
            pltpu.VMEM((6, CHUNK, 2 * HALF), F32),
            pltpu.VMEM((2 * HALF, MPOS), BF),
            pltpu.VMEM((2 * HALF, 128), BF),
            pltpu.VMEM((2 * HALF, 128), F32),
        ],
        compiler_params=params(),
        cost_estimate=cost(26),
    )(scal, pos_col, pos_row, doc_col, doc_row, q, k, v, table)


def attend_back(
    first, pairs, before, scal, q, k, v, kept, xw, sums, ctx, dctx, dattn, inverses
):
    columns = lambda rows: pl.BlockSpec((rows, 128), lambda p: (0, first + p))
    tiles = pl.BlockSpec((1, 2, 6, CHUNK, 2 * HALF), lambda p: (first + p, 0, 0, 0, 0))
    blocks = lambda rows: pl.BlockSpec((8, rows, 128), lambda p: (0, first + p, 0))
    both = pl.BlockSpec((2, GROUP, 128), lambda p: (0, 0, first + p))
    return pl.pallas_call(
        partial(attend_back_kernel, len(before)),
        name=f"attend_back_{first}",
        grid=(pairs,),
        input_output_aliases={16 + i: i for i in range(len(before))},
        out_shape=(
            shape((GROUP, OWN), BF),
            shape((2, GROUP, OWN), F32),
            shape((2, GROUP, OWN), BF),
            shape((2, GROUP, OWN), BF),
            shape((8, 3 * PART, 128), BF),
            shape((8, 3 * PART, 128), BF),
            shape((8, 3 * PART_TABLE, 128), BF),
            shape((8, 3 * PART_TABLE, 128), BF),
        ),
        in_specs=[
            SMEM,
            columns(GROUP),
            pl.BlockSpec((6, 128, CHUNK), lambda p: (0, first + p, 0)),
            columns(WINDOW),
            tiles,
            tiles,
            whole(6, MPOS, CHUNK),
            whole(D, WINDOW),
            pl.BlockSpec((16, 256), lambda p: (0, first + p)),
            pl.BlockSpec((2, HALF, 128), lambda p: (0, 0, first + p)),
            whole(2, HALF, OWN),
            columns(HALF),
            columns(HALF),
            pl.BlockSpec((HALF, 256), lambda p: (0, first + p)),
            pl.BlockSpec((HALF, 256), lambda p: (0, first + p)),
            pl.BlockSpec((1, 8, GROUP), lambda p: (first + p, 0, 0)),
        ]
        + [HBM] * len(before),
        out_specs=[
            columns(GROUP),
            both,
            both,
            both,
            blocks(PART),
            blocks(PART),
            blocks(PART_TABLE),
            blocks(PART_TABLE),
        ],
        scratch_shapes=[
            pltpu.VMEM((2 * HALF, 128), BF),
            pltpu.VMEM((2 * HALF, 128), BF),
            pltpu.VMEM((WINDOW, 128), F32),
            pltpu.VMEM((WINDOW, 128), F32),
            pltpu.VMEM((128, 2 * HALF), F32),
            pltpu.VMEM((MPOS, 2 * HALF), F32),
            pltpu.VMEM((2, MPOS, MPOS), F32),
            pltpu.VMEM((D, OWN), F32),
            pltpu.VMEM((OWN, 256), F32),
        ],
        compiler_params=params(),
        cost_estimate=cost(10 * pairs),
    )(scal, q, k, v, *kept, xw, sums, ctx, ctx, *dctx, *dattn, inverses, *before)


WIDEN = pltpu.VMEM((2, 2, 8, 48, D), BF)
SHRINK = pltpu.VMEM((8, 2, 96, D), BF)
MERGE = pltpu.VMEM((2, 8, 48, D), BF)


def feed_up(index, scal, xw, mine, other, smalls, owner, near, near_owner, spreads, wg):
    arrays = (smalls, owner, near, near_owner, *spreads)
    ctx = pl.BlockSpec((1, HALF, OWN), lambda p: (index, 0, 0))
    outs = (
        shape((HALF, D), F32),
        shape((HALF, 128), F32),
        shape((HALF, D), BF),
        shape((HALF, D), F32),
        shape((HALF, D), BF),
        shape((2, HALF, D), BF),
        shape((2, HALF, D), F32),
    )
    return pl.pallas_call(
        feed_up_kernel,
        name=f"feed_up_{index}",
        grid=(1,),
        out_shape=outs,
        in_specs=[SMEM, pl.BlockSpec((HALF, D), lambda p: (2 + index, 0)), ctx, ctx]
        + [whole(*a.shape) for a in arrays]
        + [HBM],
        out_specs=[whole(*out.shape) for out in outs],
        scratch_shapes=[
            MERGE,
            WIDEN,
            SHRINK,
            pltpu.VMEM((HALF, D), BF),
            pltpu.VMEM((2, 1, D), F32),
            pltpu.SemaphoreType.DMA((10,)),
        ],
        compiler_params=params(),
        cost_estimate=cost(8),
    )(scal, xw, mine, other, *arrays, wg)


def feed_back(index, scal, base, got, cot, cot_other, slope, smalls, owner, spread, group, wg):
    return pl.pallas_call(
        partial(feed_back_kernel, index),
        name=f"feed_back_{index}",
        out_shape=(
            shape((HALF, D), BF),
            shape((HALF, D), BF),
            shape((2, HALF, D), BF),
            shape((HALF, D), F32),
            shape((HALF, D), BF),
            shape((16, D), F32),
        ),
        in_specs=[SMEM] + [VM] * 9 + [HBM],
        out_specs=[VM] * 6,
        scratch_shapes=[WIDEN, SHRINK, pltpu.SemaphoreType.DMA((6,))],
        compiler_params=params(),
        cost_estimate=cost(7),
    )(scal, base, got, cot, cot_other, slope, smalls, owner, spread, group, wg)


def feed_close(index, scal, base, got, unit1, rstd1, sums, smalls, owner, spread, group, wg):
    return pl.pallas_call(
        feed_close_kernel,
        name=f"feed_close_{index}",
        out_shape=(
            shape((HALF, D), F32),
            shape((HALF, D), BF),
            shape((HALF, OWN), BF),
            shape((16, D), F32),
        ),
        in_specs=[SMEM] + [VM] * 9 + [HBM],
        out_specs=[VM] * 4,
        scratch_shapes=[MERGE, pltpu.SemaphoreType.DMA((4,))],
        compiler_params=params(),
        cost_estimate=cost(4),
    )(scal, base, got, unit1, rstd1, sums, smalls, owner, spread, group, wg)


def weight_grads(scal, *halves):
    return pl.pallas_call(
        weight_grad_kernel,
        name="weight_grads",
        out_shape=(shape((8, 192, D), BF), shape((8, 192, D), BF)),
        in_specs=[SMEM] + [VM] * 8,
        out_specs=[VM] * 2,
        scratch_shapes=[pltpu.VMEM((2 * D, D), F32), pltpu.VMEM((2, D, D), F32)],
        compiler_params=params(),
        cost_estimate=cost(7),
    )(scal, *halves)


def project_back(scal, parts, dh1, gathered):
    def kernel(scal, *refs):
        project_back_kernel(scal, refs[:4], refs[4:6], *refs[6:])

    return pl.pallas_call(
        kernel,
        name="project_back",
        out_shape=(shape((HALF, D), F32), shape((HALF, D), BF)),
        in_specs=[SMEM] + [VM] * 6 + [HBM],
        out_specs=[VM] * 2,
        scratch_shapes=[
            pltpu.VMEM((9, D, 128), BF),
            pltpu.VMEM((GROUP, 3 * OWN), BF),
            pltpu.SemaphoreType.DMA((16,)),
        ],
        compiler_params=params(),
        cost_estimate=cost(6),
    )(scal, *parts, *dh1, gathered)


def swap(value, axis, bit):
    count = lax.axis_size(axis)
    return lax.ppermute(value, axis, [(i, i ^ bit) for i in range(count)])


def shifted(value, axis, steps):
    count = lax.axis_size(axis)
    leading, last = (max(0, -steps), min(count, count - steps))
    return lax.ppermute(value, axis, [(source, source + steps) for source in range(leading, last)])


def tie(*values):
    return lax.optimization_barrier(values)


CORE, ALONG_Y, SIDE = ("fsdp", 1), ("fsdp", 2), ("seq", 1)


def along_z(values):
    groups = [[4 * z + i for z in range(4)] for i in range(4)]
    return lax.all_to_all(values, "fsdp", 0, 0, axis_index_groups=groups, tiled=True)


def add(mine, got):
    return (mine.astype(F32) + got.astype(F32)).astype(mine.dtype)


def by_core(value):
    return value.reshape(2, 4, *value.shape[1:])


def sum_core(keep, got):
    keep = by_core(keep)
    return add(keep[0], got[0]), add(keep[1], got[1])


def sum_z(got):
    return jnp.sum(got.astype(F32), axis=0).astype(got.dtype)


def in_order(flag, mine, other, axis):
    first = jnp.where(flag == 0, mine, other)
    second = jnp.where(flag == 0, other, mine)
    return jnp.concatenate([first, second], axis=axis)


def locate(index, opening, finish, stream_rows):
    document = jnp.sum((finish[None, :] <= index[:, None]).astype(jnp.int32), axis=1)
    begin = jnp.max(jnp.where(opening[None, :] <= index[:, None], opening[None, :], 0), axis=1)
    inside = (index >= 0) & (index < stream_rows)
    document = jnp.where(inside, document, -1)
    position = (index - begin) % MPOS
    return document, position


def own_columns(weight, nf, side, place):
    rows = weight.shape[0]
    weight = weight.reshape(rows, 3, 2, OWN)
    core = place % 2
    keep = lax.dynamic_index_in_dim(weight, side, 2, False).reshape(rows, 3 * OWN)
    give = lax.dynamic_index_in_dim(weight, 1 - side, 2, False).reshape(rows, 3 * OWN)
    straight, crossed, near = [], [], []
    for s in range(2):
        for f in range(nf):
            here = s * nf + f
            if f % 2 == s:
                straight.append((here, (1 - s) * nf + f))
            else:
                crossed.append((here, (1 - s) * nf + (f ^ 1)))
                near.append((here, s * nf + (f ^ 1)))
    axes = ("seq", "fsdp")
    same = core == side
    mine = jnp.where(same, keep, lax.ppermute(give, axes, straight))
    other = jnp.where(same, lax.ppermute(keep, axes, near), lax.ppermute(give, axes, crossed))
    return in_order(core, mine, other, 0)


def per_device(
    incoming_state,
    projection_matrix_triple,
    merge_matrix,
    widen_matrix,
    shrink_matrix,
    offset_table,
    norm_scales,
    widen_offset,
    trainable_gate_scores,
    gate_perturbation,
    softening_scale,
    passage_extents,
    result_cotangent,
):
    BOTH = ("seq", "fsdp")
    ns, nf = lax.axis_size("seq"), lax.axis_size("fsdp")
    count = ns * nf
    fast = nf == 16
    side, place = lax.axis_index("seq"), lax.axis_index("fsdp")
    tokens = incoming_state.reshape(HALF, D)
    cot = result_cotangent.reshape(HALF, D)
    stream_rows = GROUP * nf
    rows = projection_matrix_triple.shape[0]
    zero = jnp.zeros((), jnp.int32)
    core, unit = (place % 2, place // 2) if fast else (zero, zero)

    relaxed = jax.nn.sigmoid(
        (trainable_gate_scores + gate_perturbation) / softening_scale[:, None, None]
    )
    relaxed_low = relaxed.astype(BF)
    wide_cols, up_cols = D // count, FF // count
    pad_to = lambda value: jnp.pad(value, ((0, 0), (0, 128 - value.shape[1])))
    packed = jnp.concatenate(
        [
            pad_to(offset_table),
            pad_to(norm_scales),
            pad_to(widen_offset.reshape(1, up_cols)),
            jnp.zeros((7, 128), BF),
        ],
        axis=0,
    )
    lane, row = jnp.arange(D, dtype=jnp.int32)[None, :], jnp.arange(128, dtype=jnp.int32)[:, None]
    spread, group = (lane % wide_cols == row).astype(BF), lane // wide_cols
    spread_up, group_up = (lane % up_cols == row).astype(BF), lane // up_cols

    finish = jnp.cumsum(passage_extents)
    opening = finish - passage_extents
    base = place * GROUP - GROUP
    doc, pos = locate(base + jnp.arange(WINDOW, dtype=jnp.int32), opening, finish, stream_rows)
    edges = base + GROUP + jnp.asarray([0, HALF - 1, HALF, GROUP - 1], jnp.int32)
    edge_begin = jnp.max(jnp.where(opening[None, :] <= edges[:, None], opening[None, :], 0), axis=1)
    edge_end = jnp.min(
        jnp.where(finish[None, :] > edges[:, None], finish[None, :], stream_rows), axis=1
    )
    lows = jnp.clip((edge_begin - base) // CHUNK, 0, 6)
    highs = jnp.clip((edge_end - base + CHUNK - 1) // CHUNK, 0, 6)
    scal = jnp.stack(
        [unit, core, side, lows[0], highs[1], lows[2], highs[3], zero]
    ).astype(jnp.int32)
    before = shifted(tokens, "fsdp", 1)
    after = shifted(tokens, "fsdp", -1)
    other_tokens = swap(tokens, "seq", 1)
    if fast:
        halves = widen_matrix.reshape(rows, 2, FF // 2)
        keep = lax.dynamic_index_in_dim(halves, side, 1, False)
        give = lax.dynamic_index_in_dim(halves, 1 - side, 1, False)
        mine = jnp.concatenate([keep, merge_matrix], axis=1)[None]
        got = swap(jnp.concatenate([give, merge_matrix], axis=1)[None], *SIDE)
        wide = in_order(side, mine, got, 0)
        wide = jnp.concatenate(
            [wide[:, :, : FF // 2].reshape(2, rows, 2, D), wide[:, :, FF // 2 :].reshape(2, rows, 2, OWN)],
            axis=3,
        )
        mine = lax.dynamic_index_in_dim(wide, core, 2, False)
        sent = lax.dynamic_index_in_dim(wide, 1 - core, 2, False)
        wide = in_order(core, mine, swap(sent, *CORE), 1)
        shard = jnp.concatenate(
            [
                shrink_matrix,
                wide[:, :, :D].reshape(96, D),
                wide[:, :, D:].transpose(1, 0, 2).reshape(48, D),
            ],
            axis=0,
        )
        wq = own_columns(projection_matrix_triple, nf, side, place)
        pack = jnp.concatenate(
            [
                relaxed_low.reshape(6, 32, 4, 128).transpose(0, 2, 1, 3).reshape(768, 128),
                wq.reshape(48, 9, 128).transpose(1, 0, 2).reshape(432, 128),
                packed,
                jnp.zeros((32, 128), BF),
            ],
            axis=0,
        )
        gathered = lax.all_gather(pack, "fsdp", axis=0, tiled=True)
        other_tokens, before, after, scal, pos, doc = tie(
            other_tokens, before, after, scal, pos, doc
        )
        other_before = swap(before, *SIDE)
        other_after = swap(after, *SIDE)
        other_before, other_after, shard, cot = tie(other_before, other_after, shard, cot)
        wg = lax.all_gather(shard, "fsdp", axis=0, tiled=True).reshape(8, 2, 240, D)
        cot_other = swap(cot, *SIDE)
        cot_other, gathered = tie(cot_other, gathered)
        weights, table = gathered.reshape(16, 26, 48, 128), gathered.reshape(16, 39, 32, 128)
        near_owner = jnp.arange(nf, dtype=jnp.int32)[:, None]
        near = weights[:, 25, 0:16].transpose(1, 0, 2)
    else:
        other_before = swap(before, "seq", 1)
        other_after = swap(after, "seq", 1)
        full = lax.all_gather(projection_matrix_triple, BOTH, axis=0, tiled=True)
        full = lax.dynamic_index_in_dim(full.reshape(D, 3, 2, OWN), side, 2, False)
        full = full.reshape(2, 8, 48, 9, 128).transpose(1, 0, 3, 2, 4).reshape(16, 9, 48, 128)
        table = lax.all_gather(relaxed_low, "fsdp", axis=1, tiled=True)
        table = table.reshape(6, 16, 32, 4, 128).transpose(1, 0, 3, 2, 4).reshape(16, 24, 32, 128)
        weights = jnp.concatenate([table.reshape(16, 16, 48, 128), full], axis=1)
        smalls = lax.all_gather(packed[None], BOTH, axis=0, tiled=True).transpose(1, 0, 2)
        near = lax.dynamic_slice_in_dim(smalls, side * nf, nf, 1)
        near_owner = jnp.arange(nf, dtype=jnp.int32)[:, None]
        owner = jnp.arange(count, dtype=jnp.int32)[:, None]
        cot_other = swap(cot, *SIDE)
        up = lax.all_gather(widen_matrix, BOTH, axis=0, tiled=True)
        up = lax.dynamic_slice_in_dim(up, side * (FF // 2), FF // 2, 1)
        up = up.reshape(2, 8, 48, 2, D).transpose(1, 3, 0, 2, 4).reshape(8, 2, 96, D)
        down = lax.all_gather(shrink_matrix, "fsdp", axis=0, tiled=True).reshape(8, 2, 96, D)
        out = lax.all_gather(merge_matrix, BOTH, axis=0, tiled=True)
        out = out.reshape(2, 8, 48, 2, OWN).transpose(1, 3, 2, 0, 4).reshape(8, 2, 48, D)
        wg = jnp.concatenate([down, up, out], axis=2)

    pos_col, doc_col = pos.reshape(WINDOW, 1), doc.reshape(WINDOW, 1)
    pos_row, doc_row = pos.reshape(6, 1, CHUNK), doc.reshape(6, 1, CHUNK)
    pieces = (tokens, before, after, other_tokens, other_before, other_after)
    q, k, v, xw, k_turned, x_turned = project(scal, pieces, weights, near, near_owner, spread, group)
    if fast:
        far = swap(near, "seq", 1)
        smalls = jnp.concatenate([near, far], axis=1)
        owner = jnp.concatenate([side * nf + near_owner, (1 - side) * nf + near_owner], axis=0)
        q, smalls = tie(q, smalls)
    ctx, inverses, *kept = attend(scal, pos_col, pos_row, doc_col, doc_row, q, k, v, table)
    ctx_other = swap(ctx, *SIDE)
    params_of = (smalls, owner, spread, group, wg)
    up = lambda i: feed_up(
        i, scal, xw, ctx, ctx_other, smalls, owner, near, near_owner,
        (spread, group, spread_up, group_up), wg,
    )
    down = lambda i, base, got, slope: feed_back(
        i, scal, base, got, cot, cot_other, slope, *params_of
    )
    close = lambda i, base, got, unit, rstd, sums: feed_close(
        i, scal, base, got, unit, rstd, sums, *params_of
    )
    up0 = up(0)
    got0 = swap(up0[4], *SIDE)
    up1, got0 = tie(up(1), got0)
    got1 = swap(up1[4], *SIDE)
    down0, got1 = tie(down(0, up0[3], got0, up0[6]), got1)
    got0 = swap(down0[4], *SIDE)
    down1, got0 = tie(down(1, up1[3], got1, up1[6]), got0)
    got1 = swap(down1[4], *SIDE)
    closed0 = close(0, down0[3], got0, up0[0], up0[1], down0[5] + down1[5])
    feed = weight_grads(
        scal, up0[5], down0[1], up0[2], down0[2], up1[5], down1[1], up1[2], down1[2]
    )
    closed0, feed, got1 = tie(closed0, feed, got1)
    if fast:
        feed_got = swap(by_core(feed[1]), *CORE)
    closed1 = close(1, down1[3], got1, up1[0], up1[1], closed0[3])
    if fast:
        closed1, feed_got = tie(closed1, feed_got)
        feed = sum_core(feed[0], feed_got)
        feed_got = swap(feed[1], *ALONG_Y)
    dh1, dattn, dctx = [[c[i] for c in (closed0, closed1)] for i in range(3)]
    sums = closed1[3]
    lay = jnp.where(side == 0, down0[0], down1[0])
    back = lambda first, pairs, before: attend_back(
        first, pairs, before, scal, q, k_turned, v, kept, x_turned, sums, ctx, dctx, dattn, inverses
    )
    outs = back(0, 3, ())
    if fast:
        outs, feed_got = tie(outs, feed_got)
        feed = add(feed[0][:2], feed_got[:2]), add(feed[0][2:], feed_got[2:])
        outs, feed = tie(outs, feed)
    dq, own, low, high, *parts = outs

    own_cols = lambda values, at, size: lax.dynamic_slice_in_dim(values, at * size, size, 1)
    if fast:
        feed_got = swap(feed[1], "fsdp", 4)
        part_got = swap(by_core(parts[1]), *CORE)
        table_got = swap(by_core(parts[3]), *CORE)
        part_got, table_got, feed_got = tie(part_got, table_got, feed_got)
        feed = add(feed[0][0], feed_got[0]), add(feed[0][1], feed_got[1])
        part, table_part = sum_core(parts[0], part_got), sum_core(parts[2], table_got)
        part, feed = tie(part, feed)
        part_got, feed_got = swap(part[1], *ALONG_Y), swap(feed[1], "fsdp", 8)
        part_got, feed_got, table_part, low, high = tie(
            part_got, feed_got, table_part, low, high
        )
        part_got = along_z(add(part[0], part_got))
        table_got = swap(table_part[1], *ALONG_Y)
        left, right = shifted(high, "fsdp", 1), shifted(low, "fsdp", -1)
        table_got, left, right = tie(table_got, left, right)
        table_got, left, right = tie(add(table_part[0], table_got), left, right)
        table_got = along_z(table_got)
        dx, dx_send = project_back(scal, (dq, own, left, right), dh1, weights)
        dx_got = swap(dx_send, *SIDE)
        shard = add(feed[0], feed_got)
        part = sum_z(part_got)
        table_total = sum_z(table_got)
        table_total = table_total.reshape(3, 2, 4, 32, 128).transpose(0, 1, 3, 2, 4)
        table_total = table_total.reshape(6, 32, MPOS).astype(F32)
        blocks = part.reshape(3, PART, 128)
        weight = blocks[:, :PART_TOTALS].reshape(3, 3, 2, rows, 128).transpose(1, 0, 2, 3, 4)
        mine = lax.dynamic_index_in_dim(weight, side, 2, False)
        sent = lax.dynamic_index_in_dim(weight, 1 - side, 2, False)
        sums = blocks[:, PART_SUMS:PART_OUT].reshape(6, 16, 128)
        sums = sums.transpose(1, 0, 2).reshape(16, D).astype(F32)
        outs = blocks[:, PART_OUT:].reshape(6, rows, 128)
        grad_w_out = outs.transpose(1, 0, 2).reshape(rows, D).astype(F32)
        got = swap(sent.reshape(-1, 128), *SIDE)
        got = got.reshape(3, 3, rows, 128)
        mine = mine.transpose(2, 0, 1, 3).reshape(rows, 3, 1, OWN)
        got = got.transpose(2, 0, 1, 3).reshape(rows, 3, 1, OWN)
        grad_w_qkv = in_order(side, mine, got, 2).reshape(rows, 3 * D).astype(F32)
        head_sums = blocks[:, PART_TOTALS : PART_TOTALS + 2].transpose(1, 0, 2).reshape(2, OWN)
        head_sums = head_sums.astype(F32)
        head_grads = own_cols(head_sums, place, wide_cols)
        grad_w_down = shard[:96].astype(F32)
        wide = shard[96:192].reshape(2, 2, rows, D).transpose(0, 2, 1, 3).reshape(2, rows, FF // 2)
        mine = lax.dynamic_index_in_dim(wide, side, 0, False)
        got = swap(lax.dynamic_index_in_dim(wide, 1 - side, 0, False), *SIDE)
        grad_w_up = in_order(side, mine, got, 1).astype(F32)
    else:
        scatter = partial(lax.psum_scatter, axis_name=BOTH, scatter_dimension=0, tiled=True)
        left, right = shifted(high, "fsdp", 1), shifted(low, "fsdp", -1)
        dx, dx_send = project_back(scal, (dq, own, left, right), dh1, weights)
        dx_got = swap(dx_send, "seq", 1)

        def plain(pair, at=lambda u: 4 * (u & 1) + (u >> 1)):
            both = jnp.stack(pair, axis=1)
            return jnp.stack([both[at(u)] for u in range(8)], axis=0)

        blocks = plain(parts[:2]).reshape(8, 2, 3, PART, 128)
        table_grad = plain(parts[2:]).reshape(8, 2, 3, 2, 4, 32, 128).transpose(2, 3, 0, 1, 5, 4, 6)
        table_total = lax.psum_scatter(
            table_grad.reshape(6, MPOS, MPOS), "fsdp", scatter_dimension=1, tiled=True
        ).astype(F32)
        head_rows = blocks[:, :, :, :PART_TOTALS].reshape(8, 2, 3, 3, 2, 24, 128)
        head_rows = head_rows.transpose(4, 0, 1, 5, 3, 2, 6).reshape(D, 3, 1, OWN)
        blank = jnp.zeros_like(head_rows)
        both = jnp.concatenate(
            [jnp.where(side == 0, head_rows, blank), jnp.where(side == 0, blank, head_rows)], axis=2
        )
        grad_w_qkv = scatter(both.reshape(D, 3 * D)).astype(F32)
        head_sums = blocks[0, 0, :, PART_TOTALS : PART_TOTALS + 2].transpose(1, 0, 2)
        head_sums = lax.psum(head_sums.reshape(2, OWN).astype(F32), "fsdp")
        head_grads = own_cols(head_sums, place, wide_cols)
        def placed(value, axis):
            blank = jnp.zeros_like(value)
            sides = [jnp.where(side == 0, value, blank), jnp.where(side == 0, blank, value)]
            return jnp.concatenate(sides, axis=axis)

        gg = plain(feed, lambda u: 4 * (u & 1) + (u & 2) + (u >> 2)).reshape(16, 192, D)
        grad_w_down = scatter(placed(gg[:, :96].reshape(FF // 2, D), 0)).astype(F32)
        up = gg[:, 96:192].reshape(16, 2, 2, 24, D).transpose(1, 0, 3, 2, 4).reshape(D, FF // 2)
        grad_w_up = scatter(placed(up, 1)).astype(F32)
        out = blocks[:, :, :, PART_OUT:].reshape(8, 2, 3, 2, 24, 128).transpose(0, 1, 4, 2, 3, 5)
        out = out.reshape(OWN, D)
        grad_w_out = scatter(placed(out, 0)).astype(F32)
        sums = lax.psum(sums, "fsdp")
    ours = own_cols(sums[:6], side * nf + place, wide_cols)
    grad_biases = jnp.concatenate([head_grads, ours[:4]], axis=0)
    grad_gains = ours[4:]
    grad_bias_up = lax.dynamic_slice_in_dim(
        sums[8:10].reshape(-1), place * up_cols, up_cols, 0
    )
    input_grad = dx + dx_got.astype(F32)
    mask_logit_gradient = (
        table_total * relaxed * (1.0 - relaxed) / softening_scale[:, None, None]
    )
    return (
        lay.reshape(1, HALF, D),
        input_grad.reshape(1, HALF, D),
        grad_w_qkv,
        grad_w_out,
        grad_w_up,
        grad_w_down,
        grad_biases,
        grad_gains,
        grad_bias_up,
        mask_logit_gradient,
    )


def solution(mesh):
    rows = P(("seq", "fsdp"), None)
    columns = P(None, ("seq", "fsdp"))
    block = P("fsdp", "seq", None)
    table = P("seq", "fsdp", None)
    return jax.shard_map(
        per_device,
        mesh=mesh,
        in_specs=(
            block, rows, rows, rows, rows, columns, columns, P(("seq", "fsdp")),
            table, table, P("seq"), P(), block,
        ),
        out_specs=(
            block, block, rows, rows, rows, rows, columns, columns, P(("seq", "fsdp")), table,
        ),
        check_vma=False,
    )
```

```python
from functools import partial

import jax
import jax.numpy as jnp
from jax import lax
from jax.experimental import pallas as pl
from jax.experimental.pallas import tpu as pltpu
from jax.sharding import PartitionSpec as P

D = 768
FF = 3072
HEADS = 12
HDIM = 64
MPOS = 512
EPS = 1e-05
GROUP = 512
HALF = 256
WINDOW = 3 * GROUP
OWN = 384
CHUNK = 256
NEG = -1e30
BF = jnp.bfloat16
F32 = jnp.float32
HIGH = lax.Precision.HIGHEST
PART_SUMS = 144
PART_TOTALS = PART_SUMS + 6
PART_OUT = 176
PART = 224
PART_TABLE = 256


def nn(left, right):
    return jnp.dot(left, right, preferred_element_type=F32)


def nt(left, right, precision=None):
    return lax.dot_general(
        left, right, (((1,), (1,)), ((), ())), precision=precision, preferred_element_type=F32
    )


def tn(left, right):
    return lax.dot_general(left, right, (((0,), (0,)), ((), ())), preferred_element_type=F32)


def load_projection(gathered, w, sem):
    copies = []
    for f in range(16):
        row = (f % 2) * OWN + (f // 2) * 48
        copies.append(
            pltpu.make_async_copy(gathered.at[f, 16:25], w.at[:, row : row + 48, :], sem.at[f])
        )
    for copy in copies:
        copy.start()
    return copies


def table_of(table, head):
    return jnp.concatenate(
        [table[:, 4 * head + part].reshape(MPOS, 128) for part in range(4)], axis=1
    )


def spread_out(values, spread, owner, group):
    return jnp.sum(jnp.where(owner == group, nn(values, spread), 0.0), axis=0, keepdims=True)


def columns_of(w, first, count=3):
    return jnp.concatenate([w[first + part] for part in range(count)], axis=1)


def place_of(t, cr, scal):
    unit = ((t >> 2) ^ (scal[0] & 1)) | ((t & 3) << 1)
    return 2 * unit + (scal[1] ^ cr)


def near_place_of(t, cr, scal):
    unit = ((t >> 2) | (t & 2) | ((t & 1) << 2)) ^ scal[0]
    return 2 * unit + (scal[1] ^ cr)


def project_kernel(
    scal,
    x1,
    x0,
    x2,
    y1,
    y0,
    y2,
    gathered,
    near,
    owner,
    spread,
    group,
    q_ref,
    k_ref,
    v_ref,
    xw,
    k_turned,
    x_turned,
    w,
    sem,
):
    copies = load_projection(gathered, w, sem)
    side = scal[2]
    for g, (mine, other) in enumerate(((x0, y0), (x1, y1), (x2, y2))):
        xw[pl.ds(pl.multiple_of(g * GROUP + side * HALF, HALF), HALF), :] = mine[...]
        xw[pl.ds(pl.multiple_of(g * GROUP + (1 - side) * HALF, HALF), HALF), :] = other[...]
    bias = [
        spread_out(near[i], spread[:, :OWN], owner[...], group[:, :OWN]) for i in range(2)
    ]
    for copy in copies:
        copy.wait()
    for blk in range(6):
        rows = slice(blk * HALF, (blk + 1) * HALF)
        here = xw[rows, :]
        key = nn(here, columns_of(w, 3))
        k_ref[rows, :] = key.astype(BF)
        k_turned[blk] = key.T.astype(BF)
        x_turned[:, rows] = here.astype(F32).T.astype(BF)
        v_ref[rows, :] = (nn(here, columns_of(w, 6)) + bias[1]).astype(BF)
        if blk in (2, 3):
            local = slice((blk - 2) * HALF, (blk - 1) * HALF)
            query = (nn(here, columns_of(w, 0)) + bias[0]).astype(BF)
            q_ref[local, :] = query * jnp.asarray(0.125, BF)


def head_lanes():
    return lax.broadcasted_iota(jnp.int32, (1, 128), 1) < HDIM


def fill_hot(pos_col, hot):
    for blk in range(6):
        rows = slice(blk * 256, (blk + 1) * 256)
        column = lax.broadcasted_iota(jnp.int32, (256, MPOS), 1)
        hot[rows, :] = jnp.where(pos_col[rows, :] == column, 1.0, 0.0).astype(BF)


def fill_hot_turned(pos_row, hot):
    for blk in range(6):
        rows = lax.broadcasted_iota(jnp.int32, (MPOS, 256), 0)
        hot[blk] = jnp.where(pos_row[blk] == rows, 1.0, 0.0).astype(BF)


def set_pair(low, value, target):
    blank = jnp.zeros_like(value)
    target[:HALF, :] = jnp.where(low, value, blank)
    target[HALF:, :] = jnp.where(low, blank, value)


def fold(values, how):
    rows, columns = values.shape
    return how(values.reshape(rows // 8, 8, columns), axis=0)


def attend_kernel(
    scal,
    pos_col,
    pos_row,
    doc_col,
    doc_row,
    q,
    k,
    v,
    table,
    ctx,
    inverses,
    weights,
    mixes,
    hot_turned,
    hot,
    sbuf,
    looks,
    queries,
    acc,
):
    @pl.when(pl.program_id(0) == 0)
    def _():
        fill_hot(pos_col, hot)
        fill_hot_turned(pos_row, hot_turned)

    low = head_lanes()
    for qb in range(2):
        lo, hi = scal[3 + 2 * qb], scal[4 + 2 * qb]
        here = slice(qb * HALF, (qb + 1) * HALF)
        set_pair(low, q[here, :], queries)
        q_doc = jnp.concatenate([doc_row[2 + qb]] * 2, axis=1)
        q_hot = hot[GROUP + qb * HALF : GROUP + (qb + 1) * HALF, :]
        for h in range(2):
            looks[h * HALF : (h + 1) * HALF, :] = nn(q_hot, table_of(table, h)).astype(BF)

        def score_step(c, top, q_doc=q_doc):
            rows = pl.ds(pl.multiple_of(c * CHUNK, CHUNK), CHUNK)
            s = jnp.where(doc_col[rows, :] == q_doc, nt(k[rows, :], queries[...]), NEG)
            sbuf[c] = s
            return jnp.maximum(top, fold(s, jnp.max))

        top = lax.fori_loop(lo, hi, score_step, jnp.full((8, 2 * HALF), NEG, F32))
        top = jnp.max(top, axis=0, keepdims=True)
        acc[...] = jnp.zeros_like(acc)

        def mix_step(c, total, top=top, qb=qb):
            rows = pl.ds(pl.multiple_of(c * CHUNK, CHUNK), CHUNK)
            e = jnp.exp(sbuf[c] - top)
            mixed = (e * nt(hot[rows, :], looks[...])).astype(BF)
            weights[0, qb, c] = e.astype(BF)
            mixes[0, qb, c] = mixed
            acc[...] += tn(mixed, v[rows, :])
            return total + fold(e, jnp.sum)

        total = lax.fori_loop(lo, hi, mix_step, jnp.zeros((8, 2 * HALF), F32))
        total = jnp.sum(total, axis=0, keepdims=True)
        inverse = 1.0 / total
        inverses[0, 0:1, here] = inverse[:, :HALF]
        inverses[0, 1:2, here] = inverse[:, HALF:]
        inverses[0, 2:8, here] = jnp.zeros((6, HALF), F32)
        scale = jnp.concatenate(
            [
                jnp.broadcast_to(inverse[:, :HALF], (HDIM, HALF)),
                jnp.broadcast_to(inverse[:, HALF:], (HDIM, HALF)),
            ],
            axis=0,
        ).T
        ctx[qb] = (jnp.where(low, acc[:HALF, :], acc[HALF:, :]) * scale).astype(BF)


def attend_back_kernel(
    carried,
    scal,
    q,
    k,
    v,
    weights,
    mixes,
    hot_turned,
    xw,
    sums,
    ctx,
    ctx_all,
    dctx0,
    dctx1,
    dattn0,
    dattn1,
    inverses,
    *refs,
):
    outs = refs[carried : carried + 8]
    dq, own, halo_low, halo_high, part_keep, part_send, table_keep, table_send = outs
    queries, grads, dk, dv, dq_acc, tt, tg, gw, gout = refs[carried + 8 :]
    low = head_lanes()
    dk[...] = jnp.zeros_like(dk)
    dv[...] = jnp.zeros_like(dv)
    lane = lax.broadcasted_iota(jnp.int32, (8, 128), 1)
    row8 = lax.broadcasted_iota(jnp.int32, (8, 128), 0)
    pick = jnp.where((lane < HDIM) == (row8 == 0), 1.0, 0.0)
    for qb in range(2):
        lo, hi = scal[3 + 2 * qb], scal[4 + 2 * qb]
        here = slice(qb * HALF, (qb + 1) * HALF)
        inverse = inverses[0, 0:2, here]
        d_pair = (dctx0, dctx1)[qb][...].astype(F32)
        deltas = nt(pick, d_pair * ctx[qb].astype(F32), HIGH)[0:2, :] * inverse
        delta = jnp.concatenate([deltas[0:1, :], deltas[1:2, :]], axis=1)
        scale = jnp.concatenate(
            [
                jnp.broadcast_to(inverse[0:1, :], (HDIM, HALF)),
                jnp.broadcast_to(inverse[1:2, :], (HDIM, HALF)),
            ],
            axis=0,
        ).T
        set_pair(low, q[here, :], queries)
        set_pair(low, (d_pair * scale).astype(BF), grads)
        dq_acc[...] = jnp.zeros_like(dq_acc)
        tt[...] = jnp.zeros_like(tt)

        def step(c, carry, delta=delta, qb=qb):
            rows = pl.ds(pl.multiple_of(c * CHUNK, CHUNK), CHUNK)
            mixed = mixes[0, qb, c]
            e = weights[0, qb, c].astype(F32)
            dm = nt(v[rows, :], grads[...])
            ds = (mixed.astype(F32) * dm - e * delta).astype(BF)
            dv[rows, :] += nn(mixed, grads[...])
            dk[rows, :] += nn(ds, queries[...])
            dq_acc[...] += nn(k[c], ds)
            tt[...] += nn(hot_turned[c], (e * dm).astype(BF))
            return carry

        lax.fori_loop(lo, hi, step, 0)
        for h in range(2):
            piece = nt(hot_turned[2 + qb], tt[:, h * HALF : (h + 1) * HALF].astype(BF))
            if qb == 0:
                tg[h] = piece
            else:
                tg[h] += piece
        both = jnp.concatenate([dq_acc[:HDIM, :HALF], dq_acc[HDIM:, HALF:]], axis=0)
        dq[here, :] = (both.T * 0.125).astype(BF)
    own[0] = dk[GROUP : 2 * GROUP, :]
    own[1] = dv[GROUP : 2 * GROUP, :]
    halo_low[0] = dk[:GROUP, :].astype(BF)
    halo_low[1] = dv[:GROUP, :].astype(BF)
    halo_high[0] = dk[2 * GROUP :, :].astype(BF)
    halo_high[1] = dv[2 * GROUP :, :].astype(BF)
    query_grad = dq[...]
    pair_grad = jnp.concatenate([dk[...].astype(BF), dv[...].astype(BF)], axis=1)
    gw[:, 0:128] = nn(xw[:, GROUP : 2 * GROUP], query_grad)
    gw[:, 128:384] = nn(xw[...], pair_grad)
    gout[...] = tn(ctx_all[0], dattn0[...]) + tn(ctx_all[1], dattn1[...])
    totals = jnp.concatenate(
        [
            sums[0:6, 0:128],
            column_sum(query_grad.astype(F32)),
            column_sum(pair_grad[:, 128:].astype(F32)),
            sums[8:16, 0:128],
            sums[:, 128:256],
        ],
        axis=0,
    ).astype(BF)
    for cr in range(2):
        out, table = (part_keep, table_keep) if cr == 0 else (part_send, table_send)
        for t in range(8):
            place = place_of(t, cr, scal)
            rows = [
                gw[pl.ds(pl.multiple_of(part * OWN + place * 24, 8), 24), :] for part in range(2)
            ]
            both = jnp.concatenate(rows, axis=0).astype(BF)
            for i in range(3):
                out[t, i * 48 : i * 48 + 48, :] = both[:, i * 128 : (i + 1) * 128]
            out[t, PART_SUMS:PART_OUT, :] = totals
            rows = gout[pl.ds(pl.multiple_of(place * 24, 8), 24), :]
            out[t, PART_OUT:PART, :] = jnp.concatenate(
                [rows[:, 0:128], rows[:, 128:256]], axis=0
            ).astype(BF)
            for h in range(2):
                mask = tg[h, pl.ds(pl.multiple_of(place * 32, 32), 32), :].astype(BF)
                for i in range(4):
                    at = (4 * h + i) * 32
                    table[t, at : at + 32, :] = mask[:, i * 128 : (i + 1) * 128]


def norm_stats(values):
    center = values - jnp.mean(values, axis=-1, keepdims=True)
    rstd = lax.rsqrt(jnp.mean(center * center, axis=-1, keepdims=True) + EPS)
    return center * rstd, rstd


def norm_back(grad, unit, rstd, gain):
    scaled = grad * gain
    return rstd * (
        scaled
        - jnp.mean(scaled, axis=-1, keepdims=True)
        - unit * jnp.mean(scaled * unit, axis=-1, keepdims=True)
    )


def column_sum(values):
    return jnp.sum(values, axis=0, keepdims=True)


def load_feed(wg, sem, wm=None, wu=None, wd=None):
    copies = []

    def bring(source, target):
        copies.append(pltpu.make_async_copy(source, target, sem.at[len(copies)]))
        copies[-1].start()

    for c in range(2):
        for s in range(2):
            if wm is not None:
                bring(
                    wg.at[:, c, 192:240, s * OWN : (s + 1) * OWN],
                    wm.at[s, :, :, c * OWN : (c + 1) * OWN],
                )
    for c in range(2):
        for s in range(2):
            if wu is not None:
                bring(wg.at[:, c, 96 + 48 * s : 144 + 48 * s, :], wu.at[c, s])
    for c in range(2):
        if wd is not None:
            bring(wg.at[:, c, 0:96, :], wd.at[:, c])
    return copies


def shrink_rows(wd, i):
    return wd[pl.ds(4 * i, 4)].reshape(D, D)


def wait_for(copies):
    for copy in copies:
        copy.wait()


def feed_up_kernel(
    scal,
    x,
    ctx_mine,
    ctx_other,
    smalls,
    owner,
    near,
    near_owner,
    spread,
    group,
    spread_up,
    group_up,
    wg,
    unit1,
    rstd1,
    nlow,
    base,
    send,
    act,
    slope,
    wm,
    wu,
    wd,
    ctxt,
    bup,
    sem,
):
    copies = load_feed(wg, sem, wm, wu, wd)
    vector = lambda i: spread_out(smalls[i], spread[...], owner[...], group[...])
    bias_out, bias_down, shift1, gain1 = [vector(i) for i in (2, 3, 4, 6)]
    for n in range(2):
        bup[n] = spread_out(
            near[8], spread_up[...], near_owner[...], group_up[...] + n * (near.shape[1] // 2)
        )
    even = scal[2] == 0
    mine, other = ctx_mine[0], ctx_other[0]
    ctxt[:, :OWN] = jnp.where(even, mine, other)
    ctxt[:, OWN:] = jnp.where(even, other, mine)
    wait_for(copies[:4])
    attn = nn(ctxt[...], wm[...].reshape(D, D)) + bias_out
    unit, rstd = norm_stats(x[...].astype(F32) + attn)
    unit1[...] = unit
    rstd1[...] = jnp.broadcast_to(rstd, (HALF, 128))
    normed = unit * gain1 + shift1
    nlow[...] = normed.astype(BF)
    base[...] = normed + bias_down
    wait_for(copies[4:8])

    def widen(n, carry):
        up = nn(nlow[...], wu[n].reshape(D, D)) + bup[n]
        half_cdf = 0.5 * (1.0 + lax.erf(up * 0.7071067811865476))
        act[n] = (up * half_cdf).astype(BF)
        slope[n] = half_cdf + up * (0.3989422804014327 * jnp.exp(-0.5 * up * up))
        return carry

    lax.fori_loop(0, 2, widen, 0)
    wait_for(copies[8:])
    part = nn(act[0], shrink_rows(wd, 0)) + nn(act[1], shrink_rows(wd, 1))
    base[...] += part
    send[...] = part.astype(BF)


def feed_back_kernel(
    index,
    scal,
    base,
    got,
    cot_mine,
    cot_other,
    slope,
    smalls,
    owner,
    spread,
    group,
    wg,
    lay,
    ddown,
    dup,
    base2,
    send,
    sums,
    wu,
    wd,
    sem,
):
    copies = load_feed(wg, sem, None, wu, wd)
    vector = lambda i: spread_out(smalls[i], spread[...], owner[...], group[...])
    shift2, gain2 = vector(5), vector(7)
    sums[...] = jnp.zeros_like(sums)
    unit, rstd = norm_stats(base[...] + got[...].astype(F32))
    lay[...] = (unit * gain2 + shift2).astype(BF)
    dy = jnp.where(scal[2] == index, cot_mine[...], cot_other[...]).astype(F32)
    sums[3:4, :] = column_sum(dy)
    sums[5:6, :] = column_sum(dy * unit)
    grad = norm_back(dy, unit, rstd, gain2)
    ddown[...] = grad.astype(BF)
    sums[1:2, :] = column_sum(ddown[...].astype(F32))
    base2[...] = grad
    wait_for(copies)

    def back(n, carry):
        low = (nt(ddown[...], shrink_rows(wd, n)) * slope[n]).astype(BF)
        dup[n] = low
        sums[pl.ds(8 + n, 1), :] = column_sum(low.astype(F32))
        return carry

    lax.fori_loop(0, 2, back, 0)
    part = nt(dup[0], wu[0].reshape(D, D)) + nt(dup[1], wu[1].reshape(D, D))
    base2[...] += part
    send[...] = part.astype(BF)


def feed_close_kernel(
    scal,
    base,
    got,
    unit1,
    rstd1,
    sums_in,
    smalls,
    owner,
    spread,
    group,
    wg,
    dh1,
    dattn,
    dctx,
    sums,
    wm,
    sem,
):
    copies = load_feed(wg, sem, wm)
    gain1 = spread_out(smalls[6], spread[...], owner[...], group[...])
    sums[...] = sums_in[...]
    grad = base[...] + got[...].astype(F32)
    unit = unit1[...]
    sums[2:3, :] += column_sum(grad)
    sums[4:5, :] += column_sum(grad * unit)
    grad = norm_back(grad, unit, rstd1[:, 0:1], gain1)
    dh1[...] = grad
    dattn[...] = grad.astype(BF)
    sums[0:1, :] += column_sum(dattn[...].astype(F32))
    wait_for(copies)
    dctx[...] = nt(dattn[...], wm[scal[2]].reshape(OWN, D)).astype(BF)


def weight_grad_kernel(
    scal, act0, ddown0, nlow0, dup0, act1, ddown1, nlow1, dup1, keep, send, down, up
):
    for n in range(2):
        up[n] = tn(nlow0[...], dup0[n]) + tn(nlow1[...], dup1[n])
        down[n * D : (n + 1) * D, :] = tn(act0[n], ddown0[...]) + tn(act1[n], ddown1[...])
    for cr, out in enumerate((keep, send)):
        for t in range(8):
            place = near_place_of(t, cr, scal)
            out[t, 0:96, :] = down[pl.ds(pl.multiple_of(place * 96, 8), 96), :].astype(BF)
            parts = [
                up[n, pl.ds(pl.multiple_of(s * OWN + place * 24, 8), 24), :]
                for s in range(2)
                for n in range(2)
            ]
            out[t, 96:192, :] = jnp.concatenate(parts, axis=0).astype(BF)


def project_back_kernel(scal, parts, dh1s, gathered, dx, dx_send, w, dqkv, sem):
    copies = load_projection(gathered, w, sem)
    dq, own, left, right = parts
    dqkv[:, :OWN] = dq[...]
    for i in range(2):
        total = own[i] + left[i].astype(F32) + right[i].astype(F32)
        dqkv[:, (1 + i) * OWN : (2 + i) * OWN] = total.astype(BF)
    for copy in copies:
        copy.wait()
    side = scal[2]
    mine = dqkv[pl.ds(pl.multiple_of(side * HALF, HALF), HALF), :]
    other = dqkv[pl.ds(pl.multiple_of((1 - side) * HALF, HALF), HALF), :]
    for part in range(3):
        cols = slice(part * 256, (part + 1) * 256)
        rows = jnp.concatenate([w[j, cols, :] for j in range(9)], axis=1)
        dh1 = jnp.where(side == 0, dh1s[0][:, cols], dh1s[1][:, cols])
        dx[:, cols] = dh1 + nt(mine, rows)
        dx_send[:, cols] = nt(other, rows).astype(BF)


SMEM = pl.BlockSpec(memory_space=pltpu.SMEM)
VM = pl.BlockSpec()
HBM = pl.BlockSpec(memory_space=pl.ANY)


def params():
    return pltpu.CompilerParams(vmem_limit_bytes=60 * 1024 * 1024)


def cost(microseconds):
    return pl.CostEstimate(
        flops=int(microseconds * 1.15e9), bytes_accessed=1000, transcendentals=0
    )


def shape(dims, kind):
    return jax.ShapeDtypeStruct(dims, kind)


def project(scal, pieces, gathered, near, owner, spread, group):
    return pl.pallas_call(
        project_kernel,
        name="project",
        out_shape=(
            shape((GROUP, OWN), BF),
            shape((WINDOW, OWN), BF),
            shape((WINDOW, OWN), BF),
            shape((WINDOW, D), BF),
            shape((6, OWN, CHUNK), BF),
            shape((D, WINDOW), BF),
        ),
        in_specs=[SMEM] + [VM] * 6 + [HBM] + [VM] * 4,
        out_specs=[VM] * 6,
        scratch_shapes=[
            pltpu.VMEM((9, D, 128), BF),
            pltpu.SemaphoreType.DMA((16,)),
        ],
        compiler_params=params(),
        cost_estimate=cost(9),
    )(scal, *pieces, gathered, near, owner, spread, group)


def whole(*dims):
    return pl.BlockSpec(dims, lambda p: (0,) * len(dims))


def attend(scal, pos_col, pos_row, doc_col, doc_row, q, k, v, table):
    return pl.pallas_call(
        attend_kernel,
        name="attend",
        grid=(3,),
        out_shape=(
            shape((2, HALF, OWN), BF),
            shape((3, 8, GROUP), F32),
            shape((3, 2, 6, CHUNK, 2 * HALF), BF),
            shape((3, 2, 6, CHUNK, 2 * HALF), BF),
            shape((6, MPOS, CHUNK), BF),
        ),
        in_specs=[
            SMEM,
            whole(WINDOW, 1),
            whole(6, 1, CHUNK),
            whole(WINDOW, 1),
            whole(6, 1, CHUNK),
            pl.BlockSpec((GROUP, 128), lambda p: (0, p)),
            pl.BlockSpec((WINDOW, 128), lambda p: (0, p)),
            pl.BlockSpec((WINDOW, 128), lambda p: (0, p)),
            pl.BlockSpec((16, 8, 32, 128), lambda p: (0, p, 0, 0)),
        ],
        out_specs=[
            pl.BlockSpec((2, HALF, 128), lambda p: (0, 0, p)),
            pl.BlockSpec((1, 8, GROUP), lambda p: (p, 0, 0)),
            pl.BlockSpec((1, 2, 6, CHUNK, 2 * HALF), lambda p: (p, 0, 0, 0, 0)),
            pl.BlockSpec((1, 2, 6, CHUNK, 2 * HALF), lambda p: (p, 0, 0, 0, 0)),
            whole(6, MPOS, CHUNK),
        ],
        scratch_shapes=[
            pltpu.VMEM((WINDOW, MPOS), BF),
            pltpu.VMEM((6, CHUNK, 2 * HALF), F32),
            pltpu.VMEM((2 * HALF, MPOS), BF),
            pltpu.VMEM((2 * HALF, 128), BF),
            pltpu.VMEM((2 * HALF, 128), F32),
        ],
        compiler_params=params(),
        cost_estimate=cost(26),
    )(scal, pos_col, pos_row, doc_col, doc_row, q, k, v, table)


def attend_back(
    first, pairs, before, scal, q, k, v, kept, xw, sums, ctx, dctx, dattn, inverses
):
    columns = lambda rows: pl.BlockSpec((rows, 128), lambda p: (0, first + p))
    tiles = pl.BlockSpec((1, 2, 6, CHUNK, 2 * HALF), lambda p: (first + p, 0, 0, 0, 0))
    blocks = lambda rows: pl.BlockSpec((8, rows, 128), lambda p: (0, first + p, 0))
    both = pl.BlockSpec((2, GROUP, 128), lambda p: (0, 0, first + p))
    return pl.pallas_call(
        partial(attend_back_kernel, len(before)),
        name=f"attend_back_{first}",
        grid=(pairs,),
        input_output_aliases={16 + i: i for i in range(len(before))},
        out_shape=(
            shape((GROUP, OWN), BF),
            shape((2, GROUP, OWN), F32),
            shape((2, GROUP, OWN), BF),
            shape((2, GROUP, OWN), BF),
            shape((8, 3 * PART, 128), BF),
            shape((8, 3 * PART, 128), BF),
            shape((8, 3 * PART_TABLE, 128), BF),
            shape((8, 3 * PART_TABLE, 128), BF),
        ),
        in_specs=[
            SMEM,
            columns(GROUP),
            pl.BlockSpec((6, 128, CHUNK), lambda p: (0, first + p, 0)),
            columns(WINDOW),
            tiles,
            tiles,
            whole(6, MPOS, CHUNK),
            whole(D, WINDOW),
            pl.BlockSpec((16, 256), lambda p: (0, first + p)),
            pl.BlockSpec((2, HALF, 128), lambda p: (0, 0, first + p)),
            whole(2, HALF, OWN),
            columns(HALF),
            columns(HALF),
            pl.BlockSpec((HALF, 256), lambda p: (0, first + p)),
            pl.BlockSpec((HALF, 256), lambda p: (0, first + p)),
            pl.BlockSpec((1, 8, GROUP), lambda p: (first + p, 0, 0)),
        ]
        + [HBM] * len(before),
        out_specs=[
            columns(GROUP),
            both,
            both,
            both,
            blocks(PART),
            blocks(PART),
            blocks(PART_TABLE),
            blocks(PART_TABLE),
        ],
        scratch_shapes=[
            pltpu.VMEM((2 * HALF, 128), BF),
            pltpu.VMEM((2 * HALF, 128), BF),
            pltpu.VMEM((WINDOW, 128), F32),
            pltpu.VMEM((WINDOW, 128), F32),
            pltpu.VMEM((128, 2 * HALF), F32),
            pltpu.VMEM((MPOS, 2 * HALF), F32),
            pltpu.VMEM((2, MPOS, MPOS), F32),
            pltpu.VMEM((D, OWN), F32),
            pltpu.VMEM((OWN, 256), F32),
        ],
        compiler_params=params(),
        cost_estimate=cost(10 * pairs),
    )(scal, q, k, v, *kept, xw, sums, ctx, ctx, *dctx, *dattn, inverses, *before)


WIDEN = pltpu.VMEM((2, 2, 8, 48, D), BF)
SHRINK = pltpu.VMEM((8, 2, 96, D), BF)
MERGE = pltpu.VMEM((2, 8, 48, D), BF)


def feed_up(index, scal, xw, mine, other, smalls, owner, near, near_owner, spreads, wg):
    arrays = (smalls, owner, near, near_owner, *spreads)
    ctx = pl.BlockSpec((1, HALF, OWN), lambda p: (index, 0, 0))
    outs = (
        shape((HALF, D), F32),
        shape((HALF, 128), F32),
        shape((HALF, D), BF),
        shape((HALF, D), F32),
        shape((HALF, D), BF),
        shape((2, HALF, D), BF),
        shape((2, HALF, D), F32),
    )
    return pl.pallas_call(
        feed_up_kernel,
        name=f"feed_up_{index}",
        grid=(1,),
        out_shape=outs,
        in_specs=[SMEM, pl.BlockSpec((HALF, D), lambda p: (2 + index, 0)), ctx, ctx]
        + [whole(*a.shape) for a in arrays]
        + [HBM],
        out_specs=[whole(*out.shape) for out in outs],
        scratch_shapes=[
            MERGE,
            WIDEN,
            SHRINK,
            pltpu.VMEM((HALF, D), BF),
            pltpu.VMEM((2, 1, D), F32),
            pltpu.SemaphoreType.DMA((10,)),
        ],
        compiler_params=params(),
        cost_estimate=cost(8),
    )(scal, xw, mine, other, *arrays, wg)


def feed_back(index, scal, base, got, cot, cot_other, slope, smalls, owner, spread, group, wg):
    return pl.pallas_call(
        partial(feed_back_kernel, index),
        name=f"feed_back_{index}",
        out_shape=(
            shape((HALF, D), BF),
            shape((HALF, D), BF),
            shape((2, HALF, D), BF),
            shape((HALF, D), F32),
            shape((HALF, D), BF),
            shape((16, D), F32),
        ),
        in_specs=[SMEM] + [VM] * 9 + [HBM],
        out_specs=[VM] * 6,
        scratch_shapes=[WIDEN, SHRINK, pltpu.SemaphoreType.DMA((6,))],
        compiler_params=params(),
        cost_estimate=cost(7),
    )(scal, base, got, cot, cot_other, slope, smalls, owner, spread, group, wg)


def feed_close(index, scal, base, got, unit1, rstd1, sums, smalls, owner, spread, group, wg):
    return pl.pallas_call(
        feed_close_kernel,
        name=f"feed_close_{index}",
        out_shape=(
            shape((HALF, D), F32),
            shape((HALF, D), BF),
            shape((HALF, OWN), BF),
            shape((16, D), F32),
        ),
        in_specs=[SMEM] + [VM] * 9 + [HBM],
        out_specs=[VM] * 4,
        scratch_shapes=[MERGE, pltpu.SemaphoreType.DMA((4,))],
        compiler_params=params(),
        cost_estimate=cost(4),
    )(scal, base, got, unit1, rstd1, sums, smalls, owner, spread, group, wg)


def weight_grads(scal, *halves):
    return pl.pallas_call(
        weight_grad_kernel,
        name="weight_grads",
        out_shape=(shape((8, 192, D), BF), shape((8, 192, D), BF)),
        in_specs=[SMEM] + [VM] * 8,
        out_specs=[VM] * 2,
        scratch_shapes=[pltpu.VMEM((2 * D, D), F32), pltpu.VMEM((2, D, D), F32)],
        compiler_params=params(),
        cost_estimate=cost(7),
    )(scal, *halves)


def project_back(scal, parts, dh1, gathered):
    def kernel(scal, *refs):
        project_back_kernel(scal, refs[:4], refs[4:6], *refs[6:])

    return pl.pallas_call(
        kernel,
        name="project_back",
        out_shape=(shape((HALF, D), F32), shape((HALF, D), BF)),
        in_specs=[SMEM] + [VM] * 6 + [HBM],
        out_specs=[VM] * 2,
        scratch_shapes=[
            pltpu.VMEM((9, D, 128), BF),
            pltpu.VMEM((GROUP, 3 * OWN), BF),
            pltpu.SemaphoreType.DMA((16,)),
        ],
        compiler_params=params(),
        cost_estimate=cost(6),
    )(scal, *parts, *dh1, gathered)


def swap(value, axis, bit):
    count = lax.axis_size(axis)
    return lax.ppermute(value, axis, [(i, i ^ bit) for i in range(count)])


def shifted(value, axis, steps):
    count = lax.axis_size(axis)
    leading, last = (max(0, -steps), min(count, count - steps))
    return lax.ppermute(value, axis, [(source, source + steps) for source in range(leading, last)])


def tie(*values):
    return lax.optimization_barrier(values)


CORE, ALONG_Y, SIDE = ("fsdp", 1), ("fsdp", 2), ("seq", 1)


def along_z(values):
    groups = [[4 * z + i for z in range(4)] for i in range(4)]
    return lax.all_to_all(values, "fsdp", 0, 0, axis_index_groups=groups, tiled=True)


def add(mine, got):
    return (mine.astype(F32) + got.astype(F32)).astype(mine.dtype)


def by_core(value):
    return value.reshape(2, 4, *value.shape[1:])


def sum_core(keep, got):
    keep = by_core(keep)
    return add(keep[0], got[0]), add(keep[1], got[1])


def sum_z(got):
    return jnp.sum(got.astype(F32), axis=0).astype(got.dtype)


def in_order(flag, mine, other, axis):
    first = jnp.where(flag == 0, mine, other)
    second = jnp.where(flag == 0, other, mine)
    return jnp.concatenate([first, second], axis=axis)


def locate(index, opening, finish, stream_rows):
    document = jnp.sum((finish[None, :] <= index[:, None]).astype(jnp.int32), axis=1)
    begin = jnp.max(jnp.where(opening[None, :] <= index[:, None], opening[None, :], 0), axis=1)
    inside = (index >= 0) & (index < stream_rows)
    document = jnp.where(inside, document, -1)
    position = (index - begin) % MPOS
    return document, position


def own_columns(weight, nf, side, place):
    rows = weight.shape[0]
    weight = weight.reshape(rows, 3, 2, OWN)
    core = place % 2
    keep = lax.dynamic_index_in_dim(weight, side, 2, False).reshape(rows, 3 * OWN)
    give = lax.dynamic_index_in_dim(weight, 1 - side, 2, False).reshape(rows, 3 * OWN)
    straight, crossed, near = [], [], []
    for s in range(2):
        for f in range(nf):
            here = s * nf + f
            if f % 2 == s:
                straight.append((here, (1 - s) * nf + f))
            else:
                crossed.append((here, (1 - s) * nf + (f ^ 1)))
                near.append((here, s * nf + (f ^ 1)))
    axes = ("seq", "fsdp")
    same = core == side
    mine = jnp.where(same, keep, lax.ppermute(give, axes, straight))
    other = jnp.where(same, lax.ppermute(keep, axes, near), lax.ppermute(give, axes, crossed))
    return in_order(core, mine, other, 0)


def per_device(
    incoming_state,
    projection_matrix_triple,
    merge_matrix,
    widen_matrix,
    shrink_matrix,
    offset_table,
    norm_scales,
    widen_offset,
    trainable_gate_scores,
    gate_perturbation,
    softening_scale,
    passage_extents,
    result_cotangent,
):
    BOTH = ("seq", "fsdp")
    ns, nf = lax.axis_size("seq"), lax.axis_size("fsdp")
    count = ns * nf
    fast = nf == 16
    side, place = lax.axis_index("seq"), lax.axis_index("fsdp")
    tokens = incoming_state.reshape(HALF, D)
    cot = result_cotangent.reshape(HALF, D)
    stream_rows = GROUP * nf
    rows = projection_matrix_triple.shape[0]
    zero = jnp.zeros((), jnp.int32)
    core, unit = (place % 2, place // 2) if fast else (zero, zero)

    relaxed = jax.nn.sigmoid(
        (trainable_gate_scores + gate_perturbation) / softening_scale[:, None, None]
    )
    relaxed_low = relaxed.astype(BF)
    wide_cols, up_cols = D // count, FF // count
    pad_to = lambda value: jnp.pad(value, ((0, 0), (0, 128 - value.shape[1])))
    packed = jnp.concatenate(
        [
            pad_to(offset_table),
            pad_to(norm_scales),
            pad_to(widen_offset.reshape(1, up_cols)),
            jnp.zeros((7, 128), BF),
        ],
        axis=0,
    )
    lane, row = jnp.arange(D, dtype=jnp.int32)[None, :], jnp.arange(128, dtype=jnp.int32)[:, None]
    spread, group = (lane % wide_cols == row).astype(BF), lane // wide_cols
    spread_up, group_up = (lane % up_cols == row).astype(BF), lane // up_cols

    finish = jnp.cumsum(passage_extents)
    opening = finish - passage_extents
    base = place * GROUP - GROUP
    doc, pos = locate(base + jnp.arange(WINDOW, dtype=jnp.int32), opening, finish, stream_rows)
    edges = base + GROUP + jnp.asarray([0, HALF - 1, HALF, GROUP - 1], jnp.int32)
    edge_begin = jnp.max(jnp.where(opening[None, :] <= edges[:, None], opening[None, :], 0), axis=1)
    edge_end = jnp.min(
        jnp.where(finish[None, :] > edges[:, None], finish[None, :], stream_rows), axis=1
    )
    lows = jnp.clip((edge_begin - base) // CHUNK, 0, 6)
    highs = jnp.clip((edge_end - base + CHUNK - 1) // CHUNK, 0, 6)
    scal = jnp.stack(
        [unit, core, side, lows[0], highs[1], lows[2], highs[3], zero]
    ).astype(jnp.int32)
    before = shifted(tokens, "fsdp", 1)
    after = shifted(tokens, "fsdp", -1)
    other_tokens = swap(tokens, "seq", 1)
    if fast:
        halves = widen_matrix.reshape(rows, 2, FF // 2)
        keep = lax.dynamic_index_in_dim(halves, side, 1, False)
        give = lax.dynamic_index_in_dim(halves, 1 - side, 1, False)
        mine = jnp.concatenate([keep, merge_matrix], axis=1)[None]
        got = swap(jnp.concatenate([give, merge_matrix], axis=1)[None], *SIDE)
        wide = in_order(side, mine, got, 0)
        wide = jnp.concatenate(
            [wide[:, :, : FF // 2].reshape(2, rows, 2, D), wide[:, :, FF // 2 :].reshape(2, rows, 2, OWN)],
            axis=3,
        )
        mine = lax.dynamic_index_in_dim(wide, core, 2, False)
        sent = lax.dynamic_index_in_dim(wide, 1 - core, 2, False)
        wide = in_order(core, mine, swap(sent, *CORE), 1)
        shard = jnp.concatenate(
            [
                shrink_matrix,
                wide[:, :, :D].reshape(96, D),
                wide[:, :, D:].transpose(1, 0, 2).reshape(48, D),
            ],
            axis=0,
        )
        wq = own_columns(projection_matrix_triple, nf, side, place)
        pack = jnp.concatenate(
            [
                relaxed_low.reshape(6, 32, 4, 128).transpose(0, 2, 1, 3).reshape(768, 128),
                wq.reshape(48, 9, 128).transpose(1, 0, 2).reshape(432, 128),
                packed,
                jnp.zeros((32, 128), BF),
            ],
            axis=0,
        )
        gathered = lax.all_gather(pack, "fsdp", axis=0, tiled=True)
        other_tokens, before, after, scal, pos, doc = tie(
            other_tokens, before, after, scal, pos, doc
        )
        other_before = swap(before, *SIDE)
        other_after = swap(after, *SIDE)
        other_before, other_after, shard, cot = tie(other_before, other_after, shard, cot)
        wg = lax.all_gather(shard, "fsdp", axis=0, tiled=True).reshape(8, 2, 240, D)
        cot_other = swap(cot, *SIDE)
        cot_other, gathered = tie(cot_other, gathered)
        weights, table = gathered.reshape(16, 26, 48, 128), gathered.reshape(16, 39, 32, 128)
        near_owner = jnp.arange(nf, dtype=jnp.int32)[:, None]
        near = weights[:, 25, 0:16].transpose(1, 0, 2)
    else:
        other_before = swap(before, "seq", 1)
        other_after = swap(after, "seq", 1)
        full = lax.all_gather(projection_matrix_triple, BOTH, axis=0, tiled=True)
        full = lax.dynamic_index_in_dim(full.reshape(D, 3, 2, OWN), side, 2, False)
        full = full.reshape(2, 8, 48, 9, 128).transpose(1, 0, 3, 2, 4).reshape(16, 9, 48, 128)
        table = lax.all_gather(relaxed_low, "fsdp", axis=1, tiled=True)
        table = table.reshape(6, 16, 32, 4, 128).transpose(1, 0, 3, 2, 4).reshape(16, 24, 32, 128)
        weights = jnp.concatenate([table.reshape(16, 16, 48, 128), full], axis=1)
        smalls = lax.all_gather(packed[None], BOTH, axis=0, tiled=True).transpose(1, 0, 2)
        near = lax.dynamic_slice_in_dim(smalls, side * nf, nf, 1)
        near_owner = jnp.arange(nf, dtype=jnp.int32)[:, None]
        owner = jnp.arange(count, dtype=jnp.int32)[:, None]
        cot_other = swap(cot, *SIDE)
        up = lax.all_gather(widen_matrix, BOTH, axis=0, tiled=True)
        up = lax.dynamic_slice_in_dim(up, side * (FF // 2), FF // 2, 1)
        up = up.reshape(2, 8, 48, 2, D).transpose(1, 3, 0, 2, 4).reshape(8, 2, 96, D)
        down = lax.all_gather(shrink_matrix, "fsdp", axis=0, tiled=True).reshape(8, 2, 96, D)
        out = lax.all_gather(merge_matrix, BOTH, axis=0, tiled=True)
        out = out.reshape(2, 8, 48, 2, OWN).transpose(1, 3, 2, 0, 4).reshape(8, 2, 48, D)
        wg = jnp.concatenate([down, up, out], axis=2)

    pos_col, doc_col = pos.reshape(WINDOW, 1), doc.reshape(WINDOW, 1)
    pos_row, doc_row = pos.reshape(6, 1, CHUNK), doc.reshape(6, 1, CHUNK)
    pieces = (tokens, before, after, other_tokens, other_before, other_after)
    q, k, v, xw, k_turned, x_turned = project(scal, pieces, weights, near, near_owner, spread, group)
    if fast:
        far = swap(near, "seq", 1)
        smalls = jnp.concatenate([near, far], axis=1)
        owner = jnp.concatenate([side * nf + near_owner, (1 - side) * nf + near_owner], axis=0)
        q, smalls = tie(q, smalls)
    ctx, inverses, *kept = attend(scal, pos_col, pos_row, doc_col, doc_row, q, k, v, table)
    ctx_other = swap(ctx, *SIDE)
    params_of = (smalls, owner, spread, group, wg)
    up = lambda i: feed_up(
        i, scal, xw, ctx, ctx_other, smalls, owner, near, near_owner,
        (spread, group, spread_up, group_up), wg,
    )
    down = lambda i, base, got, slope: feed_back(
        i, scal, base, got, cot, cot_other, slope, *params_of
    )
    close = lambda i, base, got, unit, rstd, sums: feed_close(
        i, scal, base, got, unit, rstd, sums, *params_of
    )
    up0 = up(0)
    got0 = swap(up0[4], *SIDE)
    up1, got0 = tie(up(1), got0)
    got1 = swap(up1[4], *SIDE)
    down0, got1 = tie(down(0, up0[3], got0, up0[6]), got1)
    got0 = swap(down0[4], *SIDE)
    down1, got0 = tie(down(1, up1[3], got1, up1[6]), got0)
    got1 = swap(down1[4], *SIDE)
    closed0 = close(0, down0[3], got0, up0[0], up0[1], down0[5] + down1[5])
    feed = weight_grads(
        scal, up0[5], down0[1], up0[2], down0[2], up1[5], down1[1], up1[2], down1[2]
    )
    closed0, feed, got1 = tie(closed0, feed, got1)
    if fast:
        feed_got = swap(by_core(feed[1]), *CORE)
    closed1 = close(1, down1[3], got1, up1[0], up1[1], closed0[3])
    if fast:
        closed1, feed_got = tie(closed1, feed_got)
        feed = sum_core(feed[0], feed_got)
        feed_got = swap(feed[1], *ALONG_Y)
    dh1, dattn, dctx = [[c[i] for c in (closed0, closed1)] for i in range(3)]
    sums = closed1[3]
    lay = jnp.where(side == 0, down0[0], down1[0])
    back = lambda first, pairs, before: attend_back(
        first, pairs, before, scal, q, k_turned, v, kept, x_turned, sums, ctx, dctx, dattn, inverses
    )
    outs = back(0, 3, ())
    if fast:
        outs, feed_got = tie(outs, feed_got)
        feed = add(feed[0][:2], feed_got[:2]), add(feed[0][2:], feed_got[2:])
        outs, feed = tie(outs, feed)
    dq, own, low, high, *parts = outs

    own_cols = lambda values, at, size: lax.dynamic_slice_in_dim(values, at * size, size, 1)
    if fast:
        feed_got = swap(feed[1], "fsdp", 4)
        part_got = swap(by_core(parts[1]), *CORE)
        table_got = swap(by_core(parts[3]), *CORE)
        part_got, table_got = tie(part_got, table_got)
        part, table_part = sum_core(parts[0], part_got), sum_core(parts[2], table_got)
        part_got = swap(part[1], *ALONG_Y)
        feed = add(feed[0][0], feed_got[0]), add(feed[0][1], feed_got[1])
        feed_got = swap(feed[1], "fsdp", 8)
        part_got, feed_got, table_part, low, high = tie(
            part_got, feed_got, table_part, low, high
        )
        part_got = along_z(add(part[0], part_got))
        table_got = swap(table_part[1], *ALONG_Y)
        left, right = shifted(high, "fsdp", 1), shifted(low, "fsdp", -1)
        table_got, left, right = tie(table_got, left, right)
        table_got, left, right = tie(add(table_part[0], table_got), left, right)
        table_got = along_z(table_got)
        dx, dx_send = project_back(scal, (dq, own, left, right), dh1, weights)
        dx_got = swap(dx_send, *SIDE)
        shard = add(feed[0], feed_got)
        part = sum_z(part_got)
        table_total = sum_z(table_got)
        table_total = table_total.reshape(3, 2, 4, 32, 128).transpose(0, 1, 3, 2, 4)
        table_total = table_total.reshape(6, 32, MPOS).astype(F32)
        blocks = part.reshape(3, PART, 128)
        weight = blocks[:, :PART_SUMS].reshape(3, 3, 2, rows, 128).transpose(1, 0, 2, 3, 4)
        mine = lax.dynamic_index_in_dim(weight, side, 2, False)
        sent = lax.dynamic_index_in_dim(weight, 1 - side, 2, False)
        sums = blocks[:, PART_SUMS:PART_OUT].reshape(6, 16, 128)
        sums = sums.transpose(1, 0, 2).reshape(16, D).astype(F32)
        outs = blocks[:, PART_OUT:].reshape(6, rows, 128)
        grad_w_out = outs.transpose(1, 0, 2).reshape(rows, D).astype(F32)
        got = swap(sent.reshape(-1, 128), *SIDE)
        got = got.reshape(3, 3, rows, 128)
        mine = mine.transpose(2, 0, 1, 3).reshape(rows, 3, 1, OWN)
        got = got.transpose(2, 0, 1, 3).reshape(rows, 3, 1, OWN)
        grad_w_qkv = in_order(side, mine, got, 2).reshape(rows, 3 * D).astype(F32)
        head_sums = blocks[:, PART_TOTALS : PART_TOTALS + 2].transpose(1, 0, 2).reshape(2, OWN)
        head_sums = head_sums.astype(F32)
        head_grads = own_cols(head_sums, place, wide_cols)
        grad_w_down = shard[:96].astype(F32)
        wide = shard[96:192].reshape(2, 2, rows, D).transpose(0, 2, 1, 3).reshape(2, rows, FF // 2)
        mine = lax.dynamic_index_in_dim(wide, side, 0, False)
        got = swap(lax.dynamic_index_in_dim(wide, 1 - side, 0, False), *SIDE)
        grad_w_up = in_order(side, mine, got, 1).astype(F32)
    else:
        scatter = partial(lax.psum_scatter, axis_name=BOTH, scatter_dimension=0, tiled=True)
        left, right = shifted(high, "fsdp", 1), shifted(low, "fsdp", -1)
        dx, dx_send = project_back(scal, (dq, own, left, right), dh1, weights)
        dx_got = swap(dx_send, "seq", 1)

        def plain(pair, at=lambda u: 4 * (u & 1) + (u >> 1)):
            both = jnp.stack(pair, axis=1)
            return jnp.stack([both[at(u)] for u in range(8)], axis=0)

        blocks = plain(parts[:2]).reshape(8, 2, 3, PART, 128)
        table_grad = plain(parts[2:]).reshape(8, 2, 3, 2, 4, 32, 128).transpose(2, 3, 0, 1, 5, 4, 6)
        table_total = lax.psum_scatter(
            table_grad.reshape(6, MPOS, MPOS), "fsdp", scatter_dimension=1, tiled=True
        ).astype(F32)
        head_rows = blocks[:, :, :, :PART_SUMS].reshape(8, 2, 3, 3, 2, 24, 128)
        head_rows = head_rows.transpose(4, 0, 1, 5, 3, 2, 6).reshape(D, 3, 1, OWN)
        blank = jnp.zeros_like(head_rows)
        both = jnp.concatenate(
            [jnp.where(side == 0, head_rows, blank), jnp.where(side == 0, blank, head_rows)], axis=2
        )
        grad_w_qkv = scatter(both.reshape(D, 3 * D)).astype(F32)
        head_sums = blocks[0, 0, :, PART_TOTALS : PART_TOTALS + 2].transpose(1, 0, 2)
        head_sums = lax.psum(head_sums.reshape(2, OWN).astype(F32), "fsdp")
        head_grads = own_cols(head_sums, place, wide_cols)
        def placed(value, axis):
            blank = jnp.zeros_like(value)
            sides = [jnp.where(side == 0, value, blank), jnp.where(side == 0, blank, value)]
            return jnp.concatenate(sides, axis=axis)

        gg = plain(feed, lambda u: 4 * (u & 1) + (u & 2) + (u >> 2)).reshape(16, 192, D)
        grad_w_down = scatter(placed(gg[:, :96].reshape(FF // 2, D), 0)).astype(F32)
        up = gg[:, 96:192].reshape(16, 2, 2, 24, D).transpose(1, 0, 3, 2, 4).reshape(D, FF // 2)
        grad_w_up = scatter(placed(up, 1)).astype(F32)
        out = blocks[:, :, :, PART_OUT:].reshape(8, 2, 3, 2, 24, 128).transpose(0, 1, 4, 2, 3, 5)
        out = out.reshape(OWN, D)
        grad_w_out = scatter(placed(out, 0)).astype(F32)
        sums = lax.psum(sums, "fsdp")
    ours = own_cols(sums[:6], side * nf + place, wide_cols)
    grad_biases = jnp.concatenate([head_grads, ours[:4]], axis=0)
    grad_gains = ours[4:]
    grad_bias_up = lax.dynamic_slice_in_dim(
        sums[8:10].reshape(-1), place * up_cols, up_cols, 0
    )
    input_grad = dx + dx_got.astype(F32)
    mask_logit_gradient = (
        table_total * relaxed * (1.0 - relaxed) / softening_scale[:, None, None]
    )
    return (
        lay.reshape(1, HALF, D),
        input_grad.reshape(1, HALF, D),
        grad_w_qkv,
        grad_w_out,
        grad_w_up,
        grad_w_down,
        grad_biases,
        grad_gains,
        grad_bias_up,
        mask_logit_gradient,
    )


def solution(mesh):
    rows = P(("seq", "fsdp"), None)
    columns = P(None, ("seq", "fsdp"))
    block = P("fsdp", "seq", None)
    table = P("seq", "fsdp", None)
    return jax.shard_map(
        per_device,
        mesh=mesh,
        in_specs=(
            block, rows, rows, rows, rows, columns, columns, P(("seq", "fsdp")),
            table, table, P("seq"), P(), block,
        ),
        out_specs=(
            block, block, rows, rows, rows, rows, columns, columns, P(("seq", "fsdp")), table,
        ),
        check_vma=False,
    )
```

```python
from functools import partial

import jax
import jax.numpy as jnp
from jax import lax
from jax.experimental import pallas as pl
from jax.experimental.pallas import tpu as pltpu
from jax.sharding import PartitionSpec as P

D = 768
FF = 3072
HEADS = 12
HDIM = 64
MPOS = 512
EPS = 1e-05
GROUP = 512
HALF = 256
WINDOW = 3 * GROUP
OWN = 384
CHUNK = 256
NEG = -1e30
BF = jnp.bfloat16
F32 = jnp.float32
HIGH = lax.Precision.HIGHEST
PART_SUMS = 144
PART_TOTALS = PART_SUMS + 6
PART_OUT = 176
PART = 224
PART_TABLE = 256


def nn(left, right):
    return jnp.dot(left, right, preferred_element_type=F32)


def nt(left, right, precision=None):
    return lax.dot_general(
        left, right, (((1,), (1,)), ((), ())), precision=precision, preferred_element_type=F32
    )


def tn(left, right):
    return lax.dot_general(left, right, (((0,), (0,)), ((), ())), preferred_element_type=F32)


def load_projection(gathered, w, sem):
    copies = []
    for f in range(16):
        row = (f % 2) * OWN + (f // 2) * 48
        copies.append(
            pltpu.make_async_copy(gathered.at[f, 16:25], w.at[:, row : row + 48, :], sem.at[f])
        )
    for copy in copies:
        copy.start()
    return copies


def table_of(table, head):
    return jnp.concatenate(
        [table[:, 4 * head + part].reshape(MPOS, 128) for part in range(4)], axis=1
    )


def spread_out(values, spread, owner, group):
    return jnp.sum(jnp.where(owner == group, nn(values, spread), 0.0), axis=0, keepdims=True)


def columns_of(w, first, count=3):
    return jnp.concatenate([w[first + part] for part in range(count)], axis=1)


def place_of(t, cr, scal):
    unit = ((t >> 2) ^ (scal[0] & 1)) | ((t & 3) << 1)
    return 2 * unit + (scal[1] ^ cr)


def near_place_of(t, cr, scal):
    unit = ((t >> 2) | (t & 2) | ((t & 1) << 2)) ^ scal[0]
    return 2 * unit + (scal[1] ^ cr)


def project_kernel(
    scal,
    x1,
    x0,
    x2,
    y1,
    y0,
    y2,
    gathered,
    near,
    owner,
    spread,
    group,
    q_ref,
    k_ref,
    v_ref,
    xw,
    k_turned,
    x_turned,
    w,
    sem,
):
    copies = load_projection(gathered, w, sem)
    side = scal[2]
    for g, (mine, other) in enumerate(((x0, y0), (x1, y1), (x2, y2))):
        xw[pl.ds(pl.multiple_of(g * GROUP + side * HALF, HALF), HALF), :] = mine[...]
        xw[pl.ds(pl.multiple_of(g * GROUP + (1 - side) * HALF, HALF), HALF), :] = other[...]
    bias = [
        spread_out(near[i], spread[:, :OWN], owner[...], group[:, :OWN]) for i in range(2)
    ]
    for copy in copies:
        copy.wait()
    for blk in range(6):
        rows = slice(blk * HALF, (blk + 1) * HALF)
        here = xw[rows, :]
        key = nn(here, columns_of(w, 3))
        k_ref[rows, :] = key.astype(BF)
        k_turned[blk] = key.T.astype(BF)
        x_turned[:, rows] = here.astype(F32).T.astype(BF)
        v_ref[rows, :] = (nn(here, columns_of(w, 6)) + bias[1]).astype(BF)
        if blk in (2, 3):
            local = slice((blk - 2) * HALF, (blk - 1) * HALF)
            query = (nn(here, columns_of(w, 0)) + bias[0]).astype(BF)
            q_ref[local, :] = query * jnp.asarray(0.125, BF)


def head_lanes():
    return lax.broadcasted_iota(jnp.int32, (1, 128), 1) < HDIM


def fill_hot(pos_col, hot):
    for blk in range(6):
        rows = slice(blk * 256, (blk + 1) * 256)
        column = lax.broadcasted_iota(jnp.int32, (256, MPOS), 1)
        hot[rows, :] = jnp.where(pos_col[rows, :] == column, 1.0, 0.0).astype(BF)


def fill_hot_turned(pos_row, hot):
    for blk in range(6):
        rows = lax.broadcasted_iota(jnp.int32, (MPOS, 256), 0)
        hot[blk] = jnp.where(pos_row[blk] == rows, 1.0, 0.0).astype(BF)


def set_pair(low, value, target):
    blank = jnp.zeros_like(value)
    target[:HALF, :] = jnp.where(low, value, blank)
    target[HALF:, :] = jnp.where(low, blank, value)


def fold(values, how):
    rows, columns = values.shape
    return how(values.reshape(rows // 8, 8, columns), axis=0)


def attend_kernel(
    scal,
    pos_col,
    pos_row,
    doc_col,
    doc_row,
    q,
    k,
    v,
    table,
    ctx,
    inverses,
    weights,
    mixes,
    hot_turned,
    hot,
    sbuf,
    looks,
    queries,
    acc,
):
    @pl.when(pl.program_id(0) == 0)
    def _():
        fill_hot(pos_col, hot)
        fill_hot_turned(pos_row, hot_turned)

    low = head_lanes()
    for qb in range(2):
        lo, hi = scal[3 + 2 * qb], scal[4 + 2 * qb]
        here = slice(qb * HALF, (qb + 1) * HALF)
        set_pair(low, q[here, :], queries)
        q_doc = jnp.concatenate([doc_row[2 + qb]] * 2, axis=1)
        q_hot = hot[GROUP + qb * HALF : GROUP + (qb + 1) * HALF, :]
        for h in range(2):
            looks[h * HALF : (h + 1) * HALF, :] = nn(q_hot, table_of(table, h)).astype(BF)

        def score_step(c, top, q_doc=q_doc):
            rows = pl.ds(pl.multiple_of(c * CHUNK, CHUNK), CHUNK)
            s = jnp.where(doc_col[rows, :] == q_doc, nt(k[rows, :], queries[...]), NEG)
            sbuf[c] = s
            return jnp.maximum(top, fold(s, jnp.max))

        top = lax.fori_loop(lo, hi, score_step, jnp.full((8, 2 * HALF), NEG, F32))
        top = jnp.max(top, axis=0, keepdims=True)
        acc[...] = jnp.zeros_like(acc)

        def mix_step(c, total, top=top, qb=qb):
            rows = pl.ds(pl.multiple_of(c * CHUNK, CHUNK), CHUNK)
            e = jnp.exp(sbuf[c] - top)
            mixed = (e * nt(hot[rows, :], looks[...])).astype(BF)
            weights[0, qb, c] = e.astype(BF)
            mixes[0, qb, c] = mixed
            acc[...] += tn(mixed, v[rows, :])
            return total + fold(e, jnp.sum)

        total = lax.fori_loop(lo, hi, mix_step, jnp.zeros((8, 2 * HALF), F32))
        total = jnp.sum(total, axis=0, keepdims=True)
        inverse = 1.0 / total
        inverses[0, 0:1, here] = inverse[:, :HALF]
        inverses[0, 1:2, here] = inverse[:, HALF:]
        inverses[0, 2:8, here] = jnp.zeros((6, HALF), F32)
        scale = jnp.concatenate(
            [
                jnp.broadcast_to(inverse[:, :HALF], (HDIM, HALF)),
                jnp.broadcast_to(inverse[:, HALF:], (HDIM, HALF)),
            ],
            axis=0,
        ).T
        ctx[qb] = (jnp.where(low, acc[:HALF, :], acc[HALF:, :]) * scale).astype(BF)


def attend_back_kernel(
    carried,
    scal,
    q,
    k,
    v,
    weights,
    mixes,
    hot_turned,
    xw,
    sums,
    ctx,
    ctx_all,
    dctx0,
    dctx1,
    dattn0,
    dattn1,
    inverses,
    *refs,
):
    outs = refs[carried : carried + 8]
    dq, own, halo_low, halo_high, part_keep, part_send, table_keep, table_send = outs
    queries, grads, dk, dv, dq_acc, tt, tg, gw, gout = refs[carried + 8 :]
    low = head_lanes()
    dk[...] = jnp.zeros_like(dk)
    dv[...] = jnp.zeros_like(dv)
    lane = lax.broadcasted_iota(jnp.int32, (8, 128), 1)
    row8 = lax.broadcasted_iota(jnp.int32, (8, 128), 0)
    pick = jnp.where((lane < HDIM) == (row8 == 0), 1.0, 0.0)
    for qb in range(2):
        lo, hi = scal[3 + 2 * qb], scal[4 + 2 * qb]
        here = slice(qb * HALF, (qb + 1) * HALF)
        inverse = inverses[0, 0:2, here]
        d_pair = (dctx0, dctx1)[qb][...].astype(F32)
        deltas = nt(pick, d_pair * ctx[qb].astype(F32), HIGH)[0:2, :] * inverse
        delta = jnp.concatenate([deltas[0:1, :], deltas[1:2, :]], axis=1)
        scale = jnp.concatenate(
            [
                jnp.broadcast_to(inverse[0:1, :], (HDIM, HALF)),
                jnp.broadcast_to(inverse[1:2, :], (HDIM, HALF)),
            ],
            axis=0,
        ).T
        set_pair(low, q[here, :], queries)
        set_pair(low, (d_pair * scale).astype(BF), grads)
        dq_acc[...] = jnp.zeros_like(dq_acc)
        tt[...] = jnp.zeros_like(tt)

        def step(c, carry, delta=delta, qb=qb):
            rows = pl.ds(pl.multiple_of(c * CHUNK, CHUNK), CHUNK)
            mixed = mixes[0, qb, c]
            e = weights[0, qb, c].astype(F32)
            dm = nt(v[rows, :], grads[...])
            ds = (mixed.astype(F32) * dm - e * delta).astype(BF)
            dv[rows, :] += nn(mixed, grads[...])
            dk[rows, :] += nn(ds, queries[...])
            dq_acc[...] += nn(k[c], ds)
            tt[...] += nn(hot_turned[c], (e * dm).astype(BF))
            return carry

        lax.fori_loop(lo, hi, step, 0)
        for h in range(2):
            piece = nt(hot_turned[2 + qb], tt[:, h * HALF : (h + 1) * HALF].astype(BF))
            if qb == 0:
                tg[h] = piece
            else:
                tg[h] += piece
        both = jnp.concatenate([dq_acc[:HDIM, :HALF], dq_acc[HDIM:, HALF:]], axis=0)
        dq[here, :] = (both.T * 0.125).astype(BF)
    own[0] = dk[GROUP : 2 * GROUP, :]
    own[1] = dv[GROUP : 2 * GROUP, :]
    halo_low[0] = dk[:GROUP, :].astype(BF)
    halo_low[1] = dv[:GROUP, :].astype(BF)
    halo_high[0] = dk[2 * GROUP :, :].astype(BF)
    halo_high[1] = dv[2 * GROUP :, :].astype(BF)
    query_grad = dq[...]
    pair_grad = jnp.concatenate([dk[...].astype(BF), dv[...].astype(BF)], axis=1)
    gw[:, 0:128] = nn(xw[:, GROUP : 2 * GROUP], query_grad)
    gw[:, 128:384] = nn(xw[...], pair_grad)
    gout[...] = tn(ctx_all[0], dattn0[...]) + tn(ctx_all[1], dattn1[...])
    totals = jnp.concatenate(
        [
            sums[0:6, 0:128],
            column_sum(query_grad.astype(F32)),
            column_sum(pair_grad[:, 128:].astype(F32)),
            sums[8:16, 0:128],
            sums[:, 128:256],
        ],
        axis=0,
    ).astype(BF)
    for cr in range(2):
        out, table = (part_keep, table_keep) if cr == 0 else (part_send, table_send)
        for t in range(8):
            place = place_of(t, cr, scal)
            rows = [
                gw[pl.ds(pl.multiple_of(part * OWN + place * 24, 8), 24), :] for part in range(2)
            ]
            both = jnp.concatenate(rows, axis=0).astype(BF)
            for i in range(3):
                out[t, i * 48 : i * 48 + 48, :] = both[:, i * 128 : (i + 1) * 128]
            out[t, PART_SUMS:PART_OUT, :] = totals
            rows = gout[pl.ds(pl.multiple_of(place * 24, 8), 24), :]
            out[t, PART_OUT:PART, :] = jnp.concatenate(
                [rows[:, 0:128], rows[:, 128:256]], axis=0
            ).astype(BF)
            for h in range(2):
                mask = tg[h, pl.ds(pl.multiple_of(place * 32, 32), 32), :].astype(BF)
                for i in range(4):
                    at = (4 * h + i) * 32
                    table[t, at : at + 32, :] = mask[:, i * 128 : (i + 1) * 128]


def norm_stats(values):
    center = values - jnp.mean(values, axis=-1, keepdims=True)
    rstd = lax.rsqrt(jnp.mean(center * center, axis=-1, keepdims=True) + EPS)
    return center * rstd, rstd


def norm_back(grad, unit, rstd, gain):
    scaled = grad * gain
    return rstd * (
        scaled
        - jnp.mean(scaled, axis=-1, keepdims=True)
        - unit * jnp.mean(scaled * unit, axis=-1, keepdims=True)
    )


def column_sum(values):
    return jnp.sum(values, axis=0, keepdims=True)


def load_feed(wg, sem, wm=None, wu=None, wd=None):
    copies = []

    def bring(source, target):
        copies.append(pltpu.make_async_copy(source, target, sem.at[len(copies)]))
        copies[-1].start()

    for c in range(2):
        for s in range(2):
            if wm is not None:
                bring(
                    wg.at[:, c, 192:240, s * OWN : (s + 1) * OWN],
                    wm.at[s, :, :, c * OWN : (c + 1) * OWN],
                )
    for c in range(2):
        for s in range(2):
            if wu is not None:
                bring(wg.at[:, c, 96 + 48 * s : 144 + 48 * s, :], wu.at[c, s])
    for c in range(2):
        if wd is not None:
            bring(wg.at[:, c, 0:96, :], wd.at[:, c])
    return copies


def shrink_rows(wd, i):
    return wd[pl.ds(4 * i, 4)].reshape(D, D)


def wait_for(copies):
    for copy in copies:
        copy.wait()


def feed_up_kernel(
    scal,
    x,
    ctx_mine,
    ctx_other,
    smalls,
    owner,
    near,
    near_owner,
    spread,
    group,
    spread_up,
    group_up,
    wg,
    unit1,
    rstd1,
    nlow,
    base,
    send,
    act,
    slope,
    wm,
    wu,
    wd,
    ctxt,
    bup,
    sem,
):
    copies = load_feed(wg, sem, wm, wu, wd)
    vector = lambda i: spread_out(smalls[i], spread[...], owner[...], group[...])
    bias_out, bias_down, shift1, gain1 = [vector(i) for i in (2, 3, 4, 6)]
    for n in range(2):
        bup[n] = spread_out(
            near[8], spread_up[...], near_owner[...], group_up[...] + n * (near.shape[1] // 2)
        )
    even = scal[2] == 0
    mine, other = ctx_mine[0], ctx_other[0]
    ctxt[:, :OWN] = jnp.where(even, mine, other)
    ctxt[:, OWN:] = jnp.where(even, other, mine)
    wait_for(copies[:4])
    attn = nn(ctxt[...], wm[...].reshape(D, D)) + bias_out
    unit, rstd = norm_stats(x[...].astype(F32) + attn)
    unit1[...] = unit
    rstd1[...] = jnp.broadcast_to(rstd, (HALF, 128))
    normed = unit * gain1 + shift1
    nlow[...] = normed.astype(BF)
    base[...] = normed + bias_down
    wait_for(copies[4:8])

    def widen(n, carry):
        up = nn(nlow[...], wu[n].reshape(D, D)) + bup[n]
        half_cdf = 0.5 * (1.0 + lax.erf(up * 0.7071067811865476))
        act[n] = (up * half_cdf).astype(BF)
        slope[n] = half_cdf + up * (0.3989422804014327 * jnp.exp(-0.5 * up * up))
        return carry

    lax.fori_loop(0, 2, widen, 0)
    wait_for(copies[8:])
    part = nn(act[0], shrink_rows(wd, 0)) + nn(act[1], shrink_rows(wd, 1))
    base[...] += part
    send[...] = part.astype(BF)


def feed_back_kernel(
    index,
    scal,
    base,
    got,
    cot_mine,
    cot_other,
    slope,
    smalls,
    owner,
    spread,
    group,
    wg,
    lay,
    ddown,
    dup,
    base2,
    send,
    sums,
    wu,
    wd,
    sem,
):
    copies = load_feed(wg, sem, None, wu, wd)
    vector = lambda i: spread_out(smalls[i], spread[...], owner[...], group[...])
    shift2, gain2 = vector(5), vector(7)
    sums[...] = jnp.zeros_like(sums)
    unit, rstd = norm_stats(base[...] + got[...].astype(F32))
    lay[...] = (unit * gain2 + shift2).astype(BF)
    dy = jnp.where(scal[2] == index, cot_mine[...], cot_other[...]).astype(F32)
    sums[3:4, :] = column_sum(dy)
    sums[5:6, :] = column_sum(dy * unit)
    grad = norm_back(dy, unit, rstd, gain2)
    ddown[...] = grad.astype(BF)
    sums[1:2, :] = column_sum(ddown[...].astype(F32))
    base2[...] = grad
    wait_for(copies)

    def back(n, carry):
        low = (nt(ddown[...], shrink_rows(wd, n)) * slope[n]).astype(BF)
        dup[n] = low
        sums[pl.ds(8 + n, 1), :] = column_sum(low.astype(F32))
        return carry

    lax.fori_loop(0, 2, back, 0)
    part = nt(dup[0], wu[0].reshape(D, D)) + nt(dup[1], wu[1].reshape(D, D))
    base2[...] += part
    send[...] = part.astype(BF)


def feed_close_kernel(
    scal,
    base,
    got,
    unit1,
    rstd1,
    sums_in,
    sums_more,
    smalls,
    owner,
    spread,
    group,
    wg,
    dh1,
    dattn,
    dctx,
    sums,
    wm,
    sem,
):
    copies = load_feed(wg, sem, wm)
    gain1 = spread_out(smalls[6], spread[...], owner[...], group[...])
    sums[...] = sums_in[...] + sums_more[...]
    grad = base[...] + got[...].astype(F32)
    unit = unit1[...]
    sums[2:3, :] += column_sum(grad)
    sums[4:5, :] += column_sum(grad * unit)
    grad = norm_back(grad, unit, rstd1[:, 0:1], gain1)
    dh1[...] = grad
    dattn[...] = grad.astype(BF)
    sums[0:1, :] += column_sum(dattn[...].astype(F32))
    wait_for(copies)
    dctx[...] = nt(dattn[...], wm[scal[2]].reshape(OWN, D)).astype(BF)


def weight_grad_kernel(
    scal, act0, ddown0, nlow0, dup0, act1, ddown1, nlow1, dup1, keep, send, down, up
):
    for n in range(2):
        up[n] = tn(nlow0[...], dup0[n]) + tn(nlow1[...], dup1[n])
        down[n * D : (n + 1) * D, :] = tn(act0[n], ddown0[...]) + tn(act1[n], ddown1[...])
    for cr, out in enumerate((keep, send)):
        for t in range(8):
            place = near_place_of(t, cr, scal)
            out[t, 0:96, :] = down[pl.ds(pl.multiple_of(place * 96, 8), 96), :].astype(BF)
            parts = [
                up[n, pl.ds(pl.multiple_of(s * OWN + place * 24, 8), 24), :]
                for s in range(2)
                for n in range(2)
            ]
            out[t, 96:192, :] = jnp.concatenate(parts, axis=0).astype(BF)


def project_back_kernel(scal, parts, dh1s, gathered, dx, dx_send, w, dqkv, sem):
    copies = load_projection(gathered, w, sem)
    dq, own, left, right = parts
    dqkv[:, :OWN] = dq[...]
    for i in range(2):
        total = own[i] + left[i].astype(F32) + right[i].astype(F32)
        dqkv[:, (1 + i) * OWN : (2 + i) * OWN] = total.astype(BF)
    for copy in copies:
        copy.wait()
    side = scal[2]
    mine = dqkv[pl.ds(pl.multiple_of(side * HALF, HALF), HALF), :]
    other = dqkv[pl.ds(pl.multiple_of((1 - side) * HALF, HALF), HALF), :]
    for part in range(3):
        cols = slice(part * 256, (part + 1) * 256)
        rows = jnp.concatenate([w[j, cols, :] for j in range(9)], axis=1)
        dh1 = jnp.where(side == 0, dh1s[0][:, cols], dh1s[1][:, cols])
        dx[:, cols] = dh1 + nt(mine, rows)
        dx_send[:, cols] = nt(other, rows).astype(BF)


SMEM = pl.BlockSpec(memory_space=pltpu.SMEM)
VM = pl.BlockSpec()
HBM = pl.BlockSpec(memory_space=pl.ANY)


def params():
    return pltpu.CompilerParams(vmem_limit_bytes=60 * 1024 * 1024)


def cost(microseconds):
    return pl.CostEstimate(
        flops=int(microseconds * 1.15e9), bytes_accessed=1000, transcendentals=0
    )


def shape(dims, kind):
    return jax.ShapeDtypeStruct(dims, kind)


def project(scal, pieces, gathered, near, owner, spread, group):
    return pl.pallas_call(
        project_kernel,
        name="project",
        out_shape=(
            shape((GROUP, OWN), BF),
            shape((WINDOW, OWN), BF),
            shape((WINDOW, OWN), BF),
            shape((WINDOW, D), BF),
            shape((6, OWN, CHUNK), BF),
            shape((D, WINDOW), BF),
        ),
        in_specs=[SMEM] + [VM] * 6 + [HBM] + [VM] * 4,
        out_specs=[VM] * 6,
        scratch_shapes=[
            pltpu.VMEM((9, D, 128), BF),
            pltpu.SemaphoreType.DMA((16,)),
        ],
        compiler_params=params(),
        cost_estimate=cost(9),
    )(scal, *pieces, gathered, near, owner, spread, group)


def whole(*dims):
    return pl.BlockSpec(dims, lambda p: (0,) * len(dims))


def attend(scal, pos_col, pos_row, doc_col, doc_row, q, k, v, table):
    return pl.pallas_call(
        attend_kernel,
        name="attend",
        grid=(3,),
        out_shape=(
            shape((2, HALF, OWN), BF),
            shape((3, 8, GROUP), F32),
            shape((3, 2, 6, CHUNK, 2 * HALF), BF),
            shape((3, 2, 6, CHUNK, 2 * HALF), BF),
            shape((6, MPOS, CHUNK), BF),
        ),
        in_specs=[
            SMEM,
            whole(WINDOW, 1),
            whole(6, 1, CHUNK),
            whole(WINDOW, 1),
            whole(6, 1, CHUNK),
            pl.BlockSpec((GROUP, 128), lambda p: (0, p)),
            pl.BlockSpec((WINDOW, 128), lambda p: (0, p)),
            pl.BlockSpec((WINDOW, 128), lambda p: (0, p)),
            pl.BlockSpec((16, 8, 32, 128), lambda p: (0, p, 0, 0)),
        ],
        out_specs=[
            pl.BlockSpec((2, HALF, 128), lambda p: (0, 0, p)),
            pl.BlockSpec((1, 8, GROUP), lambda p: (p, 0, 0)),
            pl.BlockSpec((1, 2, 6, CHUNK, 2 * HALF), lambda p: (p, 0, 0, 0, 0)),
            pl.BlockSpec((1, 2, 6, CHUNK, 2 * HALF), lambda p: (p, 0, 0, 0, 0)),
            whole(6, MPOS, CHUNK),
        ],
        scratch_shapes=[
            pltpu.VMEM((WINDOW, MPOS), BF),
            pltpu.VMEM((6, CHUNK, 2 * HALF), F32),
            pltpu.VMEM((2 * HALF, MPOS), BF),
            pltpu.VMEM((2 * HALF, 128), BF),
            pltpu.VMEM((2 * HALF, 128), F32),
        ],
        compiler_params=params(),
        cost_estimate=cost(26),
    )(scal, pos_col, pos_row, doc_col, doc_row, q, k, v, table)


def attend_back(
    first, pairs, before, scal, q, k, v, kept, xw, sums, ctx, dctx, dattn, inverses
):
    columns = lambda rows: pl.BlockSpec((rows, 128), lambda p: (0, first + p))
    tiles = pl.BlockSpec((1, 2, 6, CHUNK, 2 * HALF), lambda p: (first + p, 0, 0, 0, 0))
    blocks = lambda rows: pl.BlockSpec((8, rows, 128), lambda p: (0, first + p, 0))
    both = pl.BlockSpec((2, GROUP, 128), lambda p: (0, 0, first + p))
    return pl.pallas_call(
        partial(attend_back_kernel, len(before)),
        name=f"attend_back_{first}",
        grid=(pairs,),
        input_output_aliases={16 + i: i for i in range(len(before))},
        out_shape=(
            shape((GROUP, OWN), BF),
            shape((2, GROUP, OWN), F32),
            shape((2, GROUP, OWN), BF),
            shape((2, GROUP, OWN), BF),
            shape((8, 3 * PART, 128), BF),
            shape((8, 3 * PART, 128), BF),
            shape((8, 3 * PART_TABLE, 128), BF),
            shape((8, 3 * PART_TABLE, 128), BF),
        ),
        in_specs=[
            SMEM,
            columns(GROUP),
            pl.BlockSpec((6, 128, CHUNK), lambda p: (0, first + p, 0)),
            columns(WINDOW),
            tiles,
            tiles,
            whole(6, MPOS, CHUNK),
            whole(D, WINDOW),
            pl.BlockSpec((16, 256), lambda p: (0, first + p)),
            pl.BlockSpec((2, HALF, 128), lambda p: (0, 0, first + p)),
            whole(2, HALF, OWN),
            columns(HALF),
            columns(HALF),
            pl.BlockSpec((HALF, 256), lambda p: (0, first + p)),
            pl.BlockSpec((HALF, 256), lambda p: (0, first + p)),
            pl.BlockSpec((1, 8, GROUP), lambda p: (first + p, 0, 0)),
        ]
        + [HBM] * len(before),
        out_specs=[
            columns(GROUP),
            both,
            both,
            both,
            blocks(PART),
            blocks(PART),
            blocks(PART_TABLE),
            blocks(PART_TABLE),
        ],
        scratch_shapes=[
            pltpu.VMEM((2 * HALF, 128), BF),
            pltpu.VMEM((2 * HALF, 128), BF),
            pltpu.VMEM((WINDOW, 128), F32),
            pltpu.VMEM((WINDOW, 128), F32),
            pltpu.VMEM((128, 2 * HALF), F32),
            pltpu.VMEM((MPOS, 2 * HALF), F32),
            pltpu.VMEM((2, MPOS, MPOS), F32),
            pltpu.VMEM((D, OWN), F32),
            pltpu.VMEM((OWN, 256), F32),
        ],
        compiler_params=params(),
        cost_estimate=cost(10 * pairs),
    )(scal, q, k, v, *kept, xw, sums, ctx, ctx, *dctx, *dattn, inverses, *before)


WIDEN = pltpu.VMEM((2, 2, 8, 48, D), BF)
SHRINK = pltpu.VMEM((8, 2, 96, D), BF)
MERGE = pltpu.VMEM((2, 8, 48, D), BF)


def feed_up(index, scal, xw, mine, other, smalls, owner, near, near_owner, spreads, wg):
    arrays = (smalls, owner, near, near_owner, *spreads)
    ctx = pl.BlockSpec((1, HALF, OWN), lambda p: (index, 0, 0))
    outs = (
        shape((HALF, D), F32),
        shape((HALF, 128), F32),
        shape((HALF, D), BF),
        shape((HALF, D), F32),
        shape((HALF, D), BF),
        shape((2, HALF, D), BF),
        shape((2, HALF, D), F32),
    )
    return pl.pallas_call(
        feed_up_kernel,
        name=f"feed_up_{index}",
        grid=(1,),
        out_shape=outs,
        in_specs=[SMEM, pl.BlockSpec((HALF, D), lambda p: (2 + index, 0)), ctx, ctx]
        + [whole(*a.shape) for a in arrays]
        + [HBM],
        out_specs=[whole(*out.shape) for out in outs],
        scratch_shapes=[
            MERGE,
            WIDEN,
            SHRINK,
            pltpu.VMEM((HALF, D), BF),
            pltpu.VMEM((2, 1, D), F32),
            pltpu.SemaphoreType.DMA((10,)),
        ],
        compiler_params=params(),
        cost_estimate=cost(8),
    )(scal, xw, mine, other, *arrays, wg)


def feed_back(index, scal, base, got, cot, cot_other, slope, smalls, owner, spread, group, wg):
    return pl.pallas_call(
        partial(feed_back_kernel, index),
        name=f"feed_back_{index}",
        out_shape=(
            shape((HALF, D), BF),
            shape((HALF, D), BF),
            shape((2, HALF, D), BF),
            shape((HALF, D), F32),
            shape((HALF, D), BF),
            shape((16, D), F32),
        ),
        in_specs=[SMEM] + [VM] * 9 + [HBM],
        out_specs=[VM] * 6,
        scratch_shapes=[WIDEN, SHRINK, pltpu.SemaphoreType.DMA((6,))],
        compiler_params=params(),
        cost_estimate=cost(7),
    )(scal, base, got, cot, cot_other, slope, smalls, owner, spread, group, wg)


def feed_close(index, scal, base, got, unit1, rstd1, sums, more, smalls, owner, spread, group, wg):
    return pl.pallas_call(
        feed_close_kernel,
        name=f"feed_close_{index}",
        out_shape=(
            shape((HALF, D), F32),
            shape((HALF, D), BF),
            shape((HALF, OWN), BF),
            shape((16, D), F32),
        ),
        in_specs=[SMEM] + [VM] * 10 + [HBM],
        out_specs=[VM] * 4,
        scratch_shapes=[MERGE, pltpu.SemaphoreType.DMA((4,))],
        compiler_params=params(),
        cost_estimate=cost(4),
    )(scal, base, got, unit1, rstd1, sums, more, smalls, owner, spread, group, wg)


def weight_grads(scal, *halves):
    return pl.pallas_call(
        weight_grad_kernel,
        name="weight_grads",
        out_shape=(shape((8, 192, D), BF), shape((8, 192, D), BF)),
        in_specs=[SMEM] + [VM] * 8,
        out_specs=[VM] * 2,
        scratch_shapes=[pltpu.VMEM((2 * D, D), F32), pltpu.VMEM((2, D, D), F32)],
        compiler_params=params(),
        cost_estimate=cost(7),
    )(scal, *halves)


def project_back(scal, parts, dh1, gathered):
    def kernel(scal, *refs):
        project_back_kernel(scal, refs[:4], refs[4:6], *refs[6:])

    return pl.pallas_call(
        kernel,
        name="project_back",
        out_shape=(shape((HALF, D), F32), shape((HALF, D), BF)),
        in_specs=[SMEM] + [VM] * 6 + [HBM],
        out_specs=[VM] * 2,
        scratch_shapes=[
            pltpu.VMEM((9, D, 128), BF),
            pltpu.VMEM((GROUP, 3 * OWN), BF),
            pltpu.SemaphoreType.DMA((16,)),
        ],
        compiler_params=params(),
        cost_estimate=cost(6),
    )(scal, *parts, *dh1, gathered)


def swap(value, axis, bit):
    count = lax.axis_size(axis)
    return lax.ppermute(value, axis, [(i, i ^ bit) for i in range(count)])


def shifted(value, axis, steps):
    count = lax.axis_size(axis)
    leading, last = (max(0, -steps), min(count, count - steps))
    return lax.ppermute(value, axis, [(source, source + steps) for source in range(leading, last)])


def tie(*values):
    return lax.optimization_barrier(values)


CORE, ALONG_Y, SIDE = ("fsdp", 1), ("fsdp", 2), ("seq", 1)


def along_z(values):
    groups = [[4 * z + i for z in range(4)] for i in range(4)]
    return lax.all_to_all(values, "fsdp", 0, 0, axis_index_groups=groups, tiled=True)


def add(mine, got):
    return (mine.astype(F32) + got.astype(F32)).astype(mine.dtype)


def by_core(value):
    return value.reshape(2, 4, *value.shape[1:])


def sum_core(keep, got):
    keep = by_core(keep)
    return add(keep[0], got[0]), add(keep[1], got[1])


def sum_z(got):
    return jnp.sum(got.astype(F32), axis=0).astype(got.dtype)


def in_order(flag, mine, other, axis):
    first = jnp.where(flag == 0, mine, other)
    second = jnp.where(flag == 0, other, mine)
    return jnp.concatenate([first, second], axis=axis)


def locate(index, opening, finish, stream_rows):
    document = jnp.sum((finish[None, :] <= index[:, None]).astype(jnp.int32), axis=1)
    begin = jnp.max(jnp.where(opening[None, :] <= index[:, None], opening[None, :], 0), axis=1)
    inside = (index >= 0) & (index < stream_rows)
    document = jnp.where(inside, document, -1)
    position = (index - begin) % MPOS
    return document, position


def own_columns(weight, nf, side, place):
    rows = weight.shape[0]
    weight = weight.reshape(rows, 3, 2, OWN)
    core = place % 2
    keep = lax.dynamic_index_in_dim(weight, side, 2, False).reshape(rows, 3 * OWN)
    give = lax.dynamic_index_in_dim(weight, 1 - side, 2, False).reshape(rows, 3 * OWN)
    straight, crossed, near = [], [], []
    for s in range(2):
        for f in range(nf):
            here = s * nf + f
            if f % 2 == s:
                straight.append((here, (1 - s) * nf + f))
            else:
                crossed.append((here, (1 - s) * nf + (f ^ 1)))
                near.append((here, s * nf + (f ^ 1)))
    axes = ("seq", "fsdp")
    same = core == side
    mine = jnp.where(same, keep, lax.ppermute(give, axes, straight))
    other = jnp.where(same, lax.ppermute(keep, axes, near), lax.ppermute(give, axes, crossed))
    return in_order(core, mine, other, 0)


def per_device(
    incoming_state,
    projection_matrix_triple,
    merge_matrix,
    widen_matrix,
    shrink_matrix,
    offset_table,
    norm_scales,
    widen_offset,
    trainable_gate_scores,
    gate_perturbation,
    softening_scale,
    passage_extents,
    result_cotangent,
):
    BOTH = ("seq", "fsdp")
    ns, nf = lax.axis_size("seq"), lax.axis_size("fsdp")
    count = ns * nf
    fast = nf == 16
    side, place = lax.axis_index("seq"), lax.axis_index("fsdp")
    tokens = incoming_state.reshape(HALF, D)
    cot = result_cotangent.reshape(HALF, D)
    stream_rows = GROUP * nf
    rows = projection_matrix_triple.shape[0]
    zero = jnp.zeros((), jnp.int32)
    core, unit = (place % 2, place // 2) if fast else (zero, zero)

    relaxed = jax.nn.sigmoid(
        (trainable_gate_scores + gate_perturbation) / softening_scale[:, None, None]
    )
    relaxed_low = relaxed.astype(BF)
    wide_cols, up_cols = D // count, FF // count
    pad_to = lambda value: jnp.pad(value, ((0, 0), (0, 128 - value.shape[1])))
    packed = jnp.concatenate(
        [
            pad_to(offset_table),
            pad_to(norm_scales),
            pad_to(widen_offset.reshape(1, up_cols)),
            jnp.zeros((7, 128), BF),
        ],
        axis=0,
    )
    lane, row = jnp.arange(D, dtype=jnp.int32)[None, :], jnp.arange(128, dtype=jnp.int32)[:, None]
    spread, group = (lane % wide_cols == row).astype(BF), lane // wide_cols
    spread_up, group_up = (lane % up_cols == row).astype(BF), lane // up_cols

    finish = jnp.cumsum(passage_extents)
    opening = finish - passage_extents
    base = place * GROUP - GROUP
    doc, pos = locate(base + jnp.arange(WINDOW, dtype=jnp.int32), opening, finish, stream_rows)
    edges = base + GROUP + jnp.asarray([0, HALF - 1, HALF, GROUP - 1], jnp.int32)
    edge_begin = jnp.max(jnp.where(opening[None, :] <= edges[:, None], opening[None, :], 0), axis=1)
    edge_end = jnp.min(
        jnp.where(finish[None, :] > edges[:, None], finish[None, :], stream_rows), axis=1
    )
    lows = jnp.clip((edge_begin - base) // CHUNK, 0, 6)
    highs = jnp.clip((edge_end - base + CHUNK - 1) // CHUNK, 0, 6)
    scal = jnp.stack(
        [unit, core, side, lows[0], highs[1], lows[2], highs[3], zero]
    ).astype(jnp.int32)
    before = shifted(tokens, "fsdp", 1)
    after = shifted(tokens, "fsdp", -1)
    other_tokens = swap(tokens, "seq", 1)
    if fast:
        halves = widen_matrix.reshape(rows, 2, FF // 2)
        keep = lax.dynamic_index_in_dim(halves, side, 1, False)
        give = lax.dynamic_index_in_dim(halves, 1 - side, 1, False)
        mine = jnp.concatenate([keep, merge_matrix], axis=1)[None]
        got = swap(jnp.concatenate([give, merge_matrix], axis=1)[None], *SIDE)
        wide = in_order(side, mine, got, 0)
        wide = jnp.concatenate(
            [wide[:, :, : FF // 2].reshape(2, rows, 2, D), wide[:, :, FF // 2 :].reshape(2, rows, 2, OWN)],
            axis=3,
        )
        mine = lax.dynamic_index_in_dim(wide, core, 2, False)
        sent = lax.dynamic_index_in_dim(wide, 1 - core, 2, False)
        wide = in_order(core, mine, swap(sent, *CORE), 1)
        shard = jnp.concatenate(
            [
                shrink_matrix,
                wide[:, :, :D].reshape(96, D),
                wide[:, :, D:].transpose(1, 0, 2).reshape(48, D),
            ],
            axis=0,
        )
        wq = own_columns(projection_matrix_triple, nf, side, place)
        pack = jnp.concatenate(
            [
                relaxed_low.reshape(6, 32, 4, 128).transpose(0, 2, 1, 3).reshape(768, 128),
                wq.reshape(48, 9, 128).transpose(1, 0, 2).reshape(432, 128),
                packed,
                jnp.zeros((32, 128), BF),
            ],
            axis=0,
        )
        gathered = lax.all_gather(pack, "fsdp", axis=0, tiled=True)
        other_tokens, before, after, scal, pos, doc = tie(
            other_tokens, before, after, scal, pos, doc
        )
        other_before = swap(before, *SIDE)
        other_after = swap(after, *SIDE)
        other_before, other_after, shard, cot = tie(other_before, other_after, shard, cot)
        wg = lax.all_gather(shard, "fsdp", axis=0, tiled=True).reshape(8, 2, 240, D)
        cot_other = swap(cot, *SIDE)
        cot_other, gathered = tie(cot_other, gathered)
        weights, table = gathered.reshape(16, 26, 48, 128), gathered.reshape(16, 39, 32, 128)
        near_owner = jnp.arange(nf, dtype=jnp.int32)[:, None]
        near = weights[:, 25, 0:16].transpose(1, 0, 2)
    else:
        other_before = swap(before, "seq", 1)
        other_after = swap(after, "seq", 1)
        full = lax.all_gather(projection_matrix_triple, BOTH, axis=0, tiled=True)
        full = lax.dynamic_index_in_dim(full.reshape(D, 3, 2, OWN), side, 2, False)
        full = full.reshape(2, 8, 48, 9, 128).transpose(1, 0, 3, 2, 4).reshape(16, 9, 48, 128)
        table = lax.all_gather(relaxed_low, "fsdp", axis=1, tiled=True)
        table = table.reshape(6, 16, 32, 4, 128).transpose(1, 0, 3, 2, 4).reshape(16, 24, 32, 128)
        weights = jnp.concatenate([table.reshape(16, 16, 48, 128), full], axis=1)
        smalls = lax.all_gather(packed[None], BOTH, axis=0, tiled=True).transpose(1, 0, 2)
        near = lax.dynamic_slice_in_dim(smalls, side * nf, nf, 1)
        near_owner = jnp.arange(nf, dtype=jnp.int32)[:, None]
        owner = jnp.arange(count, dtype=jnp.int32)[:, None]
        cot_other = swap(cot, *SIDE)
        up = lax.all_gather(widen_matrix, BOTH, axis=0, tiled=True)
        up = lax.dynamic_slice_in_dim(up, side * (FF // 2), FF // 2, 1)
        up = up.reshape(2, 8, 48, 2, D).transpose(1, 3, 0, 2, 4).reshape(8, 2, 96, D)
        down = lax.all_gather(shrink_matrix, "fsdp", axis=0, tiled=True).reshape(8, 2, 96, D)
        out = lax.all_gather(merge_matrix, BOTH, axis=0, tiled=True)
        out = out.reshape(2, 8, 48, 2, OWN).transpose(1, 3, 2, 0, 4).reshape(8, 2, 48, D)
        wg = jnp.concatenate([down, up, out], axis=2)

    pos_col, doc_col = pos.reshape(WINDOW, 1), doc.reshape(WINDOW, 1)
    pos_row, doc_row = pos.reshape(6, 1, CHUNK), doc.reshape(6, 1, CHUNK)
    pieces = (tokens, before, after, other_tokens, other_before, other_after)
    q, k, v, xw, k_turned, x_turned = project(scal, pieces, weights, near, near_owner, spread, group)
    if fast:
        far = swap(near, "seq", 1)
        smalls = jnp.concatenate([near, far], axis=1)
        owner = jnp.concatenate([side * nf + near_owner, (1 - side) * nf + near_owner], axis=0)
        q, smalls = tie(q, smalls)
    ctx, inverses, *kept = attend(scal, pos_col, pos_row, doc_col, doc_row, q, k, v, table)
    ctx_other = swap(ctx, *SIDE)
    params_of = (smalls, owner, spread, group, wg)
    up = lambda i: feed_up(
        i, scal, xw, ctx, ctx_other, smalls, owner, near, near_owner,
        (spread, group, spread_up, group_up), wg,
    )
    down = lambda i, base, got, slope: feed_back(
        i, scal, base, got, cot, cot_other, slope, *params_of
    )
    close = lambda i, base, got, unit, rstd, sums, more: feed_close(
        i, scal, base, got, unit, rstd, sums, more, *params_of
    )
    up0 = up(0)
    got0 = swap(up0[4], *SIDE)
    up1, got0 = tie(up(1), got0)
    got1 = swap(up1[4], *SIDE)
    down0, got1 = tie(down(0, up0[3], got0, up0[6]), got1)
    got0 = swap(down0[4], *SIDE)
    down1, got0 = tie(down(1, up1[3], got1, up1[6]), got0)
    got1 = swap(down1[4], *SIDE)
    closed0 = close(0, down0[3], got0, up0[0], up0[1], down0[5], down1[5])
    feed = weight_grads(
        scal, up0[5], down0[1], up0[2], down0[2], up1[5], down1[1], up1[2], down1[2]
    )
    closed0, feed, got1 = tie(closed0, feed, got1)
    if fast:
        feed_got = swap(by_core(feed[1]), *CORE)
    closed1 = close(1, down1[3], got1, up1[0], up1[1], closed0[3], jnp.zeros((16, D), F32))
    if fast:
        closed1, feed_got = tie(closed1, feed_got)
        feed = sum_core(feed[0], feed_got)
        feed_got = swap(feed[1], *ALONG_Y)
    dh1, dattn, dctx = [[c[i] for c in (closed0, closed1)] for i in range(3)]
    sums = closed1[3]
    lay = jnp.where(side == 0, down0[0], down1[0])
    back = lambda first, pairs, before: attend_back(
        first, pairs, before, scal, q, k_turned, v, kept, x_turned, sums, ctx, dctx, dattn, inverses
    )
    outs = back(0, 3, ())
    if fast:
        outs, feed_got = tie(outs, feed_got)
        feed = add(feed[0][:2], feed_got[:2]), add(feed[0][2:], feed_got[2:])
        outs, feed = tie(outs, feed)
    dq, own, low, high, *parts = outs

    own_cols = lambda values, at, size: lax.dynamic_slice_in_dim(values, at * size, size, 1)
    if fast:
        feed_got = swap(feed[1], "fsdp", 4)
        part_got = swap(by_core(parts[1]), *CORE)
        table_got = swap(by_core(parts[3]), *CORE)
        part_got, table_got = tie(part_got, table_got)
        part, table_part = sum_core(parts[0], part_got), sum_core(parts[2], table_got)
        part_got = swap(part[1], *ALONG_Y)
        feed = add(feed[0][0], feed_got[0]), add(feed[0][1], feed_got[1])
        feed_got = swap(feed[1], "fsdp", 8)
        part_got, feed_got, table_part, low, high = tie(
            part_got, feed_got, table_part, low, high
        )
        part_got = along_z(add(part[0], part_got))
        table_got = swap(table_part[1], *ALONG_Y)
        left, right = shifted(high, "fsdp", 1), shifted(low, "fsdp", -1)
        table_got, left, right = tie(table_got, left, right)
        table_got, left, right = tie(add(table_part[0], table_got), left, right)
        table_got = along_z(table_got)
        dx, dx_send = project_back(scal, (dq, own, left, right), dh1, weights)
        dx_got = swap(dx_send, *SIDE)
        shard = add(feed[0], feed_got)
        part = sum_z(part_got)
        table_total = sum_z(table_got)
        table_total = table_total.reshape(3, 2, 4, 32, 128).transpose(0, 1, 3, 2, 4)
        table_total = table_total.reshape(6, 32, MPOS).astype(F32)
        blocks = part.reshape(3, PART, 128)
        weight = blocks[:, :PART_SUMS].reshape(3, 3, 2, rows, 128).transpose(1, 0, 2, 3, 4)
        mine = lax.dynamic_index_in_dim(weight, side, 2, False)
        sent = lax.dynamic_index_in_dim(weight, 1 - side, 2, False)
        sums = blocks[:, PART_SUMS:PART_OUT].reshape(6, 16, 128)
        sums = sums.transpose(1, 0, 2).reshape(16, D).astype(F32)
        outs = blocks[:, PART_OUT:].reshape(6, rows, 128)
        grad_w_out = outs.transpose(1, 0, 2).reshape(rows, D).astype(F32)
        got = swap(sent.reshape(-1, 128), *SIDE)
        got = got.reshape(3, 3, rows, 128)
        mine = mine.transpose(2, 0, 1, 3).reshape(rows, 3, 1, OWN)
        got = got.transpose(2, 0, 1, 3).reshape(rows, 3, 1, OWN)
        grad_w_qkv = in_order(side, mine, got, 2).reshape(rows, 3 * D).astype(F32)
        head_sums = blocks[:, PART_TOTALS : PART_TOTALS + 2].transpose(1, 0, 2).reshape(2, OWN)
        head_sums = head_sums.astype(F32)
        head_grads = own_cols(head_sums, place, wide_cols)
        grad_w_down = shard[:96].astype(F32)
        wide = shard[96:192].reshape(2, 2, rows, D).transpose(0, 2, 1, 3).reshape(2, rows, FF // 2)
        mine = lax.dynamic_index_in_dim(wide, side, 0, False)
        got = swap(lax.dynamic_index_in_dim(wide, 1 - side, 0, False), *SIDE)
        grad_w_up = in_order(side, mine, got, 1).astype(F32)
    else:
        scatter = partial(lax.psum_scatter, axis_name=BOTH, scatter_dimension=0, tiled=True)
        left, right = shifted(high, "fsdp", 1), shifted(low, "fsdp", -1)
        dx, dx_send = project_back(scal, (dq, own, left, right), dh1, weights)
        dx_got = swap(dx_send, "seq", 1)

        def plain(pair, at=lambda u: 4 * (u & 1) + (u >> 1)):
            both = jnp.stack(pair, axis=1)
            return jnp.stack([both[at(u)] for u in range(8)], axis=0)

        blocks = plain(parts[:2]).reshape(8, 2, 3, PART, 128)
        table_grad = plain(parts[2:]).reshape(8, 2, 3, 2, 4, 32, 128).transpose(2, 3, 0, 1, 5, 4, 6)
        table_total = lax.psum_scatter(
            table_grad.reshape(6, MPOS, MPOS), "fsdp", scatter_dimension=1, tiled=True
        ).astype(F32)
        head_rows = blocks[:, :, :, :PART_SUMS].reshape(8, 2, 3, 3, 2, 24, 128)
        head_rows = head_rows.transpose(4, 0, 1, 5, 3, 2, 6).reshape(D, 3, 1, OWN)
        blank = jnp.zeros_like(head_rows)
        both = jnp.concatenate(
            [jnp.where(side == 0, head_rows, blank), jnp.where(side == 0, blank, head_rows)], axis=2
        )
        grad_w_qkv = scatter(both.reshape(D, 3 * D)).astype(F32)
        head_sums = blocks[0, 0, :, PART_TOTALS : PART_TOTALS + 2].transpose(1, 0, 2)
        head_sums = lax.psum(head_sums.reshape(2, OWN).astype(F32), "fsdp")
        head_grads = own_cols(head_sums, place, wide_cols)
        def placed(value, axis):
            blank = jnp.zeros_like(value)
            sides = [jnp.where(side == 0, value, blank), jnp.where(side == 0, blank, value)]
            return jnp.concatenate(sides, axis=axis)

        gg = plain(feed, lambda u: 4 * (u & 1) + (u & 2) + (u >> 2)).reshape(16, 192, D)
        grad_w_down = scatter(placed(gg[:, :96].reshape(FF // 2, D), 0)).astype(F32)
        up = gg[:, 96:192].reshape(16, 2, 2, 24, D).transpose(1, 0, 3, 2, 4).reshape(D, FF // 2)
        grad_w_up = scatter(placed(up, 1)).astype(F32)
        out = blocks[:, :, :, PART_OUT:].reshape(8, 2, 3, 2, 24, 128).transpose(0, 1, 4, 2, 3, 5)
        out = out.reshape(OWN, D)
        grad_w_out = scatter(placed(out, 0)).astype(F32)
        sums = lax.psum(sums, "fsdp")
    ours = own_cols(sums[:6], side * nf + place, wide_cols)
    grad_biases = jnp.concatenate([head_grads, ours[:4]], axis=0)
    grad_gains = ours[4:]
    grad_bias_up = lax.dynamic_slice_in_dim(
        sums[8:10].reshape(-1), place * up_cols, up_cols, 0
    )
    input_grad = dx + dx_got.astype(F32)
    mask_logit_gradient = (
        table_total * relaxed * (1.0 - relaxed) / softening_scale[:, None, None]
    )
    return (
        lay.reshape(1, HALF, D),
        input_grad.reshape(1, HALF, D),
        grad_w_qkv,
        grad_w_out,
        grad_w_up,
        grad_w_down,
        grad_biases,
        grad_gains,
        grad_bias_up,
        mask_logit_gradient,
    )


def solution(mesh):
    rows = P(("seq", "fsdp"), None)
    columns = P(None, ("seq", "fsdp"))
    block = P("fsdp", "seq", None)
    table = P("seq", "fsdp", None)
    return jax.shard_map(
        per_device,
        mesh=mesh,
        in_specs=(
            block, rows, rows, rows, rows, columns, columns, P(("seq", "fsdp")),
            table, table, P("seq"), P(), block,
        ),
        out_specs=(
            block, block, rows, rows, rows, rows, columns, columns, P(("seq", "fsdp")), table,
        ),
        check_vma=False,
    )
```

```python
from functools import partial

import jax
import jax.numpy as jnp
from jax import lax
from jax.experimental import pallas as pl
from jax.experimental.pallas import tpu as pltpu
from jax.sharding import PartitionSpec as P

D = 768
FF = 3072
HEADS = 12
HDIM = 64
MPOS = 512
EPS = 1e-05
GROUP = 512
HALF = 256
WINDOW = 3 * GROUP
OWN = 384
CHUNK = 256
NEG = -1e30
BF = jnp.bfloat16
F32 = jnp.float32
HIGH = lax.Precision.HIGHEST
PART_SUMS = 144
PART_TOTALS = PART_SUMS + 6
PART_OUT = 176
PART = 224
PART_TABLE = 256


def nn(left, right):
    return jnp.dot(left, right, preferred_element_type=F32)


def nt(left, right, precision=None):
    return lax.dot_general(
        left, right, (((1,), (1,)), ((), ())), precision=precision, preferred_element_type=F32
    )


def tn(left, right):
    return lax.dot_general(left, right, (((0,), (0,)), ((), ())), preferred_element_type=F32)


def load_projection(gathered, w, sem):
    copies = []
    for f in range(16):
        row = (f % 2) * OWN + (f // 2) * 48
        copies.append(
            pltpu.make_async_copy(gathered.at[f, 16:25], w.at[:, row : row + 48, :], sem.at[f])
        )
    for copy in copies:
        copy.start()
    return copies


def table_of(table, head):
    return jnp.concatenate(
        [table[:, 4 * head + part].reshape(MPOS, 128) for part in range(4)], axis=1
    )


def spread_out(values, spread, owner, group):
    return jnp.sum(jnp.where(owner == group, nn(values, spread), 0.0), axis=0, keepdims=True)


def columns_of(w, first, count=3):
    return jnp.concatenate([w[first + part] for part in range(count)], axis=1)


def place_of(t, cr, scal):
    unit = ((t >> 2) ^ (scal[0] & 1)) | ((t & 3) << 1)
    return 2 * unit + (scal[1] ^ cr)


def near_place_of(t, cr, scal):
    unit = ((t >> 2) | (t & 2) | ((t & 1) << 2)) ^ scal[0]
    return 2 * unit + (scal[1] ^ cr)


def project_kernel(
    scal,
    x1,
    x0,
    x2,
    y1,
    y0,
    y2,
    gathered,
    near,
    owner,
    spread,
    group,
    q_ref,
    k_ref,
    v_ref,
    xw,
    k_turned,
    x_turned,
    w,
    sem,
):
    copies = load_projection(gathered, w, sem)
    side = scal[2]
    for g, (mine, other) in enumerate(((x0, y0), (x1, y1), (x2, y2))):
        xw[pl.ds(pl.multiple_of(g * GROUP + side * HALF, HALF), HALF), :] = mine[...]
        xw[pl.ds(pl.multiple_of(g * GROUP + (1 - side) * HALF, HALF), HALF), :] = other[...]
    bias = [
        spread_out(near[i], spread[:, :OWN], owner[...], group[:, :OWN]) for i in range(2)
    ]
    for copy in copies:
        copy.wait()
    for blk in range(6):
        rows = slice(blk * HALF, (blk + 1) * HALF)
        here = xw[rows, :]
        key = nn(here, columns_of(w, 3))
        k_ref[rows, :] = key.astype(BF)
        k_turned[blk] = key.T.astype(BF)
        x_turned[:, rows] = here.astype(F32).T.astype(BF)
        v_ref[rows, :] = (nn(here, columns_of(w, 6)) + bias[1]).astype(BF)
        if blk in (2, 3):
            local = slice((blk - 2) * HALF, (blk - 1) * HALF)
            query = (nn(here, columns_of(w, 0)) + bias[0]).astype(BF)
            q_ref[local, :] = query * jnp.asarray(0.125, BF)


def head_lanes():
    return lax.broadcasted_iota(jnp.int32, (1, 128), 1) < HDIM


def fill_hot(pos_col, hot):
    for blk in range(6):
        rows = slice(blk * 256, (blk + 1) * 256)
        column = lax.broadcasted_iota(jnp.int32, (256, MPOS), 1)
        hot[rows, :] = jnp.where(pos_col[rows, :] == column, 1.0, 0.0).astype(BF)


def fill_hot_turned(pos_row, hot):
    for blk in range(6):
        rows = lax.broadcasted_iota(jnp.int32, (MPOS, 256), 0)
        hot[blk] = jnp.where(pos_row[blk] == rows, 1.0, 0.0).astype(BF)


def set_pair(low, value, target):
    blank = jnp.zeros_like(value)
    target[:HALF, :] = jnp.where(low, value, blank)
    target[HALF:, :] = jnp.where(low, blank, value)


def fold(values, how):
    rows, columns = values.shape
    return how(values.reshape(rows // 8, 8, columns), axis=0)


def attend_kernel(
    scal,
    pos_col,
    pos_row,
    doc_col,
    doc_row,
    q,
    k,
    v,
    table,
    ctx,
    inverses,
    weights,
    mixes,
    hot_turned,
    hot,
    sbuf,
    looks,
    queries,
    acc,
):
    @pl.when(pl.program_id(0) == 0)
    def _():
        fill_hot(pos_col, hot)
        fill_hot_turned(pos_row, hot_turned)

    low = head_lanes()
    for qb in range(2):
        lo, hi = scal[3 + 2 * qb], scal[4 + 2 * qb]
        here = slice(qb * HALF, (qb + 1) * HALF)
        set_pair(low, q[here, :], queries)
        q_doc = jnp.concatenate([doc_row[2 + qb]] * 2, axis=1)
        q_hot = hot[GROUP + qb * HALF : GROUP + (qb + 1) * HALF, :]
        for h in range(2):
            looks[h * HALF : (h + 1) * HALF, :] = nn(q_hot, table_of(table, h)).astype(BF)

        def score_step(c, top, q_doc=q_doc):
            rows = pl.ds(pl.multiple_of(c * CHUNK, CHUNK), CHUNK)
            s = jnp.where(doc_col[rows, :] == q_doc, nt(k[rows, :], queries[...]), NEG)
            sbuf[c] = s
            return jnp.maximum(top, fold(s, jnp.max))

        top = lax.fori_loop(lo, hi, score_step, jnp.full((8, 2 * HALF), NEG, F32))
        top = jnp.max(top, axis=0, keepdims=True)
        acc[...] = jnp.zeros_like(acc)

        def mix_step(c, total, top=top, qb=qb):
            rows = pl.ds(pl.multiple_of(c * CHUNK, CHUNK), CHUNK)
            e = jnp.exp(sbuf[c] - top)
            mixed = (e * nt(hot[rows, :], looks[...])).astype(BF)
            weights[0, qb, c] = e.astype(BF)
            mixes[0, qb, c] = mixed
            acc[...] += tn(mixed, v[rows, :])
            return total + fold(e, jnp.sum)

        total = lax.fori_loop(lo, hi, mix_step, jnp.zeros((8, 2 * HALF), F32))
        total = jnp.sum(total, axis=0, keepdims=True)
        inverse = 1.0 / total
        inverses[0, 0:1, here] = inverse[:, :HALF]
        inverses[0, 1:2, here] = inverse[:, HALF:]
        inverses[0, 2:8, here] = jnp.zeros((6, HALF), F32)
        scale = jnp.concatenate(
            [
                jnp.broadcast_to(inverse[:, :HALF], (HDIM, HALF)),
                jnp.broadcast_to(inverse[:, HALF:], (HDIM, HALF)),
            ],
            axis=0,
        ).T
        ctx[qb] = (jnp.where(low, acc[:HALF, :], acc[HALF:, :]) * scale).astype(BF)


def attend_back_kernel(
    carried,
    scal,
    q,
    k,
    v,
    weights,
    mixes,
    hot_turned,
    xw,
    sums,
    ctx,
    ctx_all,
    dctx0,
    dctx1,
    dattn0,
    dattn1,
    inverses,
    *refs,
):
    outs = refs[carried : carried + 8]
    dq, own, halo_low, halo_high, part_keep, part_send, table_keep, table_send = outs
    queries, grads, dk, dv, dq_acc, tt, tg, gw, gout = refs[carried + 8 :]
    low = head_lanes()
    dk[...] = jnp.zeros_like(dk)
    dv[...] = jnp.zeros_like(dv)
    lane = lax.broadcasted_iota(jnp.int32, (8, 128), 1)
    row8 = lax.broadcasted_iota(jnp.int32, (8, 128), 0)
    pick = jnp.where((lane < HDIM) == (row8 == 0), 1.0, 0.0)
    for qb in range(2):
        lo, hi = scal[3 + 2 * qb], scal[4 + 2 * qb]
        here = slice(qb * HALF, (qb + 1) * HALF)
        inverse = inverses[0, 0:2, here]
        d_pair = (dctx0, dctx1)[qb][...].astype(F32)
        deltas = nt(pick, d_pair * ctx[qb].astype(F32), HIGH)[0:2, :] * inverse
        delta = jnp.concatenate([deltas[0:1, :], deltas[1:2, :]], axis=1)
        scale = jnp.concatenate(
            [
                jnp.broadcast_to(inverse[0:1, :], (HDIM, HALF)),
                jnp.broadcast_to(inverse[1:2, :], (HDIM, HALF)),
            ],
            axis=0,
        ).T
        set_pair(low, q[here, :], queries)
        set_pair(low, (d_pair * scale).astype(BF), grads)
        dq_acc[...] = jnp.zeros_like(dq_acc)
        tt[...] = jnp.zeros_like(tt)

        def step(c, carry, delta=delta, qb=qb):
            rows = pl.ds(pl.multiple_of(c * CHUNK, CHUNK), CHUNK)
            mixed = mixes[0, qb, c]
            e = weights[0, qb, c].astype(F32)
            dm = nt(v[rows, :], grads[...])
            ds = (mixed.astype(F32) * dm - e * delta).astype(BF)
            dv[rows, :] += nn(mixed, grads[...])
            dk[rows, :] += nn(ds, queries[...])
            dq_acc[...] += nn(k[c], ds)
            tt[...] += nn(hot_turned[c], (e * dm).astype(BF))
            return carry

        lax.fori_loop(lo, hi, step, 0)
        for h in range(2):
            piece = nt(hot_turned[2 + qb], tt[:, h * HALF : (h + 1) * HALF].astype(BF))
            if qb == 0:
                tg[h] = piece
            else:
                tg[h] += piece
        both = jnp.concatenate([dq_acc[:HDIM, :HALF], dq_acc[HDIM:, HALF:]], axis=0)
        dq[here, :] = (both.T * 0.125).astype(BF)
    own[0] = dk[GROUP : 2 * GROUP, :]
    own[1] = dv[GROUP : 2 * GROUP, :]
    halo_low[0] = dk[:GROUP, :].astype(BF)
    halo_low[1] = dv[:GROUP, :].astype(BF)
    halo_high[0] = dk[2 * GROUP :, :].astype(BF)
    halo_high[1] = dv[2 * GROUP :, :].astype(BF)
    query_grad = dq[...]
    pair_grad = jnp.concatenate([dk[...].astype(BF), dv[...].astype(BF)], axis=1)
    gw[:, 0:128] = nn(xw[:, GROUP : 2 * GROUP], query_grad)
    gw[:, 128:384] = nn(xw[...], pair_grad)
    gout[...] = tn(ctx_all[0], dattn0[...]) + tn(ctx_all[1], dattn1[...])
    totals = jnp.concatenate(
        [
            sums[0:6, 0:128],
            column_sum(query_grad.astype(F32)),
            column_sum(pair_grad[:, 128:].astype(F32)),
            sums[8:16, 0:128],
            sums[:, 128:256],
        ],
        axis=0,
    ).astype(BF)
    for cr in range(2):
        out, table = (part_keep, table_keep) if cr == 0 else (part_send, table_send)
        for t in range(8):
            place = place_of(t, cr, scal)
            rows = [
                gw[pl.ds(pl.multiple_of(part * OWN + place * 24, 8), 24), :] for part in range(2)
            ]
            both = jnp.concatenate(rows, axis=0).astype(BF)
            for i in range(3):
                out[t, i * 48 : i * 48 + 48, :] = both[:, i * 128 : (i + 1) * 128]
            out[t, PART_SUMS:PART_OUT, :] = totals
            rows = gout[pl.ds(pl.multiple_of(place * 24, 8), 24), :]
            out[t, PART_OUT:PART, :] = jnp.concatenate(
                [rows[:, 0:128], rows[:, 128:256]], axis=0
            ).astype(BF)
            for h in range(2):
                mask = tg[h, pl.ds(pl.multiple_of(place * 32, 32), 32), :].astype(BF)
                for i in range(4):
                    at = (4 * h + i) * 32
                    table[t, at : at + 32, :] = mask[:, i * 128 : (i + 1) * 128]


def norm_stats(values):
    center = values - jnp.mean(values, axis=-1, keepdims=True)
    rstd = lax.rsqrt(jnp.mean(center * center, axis=-1, keepdims=True) + EPS)
    return center * rstd, rstd


def norm_back(grad, unit, rstd, gain):
    scaled = grad * gain
    return rstd * (
        scaled
        - jnp.mean(scaled, axis=-1, keepdims=True)
        - unit * jnp.mean(scaled * unit, axis=-1, keepdims=True)
    )


def column_sum(values):
    return jnp.sum(values, axis=0, keepdims=True)


def load_feed(wg, sem, wm=None, wu=None, wd=None):
    copies = []

    def bring(source, target):
        copies.append(pltpu.make_async_copy(source, target, sem.at[len(copies)]))
        copies[-1].start()

    for c in range(2):
        for s in range(2):
            if wm is not None:
                bring(
                    wg.at[:, c, 192:240, s * OWN : (s + 1) * OWN],
                    wm.at[s, :, :, c * OWN : (c + 1) * OWN],
                )
    for c in range(2):
        for s in range(2):
            if wu is not None:
                bring(wg.at[:, c, 96 + 48 * s : 144 + 48 * s, :], wu.at[c, s])
    for c in range(2):
        if wd is not None:
            bring(wg.at[:, c, 0:96, :], wd.at[:, c])
    return copies


def shrink_rows(wd, i):
    return wd[pl.ds(4 * i, 4)].reshape(D, D)


def wait_for(copies):
    for copy in copies:
        copy.wait()


def feed_up_kernel(
    scal,
    x,
    ctx_mine,
    ctx_other,
    smalls,
    owner,
    near,
    near_owner,
    spread,
    group,
    spread_up,
    group_up,
    wg,
    unit1,
    rstd1,
    nlow,
    base,
    send,
    act,
    slope,
    wm,
    wu,
    wd,
    ctxt,
    bup,
    sem,
):
    copies = load_feed(wg, sem, wm, wu, wd)
    vector = lambda i: spread_out(smalls[i], spread[...], owner[...], group[...])
    bias_out, bias_down, shift1, gain1 = [vector(i) for i in (2, 3, 4, 6)]
    for n in range(2):
        bup[n] = spread_out(
            near[8], spread_up[...], near_owner[...], group_up[...] + n * (near.shape[1] // 2)
        )
    even = scal[2] == 0
    mine, other = ctx_mine[0], ctx_other[0]
    ctxt[:, :OWN] = jnp.where(even, mine, other)
    ctxt[:, OWN:] = jnp.where(even, other, mine)
    wait_for(copies[:4])
    attn = nn(ctxt[...], wm[...].reshape(D, D)) + bias_out
    unit, rstd = norm_stats(x[...].astype(F32) + attn)
    unit1[...] = unit
    rstd1[...] = jnp.broadcast_to(rstd, (HALF, 128))
    normed = unit * gain1 + shift1
    nlow[...] = normed.astype(BF)
    base[...] = normed + bias_down
    wait_for(copies[4:8])

    def widen(n, carry):
        up = nn(nlow[...], wu[n].reshape(D, D)) + bup[n]
        half_cdf = 0.5 * (1.0 + lax.erf(up * 0.7071067811865476))
        act[n] = (up * half_cdf).astype(BF)
        slope[n] = half_cdf + up * (0.3989422804014327 * jnp.exp(-0.5 * up * up))
        return carry

    lax.fori_loop(0, 2, widen, 0)
    wait_for(copies[8:])
    part = nn(act[0], shrink_rows(wd, 0)) + nn(act[1], shrink_rows(wd, 1))
    base[...] += part
    send[...] = part.astype(BF)


def feed_back_kernel(
    index,
    scal,
    base,
    got,
    cot_mine,
    cot_other,
    slope,
    smalls,
    owner,
    spread,
    group,
    wg,
    lay,
    ddown,
    dup,
    base2,
    send,
    sums,
    wu,
    wd,
    sem,
):
    copies = load_feed(wg, sem, None, wu, wd)
    vector = lambda i: spread_out(smalls[i], spread[...], owner[...], group[...])
    shift2, gain2 = vector(5), vector(7)
    sums[...] = jnp.zeros_like(sums)
    unit, rstd = norm_stats(base[...] + got[...].astype(F32))
    lay[...] = (unit * gain2 + shift2).astype(BF)
    dy = jnp.where(scal[2] == index, cot_mine[...], cot_other[...]).astype(F32)
    sums[3:4, :] = column_sum(dy)
    sums[5:6, :] = column_sum(dy * unit)
    grad = norm_back(dy, unit, rstd, gain2)
    ddown[...] = grad.astype(BF)
    sums[1:2, :] = column_sum(ddown[...].astype(F32))
    base2[...] = grad
    wait_for(copies[4:])

    def back(n, carry):
        low = (nt(ddown[...], shrink_rows(wd, n)) * slope[n]).astype(BF)
        dup[n] = low
        sums[pl.ds(8 + n, 1), :] = column_sum(low.astype(F32))
        return carry

    lax.fori_loop(0, 2, back, 0)
    wait_for(copies[:4])
    part = nt(dup[0], wu[0].reshape(D, D)) + nt(dup[1], wu[1].reshape(D, D))
    base2[...] += part
    send[...] = part.astype(BF)


def feed_close_kernel(
    scal,
    base,
    got,
    unit1,
    rstd1,
    sums_in,
    sums_more,
    smalls,
    owner,
    spread,
    group,
    wg,
    dh1,
    dattn,
    dctx,
    sums,
    wm,
    sem,
):
    copies = load_feed(wg, sem, wm)
    gain1 = spread_out(smalls[6], spread[...], owner[...], group[...])
    sums[...] = sums_in[...] + sums_more[...]
    grad = base[...] + got[...].astype(F32)
    unit = unit1[...]
    sums[2:3, :] += column_sum(grad)
    sums[4:5, :] += column_sum(grad * unit)
    grad = norm_back(grad, unit, rstd1[:, 0:1], gain1)
    dh1[...] = grad
    dattn[...] = grad.astype(BF)
    sums[0:1, :] += column_sum(dattn[...].astype(F32))
    wait_for(copies)
    dctx[...] = nt(dattn[...], wm[scal[2]].reshape(OWN, D)).astype(BF)


def weight_grad_kernel(
    scal, act0, ddown0, nlow0, dup0, act1, ddown1, nlow1, dup1, keep, send, down, up
):
    for n in range(2):
        up[n] = tn(nlow0[...], dup0[n]) + tn(nlow1[...], dup1[n])
        down[n * D : (n + 1) * D, :] = tn(act0[n], ddown0[...]) + tn(act1[n], ddown1[...])
    for cr, out in enumerate((keep, send)):
        for t in range(8):
            place = near_place_of(t, cr, scal)
            out[t, 0:96, :] = down[pl.ds(pl.multiple_of(place * 96, 8), 96), :].astype(BF)
            parts = [
                up[n, pl.ds(pl.multiple_of(s * OWN + place * 24, 8), 24), :]
                for s in range(2)
                for n in range(2)
            ]
            out[t, 96:192, :] = jnp.concatenate(parts, axis=0).astype(BF)


def project_back_kernel(scal, parts, dh1s, gathered, dx, dx_send, w, dqkv, sem):
    copies = load_projection(gathered, w, sem)
    dq, own, left, right = parts
    dqkv[:, :OWN] = dq[...]
    for i in range(2):
        total = own[i] + left[i].astype(F32) + right[i].astype(F32)
        dqkv[:, (1 + i) * OWN : (2 + i) * OWN] = total.astype(BF)
    for copy in copies:
        copy.wait()
    side = scal[2]
    mine = dqkv[pl.ds(pl.multiple_of(side * HALF, HALF), HALF), :]
    other = dqkv[pl.ds(pl.multiple_of((1 - side) * HALF, HALF), HALF), :]
    for part in range(3):
        cols = slice(part * 256, (part + 1) * 256)
        rows = jnp.concatenate([w[j, cols, :] for j in range(9)], axis=1)
        dh1 = jnp.where(side == 0, dh1s[0][:, cols], dh1s[1][:, cols])
        dx[:, cols] = dh1 + nt(mine, rows)
        dx_send[:, cols] = nt(other, rows).astype(BF)


SMEM = pl.BlockSpec(memory_space=pltpu.SMEM)
VM = pl.BlockSpec()
HBM = pl.BlockSpec(memory_space=pl.ANY)


def params():
    return pltpu.CompilerParams(vmem_limit_bytes=60 * 1024 * 1024)


def cost(microseconds):
    return pl.CostEstimate(
        flops=int(microseconds * 1.15e9), bytes_accessed=1000, transcendentals=0
    )


def shape(dims, kind):
    return jax.ShapeDtypeStruct(dims, kind)


def project(scal, pieces, gathered, near, owner, spread, group):
    return pl.pallas_call(
        project_kernel,
        name="project",
        out_shape=(
            shape((GROUP, OWN), BF),
            shape((WINDOW, OWN), BF),
            shape((WINDOW, OWN), BF),
            shape((WINDOW, D), BF),
            shape((6, OWN, CHUNK), BF),
            shape((D, WINDOW), BF),
        ),
        in_specs=[SMEM] + [VM] * 6 + [HBM] + [VM] * 4,
        out_specs=[VM] * 6,
        scratch_shapes=[
            pltpu.VMEM((9, D, 128), BF),
            pltpu.SemaphoreType.DMA((16,)),
        ],
        compiler_params=params(),
        cost_estimate=cost(9),
    )(scal, *pieces, gathered, near, owner, spread, group)


def whole(*dims):
    return pl.BlockSpec(dims, lambda p: (0,) * len(dims))


def attend(scal, pos_col, pos_row, doc_col, doc_row, q, k, v, table):
    return pl.pallas_call(
        attend_kernel,
        name="attend",
        grid=(3,),
        out_shape=(
            shape((2, HALF, OWN), BF),
            shape((3, 8, GROUP), F32),
            shape((3, 2, 6, CHUNK, 2 * HALF), BF),
            shape((3, 2, 6, CHUNK, 2 * HALF), BF),
            shape((6, MPOS, CHUNK), BF),
        ),
        in_specs=[
            SMEM,
            whole(WINDOW, 1),
            whole(6, 1, CHUNK),
            whole(WINDOW, 1),
            whole(6, 1, CHUNK),
            pl.BlockSpec((GROUP, 128), lambda p: (0, p)),
            pl.BlockSpec((WINDOW, 128), lambda p: (0, p)),
            pl.BlockSpec((WINDOW, 128), lambda p: (0, p)),
            pl.BlockSpec((16, 8, 32, 128), lambda p: (0, p, 0, 0)),
        ],
        out_specs=[
            pl.BlockSpec((2, HALF, 128), lambda p: (0, 0, p)),
            pl.BlockSpec((1, 8, GROUP), lambda p: (p, 0, 0)),
            pl.BlockSpec((1, 2, 6, CHUNK, 2 * HALF), lambda p: (p, 0, 0, 0, 0)),
            pl.BlockSpec((1, 2, 6, CHUNK, 2 * HALF), lambda p: (p, 0, 0, 0, 0)),
            whole(6, MPOS, CHUNK),
        ],
        scratch_shapes=[
            pltpu.VMEM((WINDOW, MPOS), BF),
            pltpu.VMEM((6, CHUNK, 2 * HALF), F32),
            pltpu.VMEM((2 * HALF, MPOS), BF),
            pltpu.VMEM((2 * HALF, 128), BF),
            pltpu.VMEM((2 * HALF, 128), F32),
        ],
        compiler_params=params(),
        cost_estimate=cost(26),
    )(scal, pos_col, pos_row, doc_col, doc_row, q, k, v, table)


def attend_back(
    first, pairs, before, scal, q, k, v, kept, xw, sums, ctx, dctx, dattn, inverses
):
    columns = lambda rows: pl.BlockSpec((rows, 128), lambda p: (0, first + p))
    tiles = pl.BlockSpec((1, 2, 6, CHUNK, 2 * HALF), lambda p: (first + p, 0, 0, 0, 0))
    blocks = lambda rows: pl.BlockSpec((8, rows, 128), lambda p: (0, first + p, 0))
    both = pl.BlockSpec((2, GROUP, 128), lambda p: (0, 0, first + p))
    return pl.pallas_call(
        partial(attend_back_kernel, len(before)),
        name=f"attend_back_{first}",
        grid=(pairs,),
        input_output_aliases={16 + i: i for i in range(len(before))},
        out_shape=(
            shape((GROUP, OWN), BF),
            shape((2, GROUP, OWN), F32),
            shape((2, GROUP, OWN), BF),
            shape((2, GROUP, OWN), BF),
            shape((8, 3 * PART, 128), BF),
            shape((8, 3 * PART, 128), BF),
            shape((8, 3 * PART_TABLE, 128), BF),
            shape((8, 3 * PART_TABLE, 128), BF),
        ),
        in_specs=[
            SMEM,
            columns(GROUP),
            pl.BlockSpec((6, 128, CHUNK), lambda p: (0, first + p, 0)),
            columns(WINDOW),
            tiles,
            tiles,
            whole(6, MPOS, CHUNK),
            whole(D, WINDOW),
            pl.BlockSpec((16, 256), lambda p: (0, first + p)),
            pl.BlockSpec((2, HALF, 128), lambda p: (0, 0, first + p)),
            whole(2, HALF, OWN),
            columns(HALF),
            columns(HALF),
            pl.BlockSpec((HALF, 256), lambda p: (0, first + p)),
            pl.BlockSpec((HALF, 256), lambda p: (0, first + p)),
            pl.BlockSpec((1, 8, GROUP), lambda p: (first + p, 0, 0)),
        ]
        + [HBM] * len(before),
        out_specs=[
            columns(GROUP),
            both,
            both,
            both,
            blocks(PART),
            blocks(PART),
            blocks(PART_TABLE),
            blocks(PART_TABLE),
        ],
        scratch_shapes=[
            pltpu.VMEM((2 * HALF, 128), BF),
            pltpu.VMEM((2 * HALF, 128), BF),
            pltpu.VMEM((WINDOW, 128), F32),
            pltpu.VMEM((WINDOW, 128), F32),
            pltpu.VMEM((128, 2 * HALF), F32),
            pltpu.VMEM((MPOS, 2 * HALF), F32),
            pltpu.VMEM((2, MPOS, MPOS), F32),
            pltpu.VMEM((D, OWN), F32),
            pltpu.VMEM((OWN, 256), F32),
        ],
        compiler_params=params(),
        cost_estimate=cost(10 * pairs),
    )(scal, q, k, v, *kept, xw, sums, ctx, ctx, *dctx, *dattn, inverses, *before)


WIDEN = pltpu.VMEM((2, 2, 8, 48, D), BF)
SHRINK = pltpu.VMEM((8, 2, 96, D), BF)
MERGE = pltpu.VMEM((2, 8, 48, D), BF)


def feed_up(index, scal, xw, mine, other, smalls, owner, near, near_owner, spreads, wg):
    arrays = (smalls, owner, near, near_owner, *spreads)
    ctx = pl.BlockSpec((1, HALF, OWN), lambda p: (index, 0, 0))
    outs = (
        shape((HALF, D), F32),
        shape((HALF, 128), F32),
        shape((HALF, D), BF),
        shape((HALF, D), F32),
        shape((HALF, D), BF),
        shape((2, HALF, D), BF),
        shape((2, HALF, D), F32),
    )
    return pl.pallas_call(
        feed_up_kernel,
        name=f"feed_up_{index}",
        grid=(1,),
        out_shape=outs,
        in_specs=[SMEM, pl.BlockSpec((HALF, D), lambda p: (2 + index, 0)), ctx, ctx]
        + [whole(*a.shape) for a in arrays]
        + [HBM],
        out_specs=[whole(*out.shape) for out in outs],
        scratch_shapes=[
            MERGE,
            WIDEN,
            SHRINK,
            pltpu.VMEM((HALF, D), BF),
            pltpu.VMEM((2, 1, D), F32),
            pltpu.SemaphoreType.DMA((10,)),
        ],
        compiler_params=params(),
        cost_estimate=cost(8),
    )(scal, xw, mine, other, *arrays, wg)


def feed_back(index, scal, base, got, cot, cot_other, slope, smalls, owner, spread, group, wg):
    return pl.pallas_call(
        partial(feed_back_kernel, index),
        name=f"feed_back_{index}",
        out_shape=(
            shape((HALF, D), BF),
            shape((HALF, D), BF),
            shape((2, HALF, D), BF),
            shape((HALF, D), F32),
            shape((HALF, D), BF),
            shape((16, D), F32),
        ),
        in_specs=[SMEM] + [VM] * 9 + [HBM],
        out_specs=[VM] * 6,
        scratch_shapes=[WIDEN, SHRINK, pltpu.SemaphoreType.DMA((6,))],
        compiler_params=params(),
        cost_estimate=cost(7),
    )(scal, base, got, cot, cot_other, slope, smalls, owner, spread, group, wg)


def feed_close(index, scal, base, got, unit1, rstd1, sums, more, smalls, owner, spread, group, wg):
    return pl.pallas_call(
        feed_close_kernel,
        name=f"feed_close_{index}",
        out_shape=(
            shape((HALF, D), F32),
            shape((HALF, D), BF),
            shape((HALF, OWN), BF),
            shape((16, D), F32),
        ),
        in_specs=[SMEM] + [VM] * 10 + [HBM],
        out_specs=[VM] * 4,
        scratch_shapes=[MERGE, pltpu.SemaphoreType.DMA((4,))],
        compiler_params=params(),
        cost_estimate=cost(4),
    )(scal, base, got, unit1, rstd1, sums, more, smalls, owner, spread, group, wg)


def weight_grads(scal, *halves):
    return pl.pallas_call(
        weight_grad_kernel,
        name="weight_grads",
        out_shape=(shape((8, 192, D), BF), shape((8, 192, D), BF)),
        in_specs=[SMEM] + [VM] * 8,
        out_specs=[VM] * 2,
        scratch_shapes=[pltpu.VMEM((2 * D, D), F32), pltpu.VMEM((2, D, D), F32)],
        compiler_params=params(),
        cost_estimate=cost(7),
    )(scal, *halves)


def project_back(scal, parts, dh1, gathered):
    def kernel(scal, *refs):
        project_back_kernel(scal, refs[:4], refs[4:6], *refs[6:])

    return pl.pallas_call(
        kernel,
        name="project_back",
        out_shape=(shape((HALF, D), F32), shape((HALF, D), BF)),
        in_specs=[SMEM] + [VM] * 6 + [HBM],
        out_specs=[VM] * 2,
        scratch_shapes=[
            pltpu.VMEM((9, D, 128), BF),
            pltpu.VMEM((GROUP, 3 * OWN), BF),
            pltpu.SemaphoreType.DMA((16,)),
        ],
        compiler_params=params(),
        cost_estimate=cost(6),
    )(scal, *parts, *dh1, gathered)


def swap(value, axis, bit):
    count = lax.axis_size(axis)
    return lax.ppermute(value, axis, [(i, i ^ bit) for i in range(count)])


def shifted(value, axis, steps):
    count = lax.axis_size(axis)
    leading, last = (max(0, -steps), min(count, count - steps))
    return lax.ppermute(value, axis, [(source, source + steps) for source in range(leading, last)])


def tie(*values):
    return lax.optimization_barrier(values)


CORE, ALONG_Y, SIDE = ("fsdp", 1), ("fsdp", 2), ("seq", 1)


def along_z(values):
    groups = [[4 * z + i for z in range(4)] for i in range(4)]
    return lax.all_to_all(values, "fsdp", 0, 0, axis_index_groups=groups, tiled=True)


def add(mine, got):
    return (mine.astype(F32) + got.astype(F32)).astype(mine.dtype)


def by_core(value):
    return value.reshape(2, 4, *value.shape[1:])


def sum_core(keep, got):
    keep = by_core(keep)
    return add(keep[0], got[0]), add(keep[1], got[1])


def sum_z(got):
    return jnp.sum(got.astype(F32), axis=0).astype(got.dtype)


def in_order(flag, mine, other, axis):
    first = jnp.where(flag == 0, mine, other)
    second = jnp.where(flag == 0, other, mine)
    return jnp.concatenate([first, second], axis=axis)


def locate(index, opening, finish, stream_rows):
    document = jnp.sum((finish[None, :] <= index[:, None]).astype(jnp.int32), axis=1)
    begin = jnp.max(jnp.where(opening[None, :] <= index[:, None], opening[None, :], 0), axis=1)
    inside = (index >= 0) & (index < stream_rows)
    document = jnp.where(inside, document, -1)
    position = (index - begin) % MPOS
    return document, position


def own_columns(weight, nf, side, place):
    rows = weight.shape[0]
    weight = weight.reshape(rows, 3, 2, OWN)
    core = place % 2
    keep = lax.dynamic_index_in_dim(weight, side, 2, False).reshape(rows, 3 * OWN)
    give = lax.dynamic_index_in_dim(weight, 1 - side, 2, False).reshape(rows, 3 * OWN)
    straight, crossed, near = [], [], []
    for s in range(2):
        for f in range(nf):
            here = s * nf + f
            if f % 2 == s:
                straight.append((here, (1 - s) * nf + f))
            else:
                crossed.append((here, (1 - s) * nf + (f ^ 1)))
                near.append((here, s * nf + (f ^ 1)))
    axes = ("seq", "fsdp")
    same = core == side
    mine = jnp.where(same, keep, lax.ppermute(give, axes, straight))
    other = jnp.where(same, lax.ppermute(keep, axes, near), lax.ppermute(give, axes, crossed))
    return in_order(core, mine, other, 0)


def per_device(
    incoming_state,
    projection_matrix_triple,
    merge_matrix,
    widen_matrix,
    shrink_matrix,
    offset_table,
    norm_scales,
    widen_offset,
    trainable_gate_scores,
    gate_perturbation,
    softening_scale,
    passage_extents,
    result_cotangent,
):
    BOTH = ("seq", "fsdp")
    ns, nf = lax.axis_size("seq"), lax.axis_size("fsdp")
    count = ns * nf
    fast = nf == 16
    side, place = lax.axis_index("seq"), lax.axis_index("fsdp")
    tokens = incoming_state.reshape(HALF, D)
    cot = result_cotangent.reshape(HALF, D)
    stream_rows = GROUP * nf
    rows = projection_matrix_triple.shape[0]
    zero = jnp.zeros((), jnp.int32)
    core, unit = (place % 2, place // 2) if fast else (zero, zero)

    relaxed = jax.nn.sigmoid(
        (trainable_gate_scores + gate_perturbation) / softening_scale[:, None, None]
    )
    relaxed_low = relaxed.astype(BF)
    wide_cols, up_cols = D // count, FF // count
    pad_to = lambda value: jnp.pad(value, ((0, 0), (0, 128 - value.shape[1])))
    packed = jnp.concatenate(
        [
            pad_to(offset_table),
            pad_to(norm_scales),
            pad_to(widen_offset.reshape(1, up_cols)),
            jnp.zeros((7, 128), BF),
        ],
        axis=0,
    )
    lane, row = jnp.arange(D, dtype=jnp.int32)[None, :], jnp.arange(128, dtype=jnp.int32)[:, None]
    spread, group = (lane % wide_cols == row).astype(BF), lane // wide_cols
    spread_up, group_up = (lane % up_cols == row).astype(BF), lane // up_cols

    finish = jnp.cumsum(passage_extents)
    opening = finish - passage_extents
    base = place * GROUP - GROUP
    doc, pos = locate(base + jnp.arange(WINDOW, dtype=jnp.int32), opening, finish, stream_rows)
    edges = base + GROUP + jnp.asarray([0, HALF - 1, HALF, GROUP - 1], jnp.int32)
    edge_begin = jnp.max(jnp.where(opening[None, :] <= edges[:, None], opening[None, :], 0), axis=1)
    edge_end = jnp.min(
        jnp.where(finish[None, :] > edges[:, None], finish[None, :], stream_rows), axis=1
    )
    lows = jnp.clip((edge_begin - base) // CHUNK, 0, 6)
    highs = jnp.clip((edge_end - base + CHUNK - 1) // CHUNK, 0, 6)
    scal = jnp.stack(
        [unit, core, side, lows[0], highs[1], lows[2], highs[3], zero]
    ).astype(jnp.int32)
    before = shifted(tokens, "fsdp", 1)
    after = shifted(tokens, "fsdp", -1)
    other_tokens = swap(tokens, "seq", 1)
    if fast:
        halves = widen_matrix.reshape(rows, 2, FF // 2)
        keep = lax.dynamic_index_in_dim(halves, side, 1, False)
        give = lax.dynamic_index_in_dim(halves, 1 - side, 1, False)
        mine = jnp.concatenate([keep, merge_matrix], axis=1)[None]
        got = swap(jnp.concatenate([give, merge_matrix], axis=1)[None], *SIDE)
        wide = in_order(side, mine, got, 0)
        wide = jnp.concatenate(
            [wide[:, :, : FF // 2].reshape(2, rows, 2, D), wide[:, :, FF // 2 :].reshape(2, rows, 2, OWN)],
            axis=3,
        )
        mine = lax.dynamic_index_in_dim(wide, core, 2, False)
        sent = lax.dynamic_index_in_dim(wide, 1 - core, 2, False)
        wide = in_order(core, mine, swap(sent, *CORE), 1)
        shard = jnp.concatenate(
            [
                shrink_matrix,
                wide[:, :, :D].reshape(96, D),
                wide[:, :, D:].transpose(1, 0, 2).reshape(48, D),
            ],
            axis=0,
        )
        wq = own_columns(projection_matrix_triple, nf, side, place)
        pack = jnp.concatenate(
            [
                relaxed_low.reshape(6, 32, 4, 128).transpose(0, 2, 1, 3).reshape(768, 128),
                wq.reshape(48, 9, 128).transpose(1, 0, 2).reshape(432, 128),
                packed,
                jnp.zeros((32, 128), BF),
            ],
            axis=0,
        )
        gathered = lax.all_gather(pack, "fsdp", axis=0, tiled=True)
        other_tokens, before, after, scal, pos, doc = tie(
            other_tokens, before, after, scal, pos, doc
        )
        other_before = swap(before, *SIDE)
        other_after = swap(after, *SIDE)
        other_before, other_after, shard, cot = tie(other_before, other_after, shard, cot)
        wg = lax.all_gather(shard, "fsdp", axis=0, tiled=True).reshape(8, 2, 240, D)
        cot_other = swap(cot, *SIDE)
        cot_other, gathered = tie(cot_other, gathered)
        weights, table = gathered.reshape(16, 26, 48, 128), gathered.reshape(16, 39, 32, 128)
        near_owner = jnp.arange(nf, dtype=jnp.int32)[:, None]
        near = weights[:, 25, 0:16].transpose(1, 0, 2)
    else:
        other_before = swap(before, "seq", 1)
        other_after = swap(after, "seq", 1)
        full = lax.all_gather(projection_matrix_triple, BOTH, axis=0, tiled=True)
        full = lax.dynamic_index_in_dim(full.reshape(D, 3, 2, OWN), side, 2, False)
        full = full.reshape(2, 8, 48, 9, 128).transpose(1, 0, 3, 2, 4).reshape(16, 9, 48, 128)
        table = lax.all_gather(relaxed_low, "fsdp", axis=1, tiled=True)
        table = table.reshape(6, 16, 32, 4, 128).transpose(1, 0, 3, 2, 4).reshape(16, 24, 32, 128)
        weights = jnp.concatenate([table.reshape(16, 16, 48, 128), full], axis=1)
        smalls = lax.all_gather(packed[None], BOTH, axis=0, tiled=True).transpose(1, 0, 2)
        near = lax.dynamic_slice_in_dim(smalls, side * nf, nf, 1)
        near_owner = jnp.arange(nf, dtype=jnp.int32)[:, None]
        owner = jnp.arange(count, dtype=jnp.int32)[:, None]
        cot_other = swap(cot, *SIDE)
        up = lax.all_gather(widen_matrix, BOTH, axis=0, tiled=True)
        up = lax.dynamic_slice_in_dim(up, side * (FF // 2), FF // 2, 1)
        up = up.reshape(2, 8, 48, 2, D).transpose(1, 3, 0, 2, 4).reshape(8, 2, 96, D)
        down = lax.all_gather(shrink_matrix, "fsdp", axis=0, tiled=True).reshape(8, 2, 96, D)
        out = lax.all_gather(merge_matrix, BOTH, axis=0, tiled=True)
        out = out.reshape(2, 8, 48, 2, OWN).transpose(1, 3, 2, 0, 4).reshape(8, 2, 48, D)
        wg = jnp.concatenate([down, up, out], axis=2)

    pos_col, doc_col = pos.reshape(WINDOW, 1), doc.reshape(WINDOW, 1)
    pos_row, doc_row = pos.reshape(6, 1, CHUNK), doc.reshape(6, 1, CHUNK)
    pieces = (tokens, before, after, other_tokens, other_before, other_after)
    q, k, v, xw, k_turned, x_turned = project(scal, pieces, weights, near, near_owner, spread, group)
    if fast:
        far = swap(near, "seq", 1)
        smalls = jnp.concatenate([near, far], axis=1)
        owner = jnp.concatenate([side * nf + near_owner, (1 - side) * nf + near_owner], axis=0)
        q, smalls = tie(q, smalls)
    ctx, inverses, *kept = attend(scal, pos_col, pos_row, doc_col, doc_row, q, k, v, table)
    ctx_other = swap(ctx, *SIDE)
    params_of = (smalls, owner, spread, group, wg)
    up = lambda i: feed_up(
        i, scal, xw, ctx, ctx_other, smalls, owner, near, near_owner,
        (spread, group, spread_up, group_up), wg,
    )
    down = lambda i, base, got, slope: feed_back(
        i, scal, base, got, cot, cot_other, slope, *params_of
    )
    close = lambda i, base, got, unit, rstd, sums, more: feed_close(
        i, scal, base, got, unit, rstd, sums, more, *params_of
    )
    up0 = up(0)
    got0 = swap(up0[4], *SIDE)
    up1, got0 = tie(up(1), got0)
    got1 = swap(up1[4], *SIDE)
    down0, got1 = tie(down(0, up0[3], got0, up0[6]), got1)
    got0 = swap(down0[4], *SIDE)
    down1, got0 = tie(down(1, up1[3], got1, up1[6]), got0)
    got1 = swap(down1[4], *SIDE)
    closed0 = close(0, down0[3], got0, up0[0], up0[1], down0[5], down1[5])
    feed = weight_grads(
        scal, up0[5], down0[1], up0[2], down0[2], up1[5], down1[1], up1[2], down1[2]
    )
    closed0, feed, got1 = tie(closed0, feed, got1)
    if fast:
        feed_got = swap(by_core(feed[1]), *CORE)
    closed1 = close(1, down1[3], got1, up1[0], up1[1], closed0[3], jnp.zeros((16, D), F32))
    if fast:
        closed1, feed_got = tie(closed1, feed_got)
        feed = sum_core(feed[0], feed_got)
        feed_got = swap(feed[1], *ALONG_Y)
    dh1, dattn, dctx = [[c[i] for c in (closed0, closed1)] for i in range(3)]
    sums = closed1[3]
    lay = jnp.where(side == 0, down0[0], down1[0])
    back = lambda first, pairs, before: attend_back(
        first, pairs, before, scal, q, k_turned, v, kept, x_turned, sums, ctx, dctx, dattn, inverses
    )
    outs = back(0, 3, ())
    if fast:
        outs, feed_got = tie(outs, feed_got)
        feed = add(feed[0][:2], feed_got[:2]), add(feed[0][2:], feed_got[2:])
        outs, feed = tie(outs, feed)
    dq, own, low, high, *parts = outs

    own_cols = lambda values, at, size: lax.dynamic_slice_in_dim(values, at * size, size, 1)
    if fast:
        feed_got = swap(feed[1], "fsdp", 4)
        part_got = swap(by_core(parts[1]), *CORE)
        table_got = swap(by_core(parts[3]), *CORE)
        part_got, table_got = tie(part_got, table_got)
        part, table_part = sum_core(parts[0], part_got), sum_core(parts[2], table_got)
        part_got = swap(part[1], *ALONG_Y)
        feed = add(feed[0][0], feed_got[0]), add(feed[0][1], feed_got[1])
        feed_got = swap(feed[1], "fsdp", 8)
        part_got, feed_got, table_part, low, high = tie(
            part_got, feed_got, table_part, low, high
        )
        part_got = along_z(add(part[0], part_got))
        table_got = swap(table_part[1], *ALONG_Y)
        left, right = shifted(high, "fsdp", 1), shifted(low, "fsdp", -1)
        table_got, left, right = tie(table_got, left, right)
        table_got, left, right = tie(add(table_part[0], table_got), left, right)
        table_got = along_z(table_got)
        dx, dx_send = project_back(scal, (dq, own, left, right), dh1, weights)
        dx_got = swap(dx_send, *SIDE)
        shard = add(feed[0], feed_got)
        part = sum_z(part_got)
        table_total = sum_z(table_got)
        table_total = table_total.reshape(3, 2, 4, 32, 128).transpose(0, 1, 3, 2, 4)
        table_total = table_total.reshape(6, 32, MPOS).astype(F32)
        blocks = part.reshape(3, PART, 128)
        weight = blocks[:, :PART_SUMS].reshape(3, 3, 2, rows, 128).transpose(1, 0, 2, 3, 4)
        mine = lax.dynamic_index_in_dim(weight, side, 2, False)
        sent = lax.dynamic_index_in_dim(weight, 1 - side, 2, False)
        sums = blocks[:, PART_SUMS:PART_OUT].reshape(6, 16, 128)
        sums = sums.transpose(1, 0, 2).reshape(16, D).astype(F32)
        outs = blocks[:, PART_OUT:].reshape(6, rows, 128)
        grad_w_out = outs.transpose(1, 0, 2).reshape(rows, D).astype(F32)
        got = swap(sent.reshape(-1, 128), *SIDE)
        got = got.reshape(3, 3, rows, 128)
        mine = mine.transpose(2, 0, 1, 3).reshape(rows, 3, 1, OWN)
        got = got.transpose(2, 0, 1, 3).reshape(rows, 3, 1, OWN)
        grad_w_qkv = in_order(side, mine, got, 2).reshape(rows, 3 * D).astype(F32)
        head_sums = blocks[:, PART_TOTALS : PART_TOTALS + 2].transpose(1, 0, 2).reshape(2, OWN)
        head_sums = head_sums.astype(F32)
        head_grads = own_cols(head_sums, place, wide_cols)
        grad_w_down = shard[:96].astype(F32)
        wide = shard[96:192].reshape(2, 2, rows, D).transpose(0, 2, 1, 3).reshape(2, rows, FF // 2)
        mine = lax.dynamic_index_in_dim(wide, side, 0, False)
        got = swap(lax.dynamic_index_in_dim(wide, 1 - side, 0, False), *SIDE)
        grad_w_up = in_order(side, mine, got, 1).astype(F32)
    else:
        scatter = partial(lax.psum_scatter, axis_name=BOTH, scatter_dimension=0, tiled=True)
        left, right = shifted(high, "fsdp", 1), shifted(low, "fsdp", -1)
        dx, dx_send = project_back(scal, (dq, own, left, right), dh1, weights)
        dx_got = swap(dx_send, "seq", 1)

        def plain(pair, at=lambda u: 4 * (u & 1) + (u >> 1)):
            both = jnp.stack(pair, axis=1)
            return jnp.stack([both[at(u)] for u in range(8)], axis=0)

        blocks = plain(parts[:2]).reshape(8, 2, 3, PART, 128)
        table_grad = plain(parts[2:]).reshape(8, 2, 3, 2, 4, 32, 128).transpose(2, 3, 0, 1, 5, 4, 6)
        table_total = lax.psum_scatter(
            table_grad.reshape(6, MPOS, MPOS), "fsdp", scatter_dimension=1, tiled=True
        ).astype(F32)
        head_rows = blocks[:, :, :, :PART_SUMS].reshape(8, 2, 3, 3, 2, 24, 128)
        head_rows = head_rows.transpose(4, 0, 1, 5, 3, 2, 6).reshape(D, 3, 1, OWN)
        blank = jnp.zeros_like(head_rows)
        both = jnp.concatenate(
            [jnp.where(side == 0, head_rows, blank), jnp.where(side == 0, blank, head_rows)], axis=2
        )
        grad_w_qkv = scatter(both.reshape(D, 3 * D)).astype(F32)
        head_sums = blocks[0, 0, :, PART_TOTALS : PART_TOTALS + 2].transpose(1, 0, 2)
        head_sums = lax.psum(head_sums.reshape(2, OWN).astype(F32), "fsdp")
        head_grads = own_cols(head_sums, place, wide_cols)
        def placed(value, axis):
            blank = jnp.zeros_like(value)
            sides = [jnp.where(side == 0, value, blank), jnp.where(side == 0, blank, value)]
            return jnp.concatenate(sides, axis=axis)

        gg = plain(feed, lambda u: 4 * (u & 1) + (u & 2) + (u >> 2)).reshape(16, 192, D)
        grad_w_down = scatter(placed(gg[:, :96].reshape(FF // 2, D), 0)).astype(F32)
        up = gg[:, 96:192].reshape(16, 2, 2, 24, D).transpose(1, 0, 3, 2, 4).reshape(D, FF // 2)
        grad_w_up = scatter(placed(up, 1)).astype(F32)
        out = blocks[:, :, :, PART_OUT:].reshape(8, 2, 3, 2, 24, 128).transpose(0, 1, 4, 2, 3, 5)
        out = out.reshape(OWN, D)
        grad_w_out = scatter(placed(out, 0)).astype(F32)
        sums = lax.psum(sums, "fsdp")
    ours = own_cols(sums[:6], side * nf + place, wide_cols)
    grad_biases = jnp.concatenate([head_grads, ours[:4]], axis=0)
    grad_gains = ours[4:]
    grad_bias_up = lax.dynamic_slice_in_dim(
        sums[8:10].reshape(-1), place * up_cols, up_cols, 0
    )
    input_grad = dx + dx_got.astype(F32)
    mask_logit_gradient = (
        table_total * relaxed * (1.0 - relaxed) / softening_scale[:, None, None]
    )
    return (
        lay.reshape(1, HALF, D),
        input_grad.reshape(1, HALF, D),
        grad_w_qkv,
        grad_w_out,
        grad_w_up,
        grad_w_down,
        grad_biases,
        grad_gains,
        grad_bias_up,
        mask_logit_gradient,
    )


def solution(mesh):
    rows = P(("seq", "fsdp"), None)
    columns = P(None, ("seq", "fsdp"))
    block = P("fsdp", "seq", None)
    table = P("seq", "fsdp", None)
    return jax.shard_map(
        per_device,
        mesh=mesh,
        in_specs=(
            block, rows, rows, rows, rows, columns, columns, P(("seq", "fsdp")),
            table, table, P("seq"), P(), block,
        ),
        out_specs=(
            block, block, rows, rows, rows, rows, columns, columns, P(("seq", "fsdp")), table,
        ),
        check_vma=False,
    )
```
